32 devices in a mesh: scene: 8 (over y, x, core), rows: 4 (over z).
Axes of the slice: x: 2, y: 2, z: 4, core: 2. Of those that a mesh axis runs over, the one named last changes fastest.
Arguments:
- patches: bfloat16 [2, 8, 1024, 576], P(None, 'scene', 'rows'), may hold values from -6 to 6
- scene_length: int32 [2, 8], replicated, may hold values from 256 to 1024, as said below
- target_views: int32 [2, 8], replicated, may hold values from 1 to 12, as said below
- gauss_index: int32 [2, 8, 8, 12, 1024], P(None, 'scene', None, None, 'rows'), may hold values from 0 to 18431
- raster_weight: float32 [2, 8, 8, 12, 1024], P(None, 'scene', None, None, 'rows'), may hold values from 0.2 to 1
- target_color: float32 [2, 8, 3, 12, 1024], P(None, 'scene', None, None, 'rows'), may hold values from 0 to 1
- patch_weight: float32 [576, 1024], P('rows', 'scene'), may hold values from -0.25 to 0.25
- joint_weight: float32 [1024, 3072], P('scene', 'rows'), may hold values from -0.1875 to 0.1875
- output_weight: float32 [1024, 1024], P('scene', 'rows'), may hold values from -0.5 to 0.5
- up_weight: float32 [1024, 4096], P('scene', 'rows'), may hold values from -0.1875 to 0.1875
- down_weight: float32 [4096, 1024], P('scene', 'rows'), may hold values from -0.09375 to 0.09375
- gauss_weight: float32 [1024, 768], P('scene', 'rows'), may hold values from -0.1875 to 0.1875
- vectors: float32 [14080], replicated
- patch_moment: float32 [576, 1024], P('rows', 'scene'), may hold values from -3.0517578e-05 to 3.0517578e-05
- joint_moment: float32 [1024, 3072], P('scene', 'rows'), may hold values from -3.0517578e-05 to 3.0517578e-05
- output_moment: float32 [1024, 1024], P('scene', 'rows'), may hold values from -3.0517578e-05 to 3.0517578e-05
- up_moment: float32 [1024, 4096], P('scene', 'rows'), may hold values from -3.0517578e-05 to 3.0517578e-05
- down_moment: float32 [4096, 1024], P('scene', 'rows'), may hold values from -3.0517578e-05 to 3.0517578e-05
- gauss_moment: float32 [1024, 768], P('scene', 'rows'), may hold values from -3.0517578e-05 to 3.0517578e-05
- vector_moment: float32 [14080], replicated, may hold values from -0.00015258789 to 0.00015258789
- patch_average: float32 [576, 1024], P('rows', 'scene'), may hold values from -0.25 to 0.25
- joint_average: float32 [1024, 3072], P('scene', 'rows'), may hold values from -0.1875 to 0.1875
- output_average: float32 [1024, 1024], P('scene', 'rows'), may hold values from -0.5 to 0.5
- up_average: float32 [1024, 4096], P('scene', 'rows'), may hold values from -0.1875 to 0.1875
- down_average: float32 [4096, 1024], P('scene', 'rows'), may hold values from -0.09375 to 0.09375
- gauss_average: float32 [1024, 768], P('scene', 'rows'), may hold values from -0.1875 to 0.1875
- vector_average: float32 [14080], replicated
Outputs:
- loss_sum: float32 [], replicated
- pixel_count: float32 [], replicated
- grad_norm: float32 [], replicated
- next_patch_moment: float32 [576, 1024], P('rows', 'scene')
- next_joint_moment: float32 [1024, 3072], P('scene', 'rows')
- next_output_moment: float32 [1024, 1024], P('scene', 'rows')
- next_up_moment: float32 [1024, 4096], P('scene', 'rows')
- next_down_moment: float32 [4096, 1024], P('scene', 'rows')
- next_gauss_moment: float32 [1024, 768], P('scene', 'rows')
- next_vector_moment: float32 [14080], replicated
- next_patch_weight: float32 [576, 1024], P('rows', 'scene')
- next_joint_weight: float32 [1024, 3072], P('scene', 'rows')
- next_output_weight: float32 [1024, 1024], P('scene', 'rows')
- next_up_weight: float32 [1024, 4096], P('scene', 'rows')
- next_down_weight: float32 [4096, 1024], P('scene', 'rows')
- next_gauss_weight: float32 [1024, 768], P('scene', 'rows')
- next_vectors: float32 [14080], replicated
- next_patch_average: float32 [576, 1024], P('rows', 'scene')
- next_joint_average: float32 [1024, 3072], P('scene', 'rows')
- next_output_average: float32 [1024, 1024], P('scene', 'rows')
- next_up_average: float32 [1024, 4096], P('scene', 'rows')
- next_down_average: float32 [4096, 1024], P('scene', 'rows')
- next_gauss_average: float32 [1024, 768], P('scene', 'rows')
- next_vector_average: float32 [14080], replicated
The draws below stay inside these ranges and needn't reach their ends.
Inputs may be any that keep to these rules, and one draw needn't show every extreme that they name: `scene_length`: in each micro-batch one scene has all 1024 tokens. `target_views`: in each micro-batch one scene has 12 target views. `gauss_index`: row r of a block's table is Gaussian r % (768 // 12) of token r // (768 // 12) of the block's tokens with 16 rim tokens on each side.
All inputs are finite; a program needn't handle non-finite values.
Results may differ from the reference program's by a relative error of at most 0.0011.
The reference program's roundings to bfloat16 on the way count: a program that leaves them out, or rounds other values in their place, can miss the bound.
Values may be sent and summed in bfloat16 or wider, within the bound.
No kernel may reach another device: no remote copies, remote signals or barrier semaphores. Data moves between devices by JAX's collectives and lax.ppermute only.
A program may use at most 384 MiB of HBM per device.

```python
import jax
import jax.numpy as jnp
from jax import lax

D = 1024
HEADS = 16
HD = 64
FF = 4096
PIN = 576
POUT = 768
ROWS_DEV = 256
PIX_DEV = 256
MB = 2
TV = 12
KG = 8
HT = 16
SEQ = 1024
SCENES = 8
PIXELS = 1024
VEC = 14080
NPARAM = 13973248
N_ROWS = 4


def vector_law(key):
    gains = jax.random.uniform(jax.random.fold_in(key, 1), (3 * D,), jnp.float32, 0.6, 1.4)
    others = 0.3 * jax.random.normal(jax.random.fold_in(key, 2), (6 * D + FF + POUT,), jnp.float32)
    return jnp.concatenate([gains, others])


def draw_vectors(key, part):
    key = jax.random.fold_in(key, 11)
    return vector_law(key)


def draw_vector_average(key, part):
    key = jax.random.fold_in(key, 12)
    return vector_law(key)


def full_in_each(key, lowest, highest):
    values = jax.random.randint(jax.random.fold_in(key, 1), (MB, SCENES), lowest, highest + 1)
    chosen = jax.random.randint(jax.random.fold_in(key, 2), (MB,), 0, SCENES)
    full = jnp.arange(SCENES)[None, :] == chosen[:, None]
    return jnp.where(full, highest, values).astype(jnp.int32)


def draw_scene_length(key, part):
    key = jax.random.fold_in(key, 13)
    return full_in_each(key, SEQ // 4, SEQ)


def draw_target_views(key, part):
    key = jax.random.fold_in(key, 14)
    return full_in_each(key, 1, TV)


def plant(array, rng, smallest, high):
    longest = array.shape.index(max(array.shape))
    spots = []
    for shift in (0, 1):
        where = [jax.random.randint(jax.random.fold_in(rng, axis), (), 0, length) for axis, length in enumerate(array.shape)]
        where[longest] = (where[longest] + shift) % array.shape[longest]
        spots.append(tuple(where))
    return array.at[spots[0]].set(smallest).at[spots[1]].set(high)


def levels(own_key, shape, split, low, top_value):
    factor_of, own = 1.0, jax.random.fold_in(own_key, 6)
    for position, shards_of in split:
        draws = jnp.exp(jax.random.uniform(jax.random.fold_in(own, position), (shards_of,), jnp.float32, low / len(split), top_value / len(split)))
        factor_of = factor_of * jnp.repeat(draws, shape[position] // shards_of).reshape([-1 if axis == position else 1 for axis in range(len(shape))])
    return factor_of


def bell_draw(rng, shape, deviation, bound, cuts=(), kind=jnp.bfloat16):
    array = jax.random.normal(rng, shape, jnp.float32) * deviation
    if len(cuts) > 0:
        array = levels(rng, shape, cuts, -0.22, 0.18) * array
    return jnp.clip(array, min=-bound, max=bound).astype(kind)


def setup_inputs(seed: int = 0) -> dict:
    streams_of = jax.random.split(jax.random.key(seed), 28)
    return {
        "patches": bell_draw(streams_of[0], (MB, SCENES, SEQ, PIN), 1.0, 6.0, ((1, 8), (2, 4))),
        "scene_length": draw_scene_length(jax.random.fold_in(streams_of[27], 71), 0),
        "target_views": draw_target_views(jax.random.fold_in(streams_of[27], 71), 0),
        "gauss_index": plant(jax.random.randint(streams_of[3], (MB, SCENES, KG, TV, PIXELS), 0, (ROWS_DEV + 2 * HT) * (POUT // 12)), jax.random.fold_in(streams_of[3], 1), 0, ((ROWS_DEV + 2 * HT) * (POUT // 12)) - 1).astype(jnp.int32),
        "raster_weight": jnp.clip(0.2 + 0.8 * jax.random.uniform(streams_of[4], (MB, SCENES, KG, TV, PIXELS), jnp.float32) ** levels(streams_of[4], (MB, SCENES, KG, TV, PIXELS), ((1, 8), (4, 4)), -0.2, 0.2), 0.2, 1.0),
        "target_color": jnp.clip(1.0 * jax.random.uniform(streams_of[5], (MB, SCENES, 3, TV, PIXELS), jnp.float32) ** levels(streams_of[5], (MB, SCENES, 3, TV, PIXELS), ((1, 8), (4, 4)), -0.2, 0.2), 0.0, 1.0),
        "patch_weight": bell_draw(streams_of[6], (PIN, D), PIN ** -0.5, 0.25, ((0, 4), (1, 8)), jnp.float32),
        "joint_weight": bell_draw(streams_of[7], (D, 3 * D), D ** -0.5, 0.1875, ((0, 8), (1, 4)), jnp.float32),
        "output_weight": bell_draw(streams_of[8], (D, D), (D // 8) ** -0.5, 0.5, ((0, 8), (1, 4)), jnp.float32),
        "up_weight": bell_draw(streams_of[9], (D, FF), D ** -0.5, 0.1875, ((0, 8), (1, 4)), jnp.float32),
        "down_weight": bell_draw(streams_of[10], (FF, D), FF ** -0.5, 0.09375, ((0, 8), (1, 4)), jnp.float32),
        "gauss_weight": bell_draw(streams_of[11], (D, POUT), D ** -0.5, 0.1875, ((0, 8), (1, 4)), jnp.float32),
        "vectors": draw_vectors(jax.random.fold_in(streams_of[27], 71), 0),
        "patch_moment": bell_draw(streams_of[13], (PIN, D), (0.02 / NPARAM ** 0.5), 3.0517578125e-05, ((0, 4), (1, 8)), jnp.float32),
        "joint_moment": bell_draw(streams_of[14], (D, 3 * D), (0.02 / NPARAM ** 0.5), 3.0517578125e-05, ((0, 8), (1, 4)), jnp.float32),
        "output_moment": bell_draw(streams_of[15], (D, D), (0.02 / NPARAM ** 0.5), 3.0517578125e-05, ((0, 8), (1, 4)), jnp.float32),
        "up_moment": bell_draw(streams_of[16], (D, FF), (0.02 / NPARAM ** 0.5), 3.0517578125e-05, ((0, 8), (1, 4)), jnp.float32),
        "down_moment": bell_draw(streams_of[17], (FF, D), (0.02 / NPARAM ** 0.5), 3.0517578125e-05, ((0, 8), (1, 4)), jnp.float32),
        "gauss_moment": bell_draw(streams_of[18], (D, POUT), (0.02 / NPARAM ** 0.5), 3.0517578125e-05, ((0, 8), (1, 4)), jnp.float32),
        "vector_moment": bell_draw(streams_of[19], (VEC,), (0.1 / NPARAM ** 0.5), 0.00015258789, (), jnp.float32),
        "patch_average": bell_draw(streams_of[20], (PIN, D), PIN ** -0.5, 0.25, ((0, 4), (1, 8)), jnp.float32),
        "joint_average": bell_draw(streams_of[21], (D, 3 * D), D ** -0.5, 0.1875, ((0, 8), (1, 4)), jnp.float32),
        "output_average": bell_draw(streams_of[22], (D, D), (D // 8) ** -0.5, 0.5, ((0, 8), (1, 4)), jnp.float32),
        "up_average": bell_draw(streams_of[23], (D, FF), D ** -0.5, 0.1875, ((0, 8), (1, 4)), jnp.float32),
        "down_average": bell_draw(streams_of[24], (FF, D), FF ** -0.5, 0.09375, ((0, 8), (1, 4)), jnp.float32),
        "gauss_average": bell_draw(streams_of[25], (D, POUT), D ** -0.5, 0.1875, ((0, 8), (1, 4)), jnp.float32),
        "vector_average": draw_vector_average(jax.random.fold_in(streams_of[27], 71), 0),
    }


HIGHEST = lax.Precision.HIGHEST
EPSILON = 1e-05
CLIP_NORM = 0.002
STEP_RATE = 1250.0
MOMENTUM = 0.9
AVERAGE_DECAY = 0.9

@jax.custom_vjp
def low(v):
    return lax.optimization_barrier(v.astype(jnp.bfloat16)).astype(jnp.float32)

@jax.custom_vjp
def low_back(v):
    return v

def low_keep(v):
    return (low(v), None)

def low_pass(kept, grad):
    return (grad,)

def back_keep(v):
    return (v, None)

def back_low(kept, grad):
    return (low(grad),)
low.defvjp(low_keep, low_pass)
low_back.defvjp(back_keep, back_low)

def matmul(left, right):
    return jnp.dot(left, right, precision=HIGHEST)

def split_vectors(vectors):
    pieces = []
    offset = 0
    for extent in [D] * 9 + [FF, POUT]:
        pieces.append(lax.slice_in_dim(vectors, offset, offset + extent))
        offset = offset + extent
    return pieces

def layer_norm(hidden, gain, shift):
    centred = hidden - lax.optimization_barrier(jnp.mean(hidden, axis=-1, keepdims=True))
    variance = lax.optimization_barrier(jnp.mean(centred * centred, axis=-1, keepdims=True))
    return centred * lax.rsqrt(variance + EPSILON) * gain + shift

def features_of(colour):
    counter = jnp.arange(48).reshape(16, 3).astype(colour.dtype)
    return jnp.tanh(jnp.einsum('fc,ctp->ftp', 0.8 * jnp.cos(1.7 * counter + 0.3), colour, precision=HIGHEST))

def render_sum(extended, index, weight, target, views):
    params = extended.reshape(-1, 12)
    colour = jax.nn.sigmoid(params[:, :3])
    opacity = jax.nn.sigmoid(params[:, 3]) * jnp.exp(-0.5 * lax.optimization_barrier(jnp.mean(params[:, 4:] * params[:, 4:], axis=1)))
    table = jnp.concatenate([colour * opacity[:, None], opacity[:, None]], axis=1).T
    picked = jnp.take(table, index, axis=1)
    numerator = lax.optimization_barrier(jnp.sum(weight * picked[:3], axis=1))
    denominator = 1.0 + lax.optimization_barrier(jnp.sum(weight * picked[3], axis=0))
    rendered = numerator / denominator
    live = (jnp.arange(index.shape[1]) < views).astype(rendered.dtype)[:, None]
    difference = rendered - target
    error = lax.optimization_barrier(jnp.sum(difference * difference, axis=0))
    feature_gap = features_of(rendered) - features_of(target)
    error = error + 0.5 * lax.optimization_barrier(jnp.sum(feature_gap * feature_gap, axis=0))
    return jnp.sum(live * error)

def scene_loss(lowered, patch, length, views, index, weight, target):
    patch_w, joint_w, output_w, up_w, down_w, gauss_w, vectors = lowered
    gain_one, gain_two, gain_three, shift_one, shift_two, shift_three, bias_patch, bias_out, bias_down, bias_up, bias_gauss = split_vectors(vectors)
    hidden_zero = low_back(matmul(patch, patch_w)) + bias_patch
    normed_one = low(layer_norm(hidden_zero, gain_one, shift_one))
    projected = low_back(low(matmul(normed_one, joint_w))).reshape(SEQ, 3, HEADS, HD)
    queries, keys_all, values_all = (projected[:, 0], projected[:, 1], projected[:, 2])
    scores = HD ** (-0.5) * low_back(jnp.einsum('qhd,khd->hqk', queries, keys_all, precision=HIGHEST))
    visible = jnp.arange(SEQ) < length
    scores = jnp.where(visible[None, None, :], scores, -1e+30)
    probs = low(jax.nn.softmax(scores, axis=-1))
    mixed = low_back(low(jnp.einsum('hqk,khd->qhd', probs, values_all, precision=HIGHEST))).reshape(SEQ, D)
    hidden_one = hidden_zero + low_back(matmul(mixed, output_w)) + bias_out
    normed_two = low(layer_norm(hidden_one, gain_two, shift_two))
    up_input = low_back(matmul(normed_two, up_w)) + bias_up
    activated = low(jax.nn.gelu(up_input))
    hidden_two = hidden_one + low_back(matmul(activated, down_w)) + bias_down
    normed_three = low(layer_norm(hidden_two, gain_three, shift_three))
    gauss = low_back(matmul(normed_three, gauss_w)) + bias_gauss
    padded = jnp.pad(gauss, ((HT, HT), (0, 0)))
    total = jnp.zeros((), gauss.dtype)
    for block in range(N_ROWS):
        extended = padded[block * ROWS_DEV:block * ROWS_DEV + ROWS_DEV + 2 * HT]
        pixels = slice(block * PIX_DEV, (block + 1) * PIX_DEV)
        total = total + render_sum(extended, index[..., pixels], weight[..., pixels], target[..., pixels], views)
    return total

def reference(patches, scene_length, target_views, gauss_index, raster_weight, target_color, patch_weight, joint_weight, output_weight, up_weight, down_weight, gauss_weight, vectors, patch_moment, joint_moment, output_moment, up_moment, down_moment, gauss_moment, vector_moment, patch_average, joint_average, output_average, up_average, down_average, gauss_average, vector_average):
    masters = (patch_weight, joint_weight, output_weight, up_weight, down_weight, gauss_weight, vectors)
    moments = (patch_moment, joint_moment, output_moment, up_moment, down_moment, gauss_moment, vector_moment)
    averages = (patch_average, joint_average, output_average, up_average, down_average, gauss_average, vector_average)
    count = jnp.sum(target_views).astype(jnp.float32) * PIXELS
    flat = (patches.astype(jnp.float32).reshape(-1, SEQ, PIN), scene_length.reshape(-1), target_views.reshape(-1), gauss_index.reshape((-1,) + gauss_index.shape[2:]), raster_weight.reshape((-1,) + raster_weight.shape[2:]), target_color.reshape((-1,) + target_color.shape[2:]))

    def total_loss(params):
        lowered = tuple((low(item) for item in params[:6])) + (params[6],)

        def scene_step(carry, item):
            return (carry + scene_loss(lowered, *item), None)
        total, unused = lax.scan(jax.checkpoint(scene_step), jnp.zeros((), jnp.float32), flat)
        return total
    loss_sum, pull = jax.vjp(total_loss, masters)
    grads = pull(jnp.ones((), loss_sum.dtype) / count)[0]
    squares = sum((jnp.sum(item * item) for item in grads))
    grad_norm = jnp.sqrt(squares)
    factor = jnp.minimum(1.0, CLIP_NORM / (grad_norm + 1e-06))
    next_moments, next_weights, next_averages = ([], [], [])
    for grad, moment, master, average in zip(grads, moments, masters, averages):
        clipped = grad * factor
        moment_new = MOMENTUM * moment + clipped
        weight_new = master - STEP_RATE * (clipped + MOMENTUM * moment_new)
        next_moments.append(moment_new)
        next_weights.append(weight_new)
        next_averages.append(AVERAGE_DECAY * average + (1.0 - AVERAGE_DECAY) * weight_new)
    return (loss_sum, count, grad_norm, next_moments[0], next_moments[1], next_moments[2], next_moments[3], next_moments[4], next_moments[5], next_moments[6], next_weights[0], next_weights[1], next_weights[2], next_weights[3], next_weights[4], next_weights[5], next_weights[6], next_averages[0], next_averages[1], next_averages[2], next_averages[3], next_averages[4], next_averages[5], next_averages[6])
```

```python
import functools

import jax
import jax.numpy as jnp
import numpy as np
from jax import lax
from jax.experimental import pallas as pl
from jax.experimental.pallas import tpu as pltpu
from jax.sharding import PartitionSpec as P

D = 1024
HEADS = 16
HD = 64
FF = 4096
POUT = 768
HT = 16
GV = 12
NG = POUT // GV

EPSILON = 1e-05
CLIP_NORM = 0.002
STEP_RATE = 1250.0
MOMENTUM = 0.9
AVERAGE_DECAY = 0.9

F32 = jnp.float32
BF16 = jnp.bfloat16
HIGHEST = lax.Precision.HIGHEST
BLOCKS = 8
WIDE = D // BLOCKS
VMEM_MB = 1024 * 1024
TABLE = NG + 8


def nn(a, b):
    return lax.dot_general(a, b, (((1,), (0,)), ((), ())), preferred_element_type=F32)


def nt(a, b):
    return lax.dot_general(a, b, (((1,), (1,)), ((), ())), preferred_element_type=F32)


def tn(a, b):
    return lax.dot_general(a, b, (((0,), (0,)), ((), ())), preferred_element_type=F32)


def params(mb, n=1):
    return pltpu.CompilerParams(
        vmem_limit_bytes=mb * VMEM_MB, dimension_semantics=("arbitrary",) * n
    )


def lane_block(index, width):
    return pl.ds(pl.multiple_of(index * width, width), width)


def norm_store(perm, h_ref, g_ref, s_ref, a_ref, chunk):
    def step(i, carry):
        rows = pl.ds(pl.multiple_of(i * chunk, chunk), chunk)
        h = h_ref[rows, :]
        c = h - jnp.mean(h, axis=1, keepdims=True)
        var = jnp.mean(c * c, axis=1, keepdims=True)
        a = (c * lax.rsqrt(var + EPSILON) * g_ref[...] + s_ref[...]).astype(BF16)
        for b in range(BLOCKS):
            a_ref[rows, lane_block(perm[8 + b], WIDE)] = a[:, b * WIDE : (b + 1) * WIDE]
        return carry

    lax.fori_loop(0, h_ref.shape[0] // chunk, step, 0)


def embed_kernel(perm, x_ref, w_ref, b_ref, g_ref, s_ref, h_ref, a_ref):
    hr = nt(x_ref[...], w_ref[...])
    for j in range(BLOCKS):
        cols = lane_block(perm[j], WIDE)
        h_ref[:, cols] = hr[:, j * WIDE : (j + 1) * WIDE] + b_ref[:, cols]
    norm_store(perm, h_ref, g_ref, s_ref, a_ref, 32)


def embed(perm, x, w, b, g, s):
    rows, pin = x.shape
    part = 256
    full = lambda shape: pl.BlockSpec(shape, lambda i, p: (0, 0))
    tile = lambda n: pl.BlockSpec((part, n), lambda i, p: (i, 0))
    return pl.pallas_call(
        embed_kernel,
        grid_spec=pltpu.PrefetchScalarGridSpec(
            num_scalar_prefetch=1,
            grid=(rows // part,),
            in_specs=[tile(pin), full((D, pin)), full((1, D)), full((1, D)), full((1, D))],
            out_specs=[tile(D), tile(D)],
        ),
        out_shape=[jax.ShapeDtypeStruct((rows, D), F32), jax.ShapeDtypeStruct((rows, D), BF16)],
        compiler_params=params(32),
        cost_estimate=pl.CostEstimate(
            flops=2 * rows * D * pin, bytes_accessed=rows * D * 6 + 4 * D * pin, transcendentals=0
        ),
        name="embed_norm",
    )(perm, x, w, b, g, s)


def project_kernel(perm, a_ref, w_ref, r_ref, b_ref, g_ref, s_ref, h_ref, n_ref):
    k = pl.program_id(0)

    @pl.when(k == 0)
    def _():
        h_ref[...] = r_ref[...] + b_ref[...] + nn(a_ref[...], w_ref[...])

    @pl.when(k > 0)
    def _():
        h_ref[...] = h_ref[...] + nn(a_ref[...], w_ref[...])

    @pl.when(k == pl.num_programs(0) - 1)
    def _():
        norm_store(perm, h_ref, g_ref, s_ref, n_ref, 32)


def project(perm, a, w, res, b, g, s):
    rows, depth = a.shape
    part = 512
    full = lambda shape: pl.BlockSpec(shape, lambda k, p: (0, 0))
    return pl.pallas_call(
        project_kernel,
        grid_spec=pltpu.PrefetchScalarGridSpec(
            num_scalar_prefetch=1,
            grid=(depth // part,),
            in_specs=[
                pl.BlockSpec((rows, part), lambda k, p: (0, k)),
                pl.BlockSpec((part, D), lambda k, p: (k, 0)),
                full((rows, D)),
                full((1, D)),
                full((1, D)),
                full((1, D)),
            ],
            out_specs=[full((rows, D)), full((rows, D))],
        ),
        out_shape=[jax.ShapeDtypeStruct((rows, D), F32), jax.ShapeDtypeStruct((rows, D), BF16)],
        compiler_params=params(40),
        cost_estimate=pl.CostEstimate(
            flops=2 * rows * D * depth,
            bytes_accessed=rows * D * 10 + 2 * D * depth + 2 * rows * depth,
            transcendentals=0,
        ),
        name="project_norm",
    )(perm, a, w, res, b, g, s)


GELU_C = float(np.sqrt(2.0 / np.pi))


def up_kernel(perm, a_ref, w_ref, b_ref, u_ref, g_ref):
    u = nn(a_ref[...], w_ref[...]) + b_ref[...]
    u_ref[...] = u
    t = jnp.tanh(GELU_C * (u + 0.044715 * (u * u * u)))
    g_ref[...] = (u * (0.5 * (1.0 + t))).astype(BF16)


def up_project(perm, a, w, b):
    rows = a.shape[0]
    part = FF // BLOCKS
    return pl.pallas_call(
        up_kernel,
        grid_spec=pltpu.PrefetchScalarGridSpec(
            num_scalar_prefetch=1,
            grid=(BLOCKS,),
            in_specs=[
                pl.BlockSpec((rows, D), lambda n, p: (0, 0)),
                pl.BlockSpec((D, part), lambda n, p: (0, n)),
                pl.BlockSpec((1, part), lambda n, p: (0, n)),
            ],
            out_specs=[
                pl.BlockSpec((rows, part), lambda n, p: (0, n)),
                pl.BlockSpec((rows, part), lambda n, p: (0, p[8 + n])),
            ],
        ),
        out_shape=[jax.ShapeDtypeStruct((rows, FF), F32), jax.ShapeDtypeStruct((rows, FF), BF16)],
        compiler_params=params(32),
        cost_estimate=pl.CostEstimate(
            flops=2 * rows * D * FF, bytes_accessed=rows * FF * 6 + 2 * D * FF, transcendentals=rows * FF
        ),
        name="up_gelu",
    )(perm, a, w, b)


def down_back_kernel(perm, d_ref, w_ref, u_ref, du_ref, sum_ref):
    dg = nt(d_ref[...], w_ref[...])
    u = u_ref[...]
    u2 = u * u
    t = jnp.tanh(GELU_C * (u + 0.044715 * (u2 * u)))
    slope = 0.5 * (1.0 + t) + (0.5 * GELU_C) * u * (1.0 - t * t) * (1.0 + (3 * 0.044715) * u2)
    du = slope * dg
    du_ref[...] = du.astype(BF16)
    sum_ref[...] = jnp.sum(du, axis=0, keepdims=True)


def down_back(perm, d, w, u):
    rows = d.shape[0]
    part = FF // BLOCKS
    return pl.pallas_call(
        down_back_kernel,
        grid_spec=pltpu.PrefetchScalarGridSpec(
            num_scalar_prefetch=1,
            grid=(BLOCKS,),
            in_specs=[
                pl.BlockSpec((rows, D), lambda j, p: (0, 0)),
                pl.BlockSpec((part, D), lambda j, p: (j, 0)),
                pl.BlockSpec((rows, part), lambda j, p: (0, p[j])),
            ],
            out_specs=[
                pl.BlockSpec((rows, part), lambda j, p: (0, p[j])),
                pl.BlockSpec((1, part), lambda j, p: (0, p[j])),
            ],
        ),
        out_shape=[jax.ShapeDtypeStruct((rows, FF), BF16), jax.ShapeDtypeStruct((1, FF), F32)],
        compiler_params=params(32),
        cost_estimate=pl.CostEstimate(
            flops=2 * rows * D * FF, bytes_accessed=rows * FF * 6 + 2 * D * FF, transcendentals=rows * FF
        ),
        name="down_back_gelu",
    )(perm, d, w, u)


def back_kernel(has_res, placed, perm, *refs):
    if has_res:
        d_ref, w_ref, h_ref, g_ref, r_ref, *outs = refs
    else:
        d_ref, w_ref, h_ref, g_ref, *outs = refs
        r_ref = None
    if placed:
        low_ref, sums_ref, acc_ref, part_ref = outs
        dh_ref = None
    else:
        dh_ref, low_ref, sums_ref, acc_ref, part_ref = outs
    n = pl.program_id(0)

    @pl.when(n == 0)
    def _():
        acc_ref[...] = nt(d_ref[...], w_ref[...])

    @pl.when(n > 0)
    def _():
        acc_ref[...] = acc_ref[...] + nt(d_ref[...], w_ref[...])

    @pl.when(n == pl.num_programs(0) - 1)
    def _():
        chunk = 32
        part_ref[...] = jnp.zeros_like(part_ref)

        def fold(x):
            return jnp.sum(x.reshape(chunk // 8, 8, D), axis=0)

        def step(i, carry):
            rows = pl.ds(pl.multiple_of(i * chunk, chunk), chunk)
            h = h_ref[rows, :]
            c = h - jnp.mean(h, axis=1, keepdims=True)
            var = jnp.mean(c * c, axis=1, keepdims=True)
            rstd = lax.rsqrt(var + EPSILON)
            xh = c * rstd
            da = jnp.concatenate(
                [acc_ref[rows, lane_block(perm[8 + b], WIDE)] for b in range(BLOCKS)], axis=1
            )
            dxh = da * xh
            part_ref[0] += fold(dxh)
            part_ref[1] += fold(da)
            dy = da * g_ref[...]
            first = jnp.mean(dy, axis=1, keepdims=True)
            second = jnp.mean(dy * xh, axis=1, keepdims=True)
            dh = rstd * (dy - first - xh * second)
            if has_res:
                dh = dh + r_ref[rows, :]
            part_ref[2] += fold(dh)
            low = dh.astype(BF16)
            if placed:
                for b in range(BLOCKS):
                    low_ref[rows, lane_block(perm[8 + b], WIDE)] = low[:, b * WIDE : (b + 1) * WIDE]
            else:
                dh_ref[rows, :] = dh
                low_ref[rows, :] = low
            return carry

        lax.fori_loop(0, h_ref.shape[0] // chunk, step, 0)
        sums_ref[...] = jnp.concatenate(
            [jnp.sum(part_ref[i], axis=0, keepdims=True) for i in range(3)]
            + [jnp.zeros((5, D), F32)],
            axis=0,
        )


def norm_back(perm, d, w, h, g, res, placed):
    rows, wide = d.shape
    part = 768 if wide % 1024 else 1024
    full = lambda shape: pl.BlockSpec(shape, lambda n, p: (0, 0))
    args = [d, w, h, g]
    specs = [
        pl.BlockSpec((rows, part), lambda n, p: (0, n)),
        pl.BlockSpec((D, part), lambda n, p: (0, n)),
        full((rows, D)),
        full((1, D)),
    ]
    if res is not None:
        args.append(res)
        specs.append(full((rows, D)))
    out_specs = [full((rows, D)), full((8, D))]
    out_shape = [jax.ShapeDtypeStruct((rows, D), BF16), jax.ShapeDtypeStruct((8, D), F32)]
    if not placed:
        out_specs = [full((rows, D))] + out_specs
        out_shape = [jax.ShapeDtypeStruct((rows, D), F32)] + out_shape
    return pl.pallas_call(
        functools.partial(back_kernel, res is not None, placed),
        grid_spec=pltpu.PrefetchScalarGridSpec(
            num_scalar_prefetch=1,
            grid=(wide // part,),
            in_specs=specs,
            out_specs=out_specs,
            scratch_shapes=[pltpu.VMEM((rows, D), F32), pltpu.VMEM((3, 8, D), F32)],
        ),
        out_shape=out_shape,
        compiler_params=params(40),
        cost_estimate=pl.CostEstimate(
            flops=2 * rows * D * wide,
            bytes_accessed=rows * D * 14 + 2 * D * wide + 2 * rows * wide,
            transcendentals=0,
        ),
        name="norm_back",
    )(perm, *args)


SCALE = HD ** (-0.5)
PAIR = 2 * HD
PAIRS = HEADS // 2


def attend_kernel(perm, lens, q_ref, k0_ref, k1_ref, v0_ref, v1_ref, o_ref, l_ref):
    half = k0_ref.shape[0]
    lane = lax.broadcasted_iota(jnp.int32, (1, PAIR), 1)
    spot = lax.broadcasted_iota(jnp.int32, (1, half), 1)
    see = [spot < lens[0], spot < lens[1]]
    k0, k1, v0, v1 = k0_ref[...], k1_ref[...], v0_ref[...], v1_ref[...]
    chunk = 256
    for i in range(q_ref.shape[0] // chunk):
        rows = slice(i * chunk, (i + 1) * chunk)
        q = q_ref[rows, :] * SCALE
        outs = []
        logs = []
        for side in range(2):
            qm = jnp.where((lane < HD) == (side == 0), q, 0.0).astype(BF16)
            s0 = jnp.where(see[0], nt(qm, k0), -1e30)
            s1 = jnp.where(see[1], nt(qm, k1), -1e30)
            top = jnp.maximum(
                jnp.max(s0, axis=1, keepdims=True), jnp.max(s1, axis=1, keepdims=True)
            )
            e0 = jnp.exp(s0 - top)
            e1 = jnp.exp(s1 - top)
            total = jnp.sum(e0, axis=1, keepdims=True) + jnp.sum(e1, axis=1, keepdims=True)
            inv = 1.0 / total
            outs.append(nn((e0 * inv).astype(BF16), v0) + nn((e1 * inv).astype(BF16), v1))
            logs.append(top + jnp.log(total))
        o_ref[rows, :] = jnp.where(lane < HD, outs[0], outs[1]).astype(BF16)
        flat = jnp.where(lane < HD, logs[0], logs[1])
        turned = flat.T
        l_ref[0, 0:1, rows] = turned[0:1, :]
        l_ref[0, 1:2, rows] = turned[HD : HD + 1, :]


def attend(perm, lens, p, kv):
    rows = p.shape[0]
    block = lambda first: pl.BlockSpec((rows, PAIR), lambda h, m, n: (0, first + h))
    return pl.pallas_call(
        attend_kernel,
        grid_spec=pltpu.PrefetchScalarGridSpec(
            num_scalar_prefetch=2,
            grid=(PAIRS,),
            in_specs=[block(0), block(PAIRS), block(0), block(2 * PAIRS), block(PAIRS)],
            out_specs=[
                pl.BlockSpec((rows, PAIR), lambda h, m, n: (0, m[8 + h])),
                pl.BlockSpec((1, 8, rows), lambda h, m, n: (h, 0, 0)),
            ],
        ),
        out_shape=[
            jax.ShapeDtypeStruct((rows, D), BF16),
            jax.ShapeDtypeStruct((PAIRS, 8, rows), F32),
        ],
        compiler_params=params(40),
        cost_estimate=pl.CostEstimate(
            flops=8 * rows * rows * D,
            bytes_accessed=12 * rows * D,
            transcendentals=2 * rows * rows * HEADS,
        ),
        name="attend",
    )(perm, lens, p, p, kv, p, kv)


def attend_back_kernel(
    perm, lens, q_ref, k0_ref, k1_ref, v0_ref, v1_ref, do_ref, l_ref, dq_ref, own_ref, far_ref
):
    half = k0_ref.shape[0]
    lane = lax.broadcasted_iota(jnp.int32, (1, PAIR), 1)
    spot = lax.broadcasted_iota(jnp.int32, (half, 1), 0)
    see = [spot < lens[0], spot < lens[1]]
    keys = [k0_ref[...], k1_ref[...]]
    values = [v0_ref[...], v1_ref[...]]
    q_all, do_all = q_ref[...], do_ref[...]
    chunk = 256
    dk = [None, None]
    dv = [None, None]
    for i in range(q_ref.shape[0] // chunk):
        rows = slice(i * chunk, (i + 1) * chunk)
        dq = None
        for side in range(2):
            mine = (lane < HD) == (side == 0)
            qm = jnp.where(mine, q_all[rows, :], 0.0).astype(BF16)
            dom = jnp.where(mine, do_all[rows, :], 0.0).astype(BF16)
            qs = qm * SCALE
            logs = l_ref[0, side : side + 1, rows]
            probs = [
                jnp.exp(jnp.where(see[j], nt(keys[j], qs), -1e30) - logs) for j in range(2)
            ]
            da = [nt(values[j], dom) for j in range(2)]
            delta = sum(jnp.sum(probs[j] * da[j], axis=0, keepdims=True) for j in range(2))
            for j in range(2):
                ds = (probs[j] * (da[j] - delta) * SCALE).astype(BF16)
                km = jnp.where(mine, keys[j], 0.0).astype(BF16)
                term = tn(ds, km)
                dq = term if dq is None else dq + term
                term = nn(ds, qm)
                dk[j] = term if dk[j] is None else dk[j] + term
                term = nn(probs[j].astype(BF16), dom)
                dv[j] = term if dv[j] is None else dv[j] + term
        dq_ref[rows, :] = dq.astype(BF16)
    own_ref[0] = dk[0]
    own_ref[1] = dv[0]
    far_ref[0] = dk[1].astype(BF16)
    far_ref[1] = dv[1].astype(BF16)


def attend_back(perm, lens, p, kv, do, logs):
    rows = p.shape[0]
    block = lambda first: pl.BlockSpec((rows, PAIR), lambda h, m, n: (0, first + h))
    both = pl.BlockSpec((2, rows, PAIR), lambda h, m, n: (0, 0, h))
    return pl.pallas_call(
        attend_back_kernel,
        grid_spec=pltpu.PrefetchScalarGridSpec(
            num_scalar_prefetch=2,
            grid=(PAIRS,),
            in_specs=[
                block(0),
                block(PAIRS),
                block(0),
                block(2 * PAIRS),
                block(PAIRS),
                pl.BlockSpec((rows, PAIR), lambda h, m, n: (0, m[8 + h])),
                pl.BlockSpec((1, 8, rows), lambda h, m, n: (h, 0, 0)),
            ],
            out_specs=[block(0), both, both],
        ),
        out_shape=[
            jax.ShapeDtypeStruct((rows, D), BF16),
            jax.ShapeDtypeStruct((2, rows, D), F32),
            jax.ShapeDtypeStruct((2, rows, D), BF16),
        ],
        compiler_params=params(48),
        cost_estimate=pl.CostEstimate(
            flops=20 * rows * rows * D,
            bytes_accessed=28 * rows * D,
            transcendentals=2 * rows * rows * HEADS,
        ),
        name="attend_back",
    )(perm, lens, p, p, kv, p, kv, do, logs)


def iota(shape, dim):
    return lax.broadcasted_iota(jnp.int32, shape, dim)


def render_kernel(
    terms, views_ref, inv_ref, z_ref, zx_ref, rd_ref, mc_ref, dz_ref, dzx_ref, loss_ref,
    tf_ref, hi_ref, lo_ref, o_ref, wm_ref, a_ref, b_ref, dt_ref, tok_ref, edge_ref, zs_ref,
):
    width = 256
    pixels = rd_ref.shape[-1]
    kg = 8

    lanes = 128
    parts = z_ref.shape[1] // lanes
    for i in range(parts):
        zs_ref[i] = z_ref[:, i * lanes : (i + 1) * lanes]
    zs_ref[parts] = zx_ref[...]

    def values(i):
        return [zs_ref[i, pl.ds(v, NG, stride=GV), :] for v in range(GV)]

    def shade(z):
        colour = [jax.nn.sigmoid(z[i]) for i in range(3)]
        gate = jax.nn.sigmoid(z[3])
        square = z[4] * z[4]
        for i in range(5, GV):
            square = square + z[i] * z[i]
        opacity = gate * jnp.exp(-0.5 * (square / (GV - 4)))
        return colour, gate, opacity

    own_group = iota((NG, width), 0) % 16 == iota((NG, width), 1) // 16

    def spread(base):
        return (iota((128, width), 0) == base + iota((128, width), 1) % 16).astype(F32)

    def rim_rows(table, base):
        wide = lax.dot_general(
            table, spread(base), (((1,), (0,)), ((), ())), precision=HIGHEST,
            preferred_element_type=F32,
        )
        return jnp.sum(jnp.where(own_group, wide, 0.0).reshape(4, 16, width), axis=1)

    def rim_back(rows, base):
        wide = jnp.concatenate(
            [jnp.broadcast_to(rows[j : j + 1, :], (16, width)) for j in range(4)], axis=0
        )
        return lax.dot_general(
            jnp.where(own_group, wide, 0.0), spread(base), (((1,), (1,)), ((), ())),
            precision=HIGHEST, preferred_element_type=F32,
        )

    def place(i):
        if i == parts:
            return edge_ref, slice(0, lanes)
        return tok_ref, slice(i * lanes, (i + 1) * lanes)

    for i in range(parts + 1):
        out_ref, cols = place(i)
        colour, gate, opacity = shade(values(i))
        for ch in range(3):
            out_ref[ch * NG : (ch + 1) * NG, cols] = colour[ch] * opacity
        out_ref[3 * NG : 4 * NG, cols] = opacity

    for ch in range(4):
        rows = slice(ch * NG, (ch + 1) * NG)
        at = ch * TABLE
        tf_ref[0, at : at + NG, :] = tok_ref[rows, 0:width]
        tf_ref[1, at : at + NG, :] = tok_ref[rows, width : 2 * width]
        tf_ref[0, at + NG : at + NG + 4, :] = rim_rows(edge_ref[rows, :], 0)
        tf_ref[0, at + NG + 4 : at + NG + 8, :] = rim_rows(tok_ref[rows, width : width + 128], 0)
        tf_ref[1, at + NG : at + NG + 4, :] = rim_rows(tok_ref[rows, width - 128 : width], 112)
        tf_ref[1, at + NG + 4 : at + NG + 8, :] = rim_rows(edge_ref[rows, :], 16)
    for block in range(2):
        table = tf_ref[block]
        high = table.astype(BF16)
        hi_ref[block] = high
        lo_ref[block] = (table - high.astype(F32)).astype(BF16)
    dt_ref[...] = jnp.zeros_like(dt_ref)
    inverse = inv_ref[0]
    row_hi = iota((width, pixels), 0)
    row_lo = iota((TABLE, pixels), 0)

    def features(c):
        return jnp.tanh(mc_ref[0] * c[0] + mc_ref[1] * c[1] + mc_ref[2] * c[2])

    def view(t, loss):
        for block in range(2):
            r = rd_ref[block, t, 0:kg, :].astype(jnp.int32)
            weight = rd_ref[block, t, kg : 2 * kg, :]
            token = lax.shift_right_logical(r, 6)
            g = jnp.bitwise_and(r, NG - 1)
            after = token >= HT + width
            inside = jnp.logical_and(token >= HT, jnp.logical_not(after))
            rim = jnp.where(after, token - (HT + width), token)
            high = jnp.where(inside, token - HT, jnp.bitwise_and(g, 15) * 16 + rim)
            low = jnp.where(
                inside, g, NG + lax.shift_right_logical(g, 4) + jnp.where(after, 4, 0)
            )
            sums = [jnp.zeros((8, pixels), F32) for _ in range(4)]
            t_hi = hi_ref[block]
            t_lo = lo_ref[block]
            for k in range(kg):
                cols = slice(k * pixels, (k + 1) * pixels)
                one = jnp.where(row_hi == high[k : k + 1, :], 1.0, 0.0).astype(BF16)
                o_ref[:, cols] = one
                wm = jnp.where(row_lo == low[k : k + 1, :], weight[k : k + 1, :], 0.0)
                wm_ref[:, cols] = wm
                picked = nn(t_hi, one) + nn(t_lo, one)
                for ch in range(4):
                    part = picked[ch * TABLE : (ch + 1) * TABLE, :] * wm
                    sums[ch] = sums[ch] + jnp.sum(part.reshape(TABLE // 8, 8, pixels), axis=0)
            sums = [jnp.sum(s, axis=0, keepdims=True) for s in sums]
            scale = 1.0 / (1.0 + sums[3])
            seen = [sums[i] * scale for i in range(3)]
            goal = [rd_ref[block, t, 2 * kg + i : 2 * kg + i + 1, :] for i in range(3)]
            f_seen = features(seen)
            gap = f_seen - features(goal)
            diff = [seen[i] - goal[i] for i in range(3)]
            loss = loss + diff[0] * diff[0] + diff[1] * diff[1] + diff[2] * diff[2]
            loss = loss + 0.5 * jnp.sum(gap * gap, axis=0, keepdims=True)
            pull = gap * (1.0 - f_seen * f_seen)
            d_seen = [
                inverse * (2.0 * diff[i] + jnp.sum(pull * mc_ref[i], axis=0, keepdims=True))
                for i in range(3)
            ]
            d_sum = [d * scale for d in d_seen]
            d_sum.append(
                -(d_seen[0] * seen[0] + d_seen[1] * seen[1] + d_seen[2] * seen[2]) * scale
            )
            for k in range(kg):
                cols = slice(k * pixels, (k + 1) * pixels)
                wm = wm_ref[:, cols]
                full = jnp.concatenate([wm * d_sum[ch] for ch in range(4)], axis=0)
                first = full.astype(BF16)
                a_ref[:, cols] = first
                if terms > 1:
                    b_ref[:, cols] = (full - first.astype(F32)).astype(BF16)
            ones = o_ref[...]
            grad = nt(a_ref[...], ones)
            if terms > 1:
                grad = grad + nt(b_ref[...], ones)
            dt_ref[block] += grad
        return loss

    loss = lax.fori_loop(0, views_ref[0], view, jnp.zeros((1, pixels), F32))
    loss_ref[...] = jnp.broadcast_to(jnp.sum(loss, axis=1, keepdims=True), loss_ref.shape)

    for ch in range(4):
        rows = slice(ch * NG, (ch + 1) * NG)
        at = ch * TABLE + NG
        tok_ref[rows, 0:width] = dt_ref[0, at - NG : at, :]
        tok_ref[rows, width : 2 * width] = dt_ref[1, at - NG : at, :]
        tok_ref[rows, width : width + 128] += rim_back(dt_ref[0, at + 4 : at + 8, :], 0)
        tok_ref[rows, width - 128 : width] += rim_back(dt_ref[1, at : at + 4, :], 112)
        edge_ref[rows, :] = rim_back(dt_ref[0, at : at + 4, :], 0) + rim_back(
            dt_ref[1, at + 4 : at + 8, :], 16
        )

    for part in range(parts + 1):
        grad_ref, cols = place(part)
        z = values(part)
        colour, gate, opacity = shade(z)
        d = [grad_ref[i * NG : (i + 1) * NG, cols] for i in range(4)]
        d_opacity = d[3]
        for i in range(3):
            d_opacity = d_opacity + d[i] * colour[i]
            zs_ref[part, pl.ds(i, NG, stride=GV), :] = d[i] * opacity * colour[i] * (1.0 - colour[i])
        both = d_opacity * opacity
        zs_ref[part, pl.ds(3, NG, stride=GV), :] = both * (1.0 - gate)
        for i in range(4, GV):
            zs_ref[part, pl.ds(i, NG, stride=GV), :] = both * z[i] * (-1.0 / (GV - 4))
    for i in range(parts):
        dz_ref[:, i * lanes : (i + 1) * lanes] = zs_ref[i]
    dzx_ref[...] = zs_ref[parts]


def render(views, inverse, zt, zx, rd, terms):
    tokens = zt.shape[1]
    pixels = rd.shape[-1]
    slots = 8 * pixels
    counter = np.arange(48, dtype=np.float32).reshape(16, 3)
    mix = (np.float32(0.8) * np.cos(np.float32(1.7) * counter + np.float32(0.3))).astype(np.float32)
    mix = jnp.broadcast_to(jnp.asarray(mix.T)[:, :, None], (3, 16, pixels))
    whole = lambda x: pl.BlockSpec(x.shape, lambda: (0,) * x.ndim)
    smem = pl.BlockSpec(memory_space=pltpu.SMEM)
    shape = jax.ShapeDtypeStruct
    return pl.pallas_call(
        functools.partial(render_kernel, terms),
        in_specs=[smem, smem, whole(zt), whole(zx), whole(rd), whole(mix)],
        out_specs=[whole(zt), whole(zx), pl.BlockSpec((8, 128), lambda: (0, 0))],
        out_shape=[shape(zt.shape, F32), shape(zx.shape, F32), shape((8, 128), F32)],
        scratch_shapes=[
            pltpu.VMEM((2, 4 * TABLE, 256), F32),
            pltpu.VMEM((2, 4 * TABLE, 256), BF16),
            pltpu.VMEM((2, 4 * TABLE, 256), BF16),
            pltpu.VMEM((256, slots), BF16),
            pltpu.VMEM((TABLE, slots), F32),
            pltpu.VMEM((4 * TABLE, slots), BF16),
            pltpu.VMEM((4 * TABLE, slots), BF16),
            pltpu.VMEM((2, 4 * TABLE, 256), F32),
            pltpu.VMEM((4 * NG, tokens), F32),
            pltpu.VMEM((4 * NG, 128), F32),
            pltpu.VMEM((tokens // 128 + 1, POUT, 128), F32),
        ],
        compiler_params=pltpu.CompilerParams(vmem_limit_bytes=48 * VMEM_MB),
        cost_estimate=pl.CostEstimate(
            flops=24 * slots * 4 * TABLE * 256 * 6, bytes_accessed=4 * 1024 * 1024, transcendentals=0
        ),
        name="render",
    )(views, inverse, zt, zx, rd, mix)


def flip_pairs(n, bit):
    return [(i, i ^ bit) for i in range(n)]


def swap(x, axis, bit):
    return lax.ppermute(x, axis, flip_pairs(lax.axis_size(axis), bit))


def total_sum(x):
    for axis in ("scene", "rows"):
        bit = 1
        while bit < lax.axis_size(axis):
            x = x + swap(x, axis, bit)
            bit = 2 * bit
    return x


def gather_plain(shard):
    return lax.all_gather(
        lax.all_gather(shard, "rows", axis=1, tiled=True), "scene", axis=0, tiled=True
    )


def scatter_plain(grad):
    part = lax.psum_scatter(grad, "scene", scatter_dimension=0, tiled=True)
    return lax.psum_scatter(part, "rows", scatter_dimension=1, tiled=True).astype(F32)


def to_items(x):
    scenes, rows = lax.axis_size("scene"), lax.axis_size("rows")
    z = lax.axis_index("rows")
    pairs = [[], []]
    for s in range(scenes):
        for b in range(rows):
            for turn in range(2):
                m = (b % 2) ^ turn
                to = ((s // 2) * 2 + b // 2) * rows + 2 * m + s % 2
                pairs[turn].append((s * rows + b, to))
    even = z % 2 == 0
    first = lax.ppermute(jnp.where(even, x[0], x[1]), ("scene", "rows"), pairs[0])
    second = lax.ppermute(jnp.where(even, x[1], x[0]), ("scene", "rows"), pairs[1])
    early = z // 2 == 0
    return jnp.stack([jnp.where(early, first, second), jnp.where(early, second, first)])


def body(patches, scene_length, target_views, gauss_index, raster_weight, target_color, *state):
    masters, moments, averages = state[:7], state[7:14], state[14:]
    vectors = masters[6]
    scene, row = lax.axis_index("scene"), lax.axis_index("rows")
    side = scene % 2
    item_m, item_s = row // 2, (scene // 2) * 2 + row % 2
    block_rows = patches.shape[2]
    tokens = 2 * block_rows
    length = scene_length[item_m, item_s]
    views = target_views[item_m, item_s].reshape(1)
    lens = jnp.stack([length - side * tokens, length - (1 - side) * tokens])
    pixel_count = jnp.sum(target_views).astype(F32) * (
        raster_weight.shape[-1] * lax.axis_size("rows")
    )
    perm = jnp.concatenate([jnp.arange(8, dtype=jnp.int32)] * 2)

    gains = [vectors[None, i * D : (i + 1) * D] for i in range(9)]
    bias_up = vectors[None, 9 * D : 9 * D + FF]
    bias_gauss = vectors[9 * D + FF :]

    low = [w.astype(BF16) for w in masters[:6]]
    low[0] = low[0].T
    weights = [gather_plain(w) for w in low]
    w_patch, w_joint, w_out, w_up, w_down, w_gauss = weights

    x = to_items(patches[:, 0]).reshape(tokens, -1)
    drawn = jnp.concatenate(
        [gauss_index[:, 0].astype(F32), raster_weight[:, 0], target_color[:, 0]], axis=1
    )
    rd = to_items(jnp.transpose(drawn, (0, 2, 1, 3)))

    h0, a1 = embed(perm, x, w_patch, gains[6], gains[0], gains[3])
    p = nn(a1, w_joint).astype(BF16)
    kv = swap(p[:, D:], "scene", 1)
    mixed, logs = attend(perm, lens, p, kv)
    h1, a2 = project(perm, mixed, w_out, h0, gains[7], gains[1], gains[4])
    u, act = up_project(perm, a2, w_up, bias_up)
    h2, a3 = project(perm, act, w_down, h1, gains[8], gains[2], gains[5])
    zt = lax.dot_general(w_gauss, a3, (((0,), (1,)), ((), ())), preferred_element_type=F32)
    zt = zt + bias_gauss[:, None]

    edge = swap(jnp.where(side == 0, zt[:, tokens - HT :], zt[:, :HT]), "scene", 1)
    before = jnp.where(side == 0, 0.0, edge)
    after = jnp.where(side == 0, edge, 0.0)
    zx = jnp.concatenate([before, after, jnp.zeros((POUT, 128 - 2 * HT), F32)], axis=1)
    dzt, dzx, loss = render(views, (1.0 / pixel_count).reshape(1), zt, zx, rd, 2)
    back = swap(jnp.where(side == 0, dzx[:, HT : 2 * HT], dzx[:, :HT]), "scene", 1)
    dzt = jnp.concatenate(
        [
            dzt[:, :HT] + jnp.where(side == 0, 0.0, back),
            dzt[:, HT : tokens - HT],
            dzt[:, tokens - HT :] + jnp.where(side == 0, back, 0.0),
        ],
        axis=1,
    )
    d_bias_gauss = jnp.sum(dzt, axis=1)
    dz = dzt.astype(BF16).T

    dw_gauss = tn(a3, dz).astype(BF16)
    dh2, dh2_low, sums3 = norm_back(perm, dz, w_gauss, h2, gains[2], None, False)
    dw_down = tn(act, dh2_low).astype(BF16)
    du, d_bias_up = down_back(perm, dh2_low, w_down, u)
    dw_up = tn(a2, du).astype(BF16)
    dh1, dh1_low, sums2 = norm_back(perm, du, w_up, h1, gains[1], dh2, False)
    dw_out = tn(mixed, dh1_low).astype(BF16)
    do = nt(dh1_low, w_out).astype(BF16)
    dq, own, far = attend_back(perm, lens, p, kv, do, logs)
    got = swap(far, "scene", 1)
    dkv = (own + got.astype(F32)).astype(BF16)
    dp = jnp.concatenate([dq, dkv[0], dkv[1]], axis=1)
    dw_joint = tn(a1, dp).astype(BF16)
    dh0_low, sums1 = norm_back(perm, dp, w_joint, h0, gains[0], dh1, True)
    dw_patch = tn(dh0_low, x).astype(BF16)

    reduced = [
        scatter_plain(g) for g in (dw_patch, dw_joint, dw_out, dw_up, dw_down, dw_gauss)
    ]
    reduced[0] = reduced[0].T
    vector_part = jnp.concatenate(
        [sums1[0], sums2[0], sums3[0], sums1[1], sums2[1], sums3[1], sums1[2], sums2[2], sums3[2]]
        + [d_bias_up[0], d_bias_gauss, loss[0]]
    )
    squares = sum(jnp.sum(item * item) for item in reduced)
    totals = total_sum(jnp.concatenate([vector_part, jnp.broadcast_to(squares, (128,))]).reshape(-1, 128))
    totals = totals.reshape(-1)
    vec = vectors.shape[0]
    vector_grad, loss_sum, square_sum = totals[:vec], totals[vec], totals[vec + 128]
    grad_norm = jnp.sqrt(square_sum + jnp.sum(vector_grad * vector_grad))
    factor = jnp.minimum(1.0, CLIP_NORM / (grad_norm + 1e-06))
    next_moments, next_weights, next_averages = ([], [], [])
    for grad, moment, master, average in zip(reduced + [vector_grad], moments, masters, averages):
        clipped = grad * factor
        moment_new = MOMENTUM * moment + clipped
        weight_new = master - STEP_RATE * (clipped + MOMENTUM * moment_new)
        next_moments.append(moment_new)
        next_weights.append(weight_new)
        next_averages.append(AVERAGE_DECAY * average + (1.0 - AVERAGE_DECAY) * weight_new)
    return (loss_sum, pixel_count, grad_norm, *next_moments, *next_weights, *next_averages)


def solution(mesh):
    item = P(None, "scene", None, None, "rows")
    weight_specs = (P("rows", "scene"),) + (P("scene", "rows"),) * 5 + (P(),)
    in_specs = (P(None, "scene", "rows", None), P(), P(), item, item, item) + 3 * weight_specs
    out_specs = (P(), P(), P()) + 3 * weight_specs
    return jax.shard_map(body, mesh=mesh, in_specs=in_specs, out_specs=out_specs, check_vma=False)
```

```python
import functools

import jax
import jax.numpy as jnp
import numpy as np
from jax import lax
from jax.experimental import pallas as pl
from jax.experimental.pallas import tpu as pltpu
from jax.sharding import PartitionSpec as P

D = 1024
HEADS = 16
HD = 64
FF = 4096
POUT = 768
HT = 16
GV = 12
NG = POUT // GV

EPSILON = 1e-05
CLIP_NORM = 0.002
STEP_RATE = 1250.0
MOMENTUM = 0.9
AVERAGE_DECAY = 0.9

F32 = jnp.float32
BF16 = jnp.bfloat16
HIGHEST = lax.Precision.HIGHEST
BLOCKS = 8
WIDE = D // BLOCKS
VMEM_MB = 1024 * 1024
VMEM = 28
TABLE = NG + 8


def nn(a, b):
    return lax.dot_general(a, b, (((1,), (0,)), ((), ())), preferred_element_type=F32)


def nt(a, b):
    return lax.dot_general(a, b, (((1,), (1,)), ((), ())), preferred_element_type=F32)


def tn(a, b):
    return lax.dot_general(a, b, (((0,), (0,)), ((), ())), preferred_element_type=F32)


def params(mb, n=1):
    return pltpu.CompilerParams(
        vmem_limit_bytes=mb * VMEM_MB, dimension_semantics=("arbitrary",) * n
    )


def lane_block(index, width):
    return pl.ds(pl.multiple_of(index * width, width), width)


PATCH = 144
GAUSS = POUT // 4


def side_rows(w_ref, place, first, count):
    return jnp.concatenate(
        [w_ref[j, place, first : first + count, :] for j in range(4)], axis=1
    )


def norm_store(perm, h_ref, g_ref, s_ref, a_ref, chunk):
    def step(i, carry):
        rows = pl.ds(pl.multiple_of(i * chunk, chunk), chunk)
        h = h_ref[rows, :]
        c = h - jnp.mean(h, axis=1, keepdims=True)
        var = jnp.mean(c * c, axis=1, keepdims=True)
        a = (c * lax.rsqrt(var + EPSILON) * g_ref[...] + s_ref[...]).astype(BF16)
        for b in range(BLOCKS):
            a_ref[rows, lane_block(perm[8 + b], WIDE)] = a[:, b * WIDE : (b + 1) * WIDE]
        return carry

    lax.fori_loop(0, h_ref.shape[0] // chunk, step, 0)


def rows_of(w_ref, z, width):
    block = w_ref[:, z]
    if block.shape[-1] != width:
        block = block[:, :, :width]
    return block.reshape(block.shape[0] * block.shape[1], width)


def embed_kernel(perm, x_ref, w0_ref, w1_ref, b_ref, g_ref, s_ref, h_ref, a_ref):
    x = x_ref[...]
    for i, w_ref in enumerate((w0_ref, w1_ref)):
        weight = jnp.concatenate(
            [side_rows(w_ref, perm[16 + z], 0, PATCH) for z in range(4)], axis=0
        )
        hr = nn(x, weight)
        for j in range(BLOCKS // 2):
            cols = lane_block(perm[i * BLOCKS // 2 + j], WIDE)
            h_ref[:, cols] = hr[:, j * WIDE : (j + 1) * WIDE] + b_ref[:, cols]
    norm_store(perm, h_ref, g_ref, s_ref, a_ref, 32)


def embed(perm, x, chunk, b, g, s):
    rows = x.shape[0]
    part = 256
    full = lambda shape: pl.BlockSpec(shape, lambda i, p: (0, 0))
    tile = lambda n: pl.BlockSpec((part, n), lambda i, p: (i, 0))
    weight = pl.BlockSpec((4, 4, PATCH + GAUSS, WIDE), lambda i, p: (0, 0, 0, 0))
    return pl.pallas_call(
        embed_kernel,
        grid_spec=pltpu.PrefetchScalarGridSpec(
            num_scalar_prefetch=1,
            grid=(rows // part,),
            in_specs=[tile(x.shape[1]), weight, weight]
            + [full((1, D))] * 3,
            out_specs=[tile(D), tile(D)],
        ),
        out_shape=[jax.ShapeDtypeStruct((rows, D), F32), jax.ShapeDtypeStruct((rows, D), BF16)],
        compiler_params=params(VMEM),
        cost_estimate=pl.CostEstimate(
            flops=2 * rows * D * 576, bytes_accessed=rows * D * 6 + 4 * D * 576, transcendentals=0
        ),
        name="embed_norm",
    )(perm, x, *chunk, b, g, s)


def first_of(chunk):
    return (0, 0) if chunk[0].shape[0] == 4 else (0, 1)


def project_kernel(perm, a_ref, w0_ref, w1_ref, r_ref, b_ref, g_ref, s_ref, h_ref, n_ref):
    z = pl.program_id(0)
    middle = a_ref.shape[1] // 2
    width = D // 4
    cols = lane_block(z, width)
    h_ref[:, cols] = (
        r_ref[...]
        + b_ref[...]
        + nn(a_ref[:, :middle], rows_of(w0_ref, 0, width))
        + nn(a_ref[:, middle:], rows_of(w1_ref, 0, width))
    )

    @pl.when(z == pl.num_programs(0) - 1)
    def _():
        norm_store(perm, h_ref, g_ref, s_ref, n_ref, 32)


def project(perm, a, chunk, at, res, b, g, s):
    rows, depth = a.shape
    width = D // 4
    full = lambda shape: pl.BlockSpec(shape, lambda z, p: (0, 0))
    weights = [
        pl.BlockSpec((4, 1, depth // 8, width), lambda z, p, i=i: (i, p[16 + z], 0, at))
        for i in first_of(chunk)
    ]
    return pl.pallas_call(
        project_kernel,
        grid_spec=pltpu.PrefetchScalarGridSpec(
            num_scalar_prefetch=1,
            grid=(4,),
            in_specs=[
                full((rows, depth)),
                *weights,
                pl.BlockSpec((rows, width), lambda z, p: (0, z)),
                pl.BlockSpec((1, width), lambda z, p: (0, z)),
                full((1, D)),
                full((1, D)),
            ],
            out_specs=[full((rows, D)), full((rows, D))],
        ),
        out_shape=[jax.ShapeDtypeStruct((rows, D), F32), jax.ShapeDtypeStruct((rows, D), BF16)],
        compiler_params=params(VMEM),
        cost_estimate=pl.CostEstimate(
            flops=2 * rows * D * depth,
            bytes_accessed=rows * D * 10 + 2 * D * depth + 2 * rows * depth,
            transcendentals=0,
        ),
        name="project_norm",
    )(perm, a, *chunk, res, b, g, s)


def halves(a_ref, w0_ref, w1_ref, width):
    middle = a_ref.shape[1] // 2
    return nn(a_ref[:, :middle], rows_of(w0_ref, 0, width)) + nn(
        a_ref[:, middle:], rows_of(w1_ref, 0, width)
    )


def joint_kernel(perm, a_ref, w0_ref, w1_ref, p_ref):
    p_ref[...] = halves(a_ref, w0_ref, w1_ref, p_ref.shape[1]).astype(BF16)


def joint(perm, a, chunk):
    rows = a.shape[0]
    part = 3 * D // 4
    weight = pl.BlockSpec((4, 1, WIDE, part), lambda z, p: (0, p[16 + z], 0, 0))
    return pl.pallas_call(
        joint_kernel,
        grid_spec=pltpu.PrefetchScalarGridSpec(
            num_scalar_prefetch=1,
            grid=(4,),
            in_specs=[pl.BlockSpec((rows, D), lambda z, p: (0, 0)), weight, weight],
            out_specs=pl.BlockSpec((rows, part), lambda z, p: (0, z)),
        ),
        out_shape=jax.ShapeDtypeStruct((rows, 3 * D), BF16),
        compiler_params=params(VMEM),
        cost_estimate=pl.CostEstimate(
            flops=6 * rows * D * D, bytes_accessed=rows * D * 8 + 6 * D * D, transcendentals=0
        ),
        name="joint",
    )(perm, a, *chunk)


def gauss_kernel(perm, a_ref, w0_ref, w1_ref, b_ref, z_ref):
    half = D // 2
    z_ref[...] = (
        nt(side_rows(w0_ref, 0, PATCH, GAUSS), a_ref[:, :half])
        + nt(side_rows(w1_ref, 0, PATCH, GAUSS), a_ref[:, half:])
        + b_ref[...]
    )


def gauss(perm, a, chunk, b):
    rows = a.shape[0]
    weight = pl.BlockSpec((4, 1, PATCH + GAUSS, WIDE), lambda z, p: (0, p[16 + z], 0, 0))
    return pl.pallas_call(
        gauss_kernel,
        grid_spec=pltpu.PrefetchScalarGridSpec(
            num_scalar_prefetch=1,
            grid=(4,),
            in_specs=[
                pl.BlockSpec((rows, D), lambda z, p: (0, 0)),
                weight,
                weight,
                pl.BlockSpec((GAUSS, 1), lambda z, p: (z, 0)),
            ],
            out_specs=pl.BlockSpec((GAUSS, rows), lambda z, p: (z, 0)),
        ),
        out_shape=jax.ShapeDtypeStruct((POUT, rows), F32),
        compiler_params=params(VMEM),
        cost_estimate=pl.CostEstimate(
            flops=2 * rows * D * POUT, bytes_accessed=rows * D * 5 + 2 * D * POUT, transcendentals=0
        ),
        name="gauss",
    )(perm, a, *chunk, b[:, None])


def out_back_kernel(perm, d_ref, w0_ref, w1_ref, o_ref):
    width = D // 4
    for i, w_ref in enumerate((w0_ref, w1_ref)):
        total = sum(
            nt(d_ref[:, z * width : (z + 1) * width], rows_of(w_ref, perm[16 + z], width))
            for z in range(4)
        )
        o_ref[:, i * D // 2 : (i + 1) * D // 2] = total.astype(BF16)


def out_back(perm, d, chunk):
    rows = d.shape[0]
    part = 256
    weight = pl.BlockSpec((4, 4, WIDE, D // 4), lambda i, p: (0, 0, 0, 4))
    tile = pl.BlockSpec((part, D), lambda i, p: (i, 0))
    return pl.pallas_call(
        out_back_kernel,
        grid_spec=pltpu.PrefetchScalarGridSpec(
            num_scalar_prefetch=1,
            grid=(rows // part,),
            in_specs=[tile, weight, weight],
            out_specs=tile,
        ),
        out_shape=jax.ShapeDtypeStruct((rows, D), BF16),
        compiler_params=params(VMEM),
        cost_estimate=pl.CostEstimate(
            flops=2 * rows * D * D, bytes_accessed=rows * D * 4 + 2 * D * D, transcendentals=0
        ),
        name="out_back",
    )(perm, d, *chunk)


def grad_kernel(perm, a_ref, d_ref, *refs):
    *outs, turned_ref = refs
    middle = a_ref.shape[1] // 2

    @pl.when(pl.program_id(0) == 0)
    def _():
        turned_ref[...] = a_ref[...].T

    for i in (1, 0):
        g = nn(turned_ref[i * middle : (i + 1) * middle, :], d_ref[...]).astype(BF16)
        g = g.reshape(4, 1, middle // 4, g.shape[1])
        if len(outs) == 2:
            outs[i][...] = g
        else:
            for j in range(4):
                outs[0][perm[4 * i + j]] = g[j]


def weight_grad(perm, a, d, whole=False):
    tokens, depth = a.shape
    n = d.shape[1] // 4
    right = pl.BlockSpec((tokens, n), lambda z, p: (0, z))
    count = 8 if whole else 4
    out = pl.BlockSpec((count, 1, depth // 8, n), lambda z, p: (0, p[16 + z], 0, 0))
    shape = jax.ShapeDtypeStruct((count, 4, depth // 8, n), BF16)
    return pl.pallas_call(
        grad_kernel,
        grid_spec=pltpu.PrefetchScalarGridSpec(
            num_scalar_prefetch=1,
            grid=(4,),
            in_specs=[pl.BlockSpec((tokens, depth), lambda z, p: (0, 0)), right],
            out_specs=[out] * (8 // count),
            scratch_shapes=[pltpu.VMEM((depth, tokens), BF16)],
        ),
        out_shape=[shape] * (8 // count),
        compiler_params=params(VMEM),
        cost_estimate=pl.CostEstimate(
            flops=8 * tokens * depth * n,
            bytes_accessed=2 * tokens * (depth + 4 * n) + 8 * depth * n,
            transcendentals=0,
        ),
        name="weight_grad",
    )(perm, a, d)


def side_grad_kernel(perm, d_ref, a_ref, *outs):
    g = nn(d_ref[...], a_ref[...]).astype(BF16)
    for j in range(BLOCKS):
        block = g[:, j * WIDE : (j + 1) * WIDE]
        if len(outs) == 2:
            outs[j // 4][j % 4, 0] = block
        else:
            outs[0][perm[j], 0] = block


def side_grad(perm, d, a, whole=False):
    tokens = a.shape[0]
    n = d.shape[0] // 4
    count = 8 if whole else 4
    out = pl.BlockSpec((count, 1, n, WIDE), lambda z, p: (0, p[16 + z], 0, 0))
    shape = jax.ShapeDtypeStruct((count, 4, n, WIDE), BF16)
    return pl.pallas_call(
        side_grad_kernel,
        grid_spec=pltpu.PrefetchScalarGridSpec(
            num_scalar_prefetch=1,
            grid=(4,),
            in_specs=[
                pl.BlockSpec((n, tokens), lambda z, p: (z, 0)),
                pl.BlockSpec((tokens, D), lambda z, p: (0, 0)),
            ],
            out_specs=[out] * (8 // count),
        ),
        out_shape=[shape] * (8 // count),
        compiler_params=params(VMEM),
        cost_estimate=pl.CostEstimate(
            flops=8 * tokens * D * n, bytes_accessed=2 * tokens * D + 16 * D * n, transcendentals=0
        ),
        name="side_grad",
    )(perm, d, a)


GELU_C = float(np.sqrt(2.0 / np.pi))


def up_kernel(perm, a_ref, w0_ref, w1_ref, b_ref, u_ref, g_ref):
    u = halves(a_ref, w0_ref, w1_ref, u_ref.shape[1]) + b_ref[...]
    u_ref[...] = u
    t = jnp.tanh(GELU_C * (u + 0.044715 * (u * u * u)))
    g_ref[...] = (u * (0.5 * (1.0 + t))).astype(BF16)


def up_project(perm, a, chunk, b):
    rows = a.shape[0]
    part = FF // BLOCKS
    weight = pl.BlockSpec((4, 1, WIDE, part), lambda n, p: (0, p[16 + n // 2], 0, n % 2))
    return pl.pallas_call(
        up_kernel,
        grid_spec=pltpu.PrefetchScalarGridSpec(
            num_scalar_prefetch=1,
            grid=(BLOCKS,),
            in_specs=[
                pl.BlockSpec((rows, D), lambda n, p: (0, 0)),
                weight,
                weight,
                pl.BlockSpec((1, part), lambda n, p: (0, n)),
            ],
            out_specs=[
                pl.BlockSpec((rows, part), lambda n, p: (0, n)),
                pl.BlockSpec((rows, part), lambda n, p: (0, p[8 + n])),
            ],
        ),
        out_shape=[jax.ShapeDtypeStruct((rows, FF), F32), jax.ShapeDtypeStruct((rows, FF), BF16)],
        compiler_params=params(VMEM),
        cost_estimate=pl.CostEstimate(
            flops=2 * rows * D * FF, bytes_accessed=rows * FF * 6 + 2 * D * FF, transcendentals=rows * FF
        ),
        name="up_gelu",
    )(perm, a, *chunk, b)


def down_back_kernel(perm, d_ref, w0_ref, w1_ref, u_ref, du_ref, sum_ref, dg_ref):
    width = D // 4

    def product(w_ref):
        dg_ref[...] = sum(
            nt(d_ref[:, z * width : (z + 1) * width], rows_of(w_ref, perm[16 + z], width))
            for z in range(4)
        )

    first = pl.program_id(0) < pl.num_programs(0) // 2
    pl.when(first)(lambda: product(w0_ref))
    pl.when(jnp.logical_not(first))(lambda: product(w1_ref))
    dg = dg_ref[...]
    u = u_ref[...]
    u2 = u * u
    t = jnp.tanh(GELU_C * (u + 0.044715 * (u2 * u)))
    slope = 0.5 * (1.0 + t) + (0.5 * GELU_C) * u * (1.0 - t * t) * (1.0 + (3 * 0.044715) * u2)
    du = slope * dg
    du_ref[...] = du.astype(BF16)
    sum_ref[...] = jnp.sum(du, axis=0, keepdims=True)


def down_back(perm, d, chunk, u):
    rows = d.shape[0]
    second = 4 * first_of(chunk)[1]
    part = FF // BLOCKS
    return pl.pallas_call(
        down_back_kernel,
        grid_spec=pltpu.PrefetchScalarGridSpec(
            num_scalar_prefetch=1,
            grid=(BLOCKS,),
            in_specs=[
                pl.BlockSpec((rows, D), lambda j, p: (0, 0)),
                pl.BlockSpec((1, 4, part, D // 4), lambda j, p: (jnp.minimum(j, 3), 0, 0, 0)),
                pl.BlockSpec(
                    (1, 4, part, D // 4), lambda j, p: (jnp.maximum(j - 4, 0) + second, 0, 0, 0)
                ),
                pl.BlockSpec((rows, part), lambda j, p: (0, p[j])),
            ],
            out_specs=[
                pl.BlockSpec((rows, part), lambda j, p: (0, p[j])),
                pl.BlockSpec((1, part), lambda j, p: (0, p[j])),
            ],
            scratch_shapes=[pltpu.VMEM((rows, part), F32)],
        ),
        out_shape=[jax.ShapeDtypeStruct((rows, FF), BF16), jax.ShapeDtypeStruct((1, FF), F32)],
        compiler_params=params(VMEM),
        cost_estimate=pl.CostEstimate(
            flops=2 * rows * D * FF, bytes_accessed=rows * FF * 6 + 2 * D * FF, transcendentals=rows * FF
        ),
        name="down_back_gelu",
    )(perm, d, *chunk, u)


def back_kernel(has_res, placed, turned, perm, *refs):
    if has_res:
        d_ref, w0_ref, w1_ref, h_ref, g_ref, r_ref, *outs = refs
    else:
        d_ref, w0_ref, w1_ref, h_ref, g_ref, *outs = refs
        r_ref = None
    if placed:
        low_ref, sums_ref, acc_ref, part_ref = outs
        dh_ref = None
    else:
        dh_ref, low_ref, sums_ref, acc_ref, part_ref = outs
    n = pl.program_id(0)

    if turned:
        d = d_ref[...].T
        for i, w_ref in enumerate((w0_ref, w1_ref)):
            weight = jnp.concatenate(
                [side_rows(w_ref, perm[16 + z], PATCH, GAUSS) for z in range(4)], axis=0
            )
            acc_ref[:, i * D // 2 : (i + 1) * D // 2] = nn(d, weight)
    else:
        d = d_ref[...]
        width = d.shape[1]

        @pl.when(n == 0)
        def _():
            acc_ref[:, : D // 2] = nt(d, rows_of(w0_ref, 0, width))
            acc_ref[:, D // 2 :] = nt(d, rows_of(w1_ref, 0, width))

        @pl.when(n > 0)
        def _():
            acc_ref[:, : D // 2] += nt(d, rows_of(w0_ref, 0, width))
            acc_ref[:, D // 2 :] += nt(d, rows_of(w1_ref, 0, width))

    @pl.when(n == pl.num_programs(0) - 1)
    def _():
        chunk = 32
        part_ref[...] = jnp.zeros_like(part_ref)

        def fold(x):
            return jnp.sum(x.reshape(chunk // 8, 8, D), axis=0)

        def step(i, carry):
            rows = pl.ds(pl.multiple_of(i * chunk, chunk), chunk)
            h = h_ref[rows, :]
            c = h - jnp.mean(h, axis=1, keepdims=True)
            var = jnp.mean(c * c, axis=1, keepdims=True)
            rstd = lax.rsqrt(var + EPSILON)
            xh = c * rstd
            da = jnp.concatenate(
                [acc_ref[rows, lane_block(perm[8 + b], WIDE)] for b in range(BLOCKS)], axis=1
            )
            dxh = da * xh
            part_ref[0] += fold(dxh)
            part_ref[1] += fold(da)
            dy = da * g_ref[...]
            first = jnp.mean(dy, axis=1, keepdims=True)
            second = jnp.mean(dy * xh, axis=1, keepdims=True)
            dh = rstd * (dy - first - xh * second)
            if has_res:
                dh = dh + r_ref[rows, :]
            part_ref[2] += fold(dh)
            low = dh.astype(BF16)
            if placed:
                for b in range(BLOCKS):
                    low_ref[rows, lane_block(perm[8 + b], WIDE)] = low[:, b * WIDE : (b + 1) * WIDE]
            else:
                dh_ref[rows, :] = dh
                low_ref[rows, :] = low
            return carry

        lax.fori_loop(0, h_ref.shape[0] // chunk, step, 0)
        sums_ref[...] = jnp.concatenate(
            [jnp.sum(part_ref[i], axis=0, keepdims=True) for i in range(3)]
            + [jnp.zeros((5, D), F32)],
            axis=0,
        )


def norm_back(perm, d, chunk, turned, h, g, res, placed):
    full = lambda shape: pl.BlockSpec(shape, lambda n, p: (0, 0))
    rows = h.shape[0]
    wide = d.size // rows
    if turned:
        left = full(d.shape)
        weight = pl.BlockSpec((4, 4, PATCH + GAUSS, WIDE), lambda n, p: (0, 0, 0, 0))
    else:
        part = wide // 4
        left = pl.BlockSpec((rows, part), lambda n, p: (0, n))
        weight = pl.BlockSpec((4, 1, WIDE, part), lambda n, p: (0, p[16 + n], 0, 0))
    args = [d, *chunk, h, g]
    specs = [left, weight, weight, full((rows, D)), full((1, D))]
    if res is not None:
        args.append(res)
        specs.append(full((rows, D)))
    out_specs = [full((rows, D)), full((8, D))]
    out_shape = [jax.ShapeDtypeStruct((rows, D), BF16), jax.ShapeDtypeStruct((8, D), F32)]
    if not placed:
        out_specs = [full((rows, D))] + out_specs
        out_shape = [jax.ShapeDtypeStruct((rows, D), F32)] + out_shape
    return pl.pallas_call(
        functools.partial(back_kernel, res is not None, placed, turned),
        grid_spec=pltpu.PrefetchScalarGridSpec(
            num_scalar_prefetch=1,
            grid=(1 if turned else 4,),
            in_specs=specs,
            out_specs=out_specs,
            scratch_shapes=[pltpu.VMEM((rows, D), F32), pltpu.VMEM((3, 8, D), F32)],
        ),
        out_shape=out_shape,
        compiler_params=params(VMEM),
        cost_estimate=pl.CostEstimate(
            flops=2 * rows * D * wide,
            bytes_accessed=rows * D * 14 + 2 * D * wide + 2 * rows * wide,
            transcendentals=0,
        ),
        name="norm_back",
    )(perm, *args)


SCALE = HD ** (-0.5)
PAIR = 2 * HD
PAIRS = HEADS // 2


def lanes_of(side):
    lane = lax.broadcasted_iota(jnp.int32, (1, PAIR), 1)
    mine = (lane < HD) == (side == 0)
    return lane, mine, HD * (1 - side)


def masked_keys(keys, first, length, extra):
    lane, mine, free = first
    spot = lax.broadcasted_iota(jnp.int32, (keys.shape[0], 1), 0)
    hidden = jnp.where(spot < length, 0.0, -1e30).astype(BF16)
    rest = jnp.where(lane == free, hidden, 0.0).astype(BF16)
    if extra:
        ones = jnp.logical_and(lane > free, lane <= free + extra)
        rest = jnp.where(ones, 1.0, rest).astype(BF16)
    return jnp.where(mine, keys, rest)


def attend_kernel(perm, lens, q_ref, k0_ref, k1_ref, v0_ref, v1_ref, o_ref, l_ref):
    v0, v1 = v0_ref[...], v1_ref[...]
    sides = [lanes_of(side) for side in range(2)]
    keys = [
        [masked_keys(ref[...], where, lens[j], 0) for j, ref in enumerate((k0_ref, k1_ref))]
        for where in sides
    ]
    chunk = 256
    for i in range(q_ref.shape[0] // chunk):
        rows = slice(i * chunk, (i + 1) * chunk)
        q = (q_ref[rows, :] * SCALE).astype(BF16)
        outs = []
        logs = []
        for (lane, mine, free), (k0, k1) in zip(sides, keys):
            qm = jnp.where(mine, q, jnp.where(lane == free, 1.0, 0.0).astype(BF16))
            s0 = nt(qm, k0)
            s1 = nt(qm, k1)
            top = jnp.max(jnp.maximum(s0, s1), axis=1, keepdims=True)
            e0 = jnp.exp(s0 - top)
            e1 = jnp.exp(s1 - top)
            total = jnp.sum(e0 + e1, axis=1, keepdims=True)
            outs.append((nn(e0.astype(BF16), v0) + nn(e1.astype(BF16), v1)) * (1.0 / total))
            logs.append(top + jnp.log(total))
        lane = sides[0][0]
        o_ref[rows, :] = jnp.where(lane < HD, outs[0], outs[1]).astype(BF16)
        l_ref[rows, :] = jnp.where(lane < HD, logs[1], logs[0])


def attend(perm, lens, p, kv):
    rows = p.shape[0]
    block = lambda first: pl.BlockSpec((rows, PAIR), lambda h, m, n: (0, first + h))
    return pl.pallas_call(
        attend_kernel,
        grid_spec=pltpu.PrefetchScalarGridSpec(
            num_scalar_prefetch=2,
            grid=(PAIRS,),
            in_specs=[block(0), block(PAIRS), block(0), block(2 * PAIRS), block(PAIRS)],
            out_specs=[
                pl.BlockSpec((rows, PAIR), lambda h, m, n: (0, m[8 + h])),
                block(0),
            ],
        ),
        out_shape=[
            jax.ShapeDtypeStruct((rows, D), BF16),
            jax.ShapeDtypeStruct((rows, D), F32),
        ],
        compiler_params=params(VMEM),
        cost_estimate=pl.CostEstimate(
            flops=8 * rows * rows * D,
            bytes_accessed=12 * rows * D,
            transcendentals=2 * rows * rows * HEADS,
        ),
        name="attend",
    )(perm, lens, p, p, kv, p, kv)


def attend_back_kernel(
    perm, lens, q_ref, k0_ref, k1_ref, v0_ref, v1_ref, do_ref, l_ref, dq_ref, own_ref, far_ref
):
    values = [v0_ref[...], v1_ref[...]]
    q_all, do_all = q_ref[...], do_ref[...]
    sides = [lanes_of(side) for side in range(2)]
    keys = [
        [masked_keys(ref[...], where, lens[j], 3) for j, ref in enumerate((k0_ref, k1_ref))]
        for where in sides
    ]
    chunk = 256
    dk = [None, None]
    dv = [None, None]
    for i in range(q_ref.shape[0] // chunk):
        rows = slice(i * chunk, (i + 1) * chunk)
        logs = l_ref[rows, :]
        first = logs.astype(BF16)
        left = logs - first.astype(F32)
        second = left.astype(BF16)
        third = (left - second.astype(F32)).astype(BF16)
        dqs = []
        for (lane, mine, free), (k0, k1) in zip(sides, keys):
            qm = jnp.where(mine, q_all[rows, :], 0.0).astype(BF16)
            dom = jnp.where(mine, do_all[rows, :], 0.0).astype(BF16)
            rest = jnp.where(lane == free, 1.0, 0.0).astype(BF16)
            for at, part in enumerate((first, second, third)):
                rest = jnp.where(lane == free + 1 + at, -part, rest)
            qs = jnp.where(mine, (q_all[rows, :] * SCALE).astype(BF16), rest)
            probs = [jnp.exp(nt(k, qs)) for k in (k0, k1)]
            da = [nt(v, dom) for v in values]
            delta = jnp.sum(probs[0] * da[0] + probs[1] * da[1], axis=0, keepdims=True)
            dq = None
            for j, k in enumerate((k0, k1)):
                ds = (probs[j] * (da[j] - delta)).astype(BF16)
                term = tn(ds, k)
                dq = term if dq is None else dq + term
                term = nn(ds, qm)
                dk[j] = term if dk[j] is None else dk[j] + term
                term = nn(probs[j].astype(BF16), dom)
                dv[j] = term if dv[j] is None else dv[j] + term
            dqs.append(dq)
        lane = sides[0][0]
        dq_ref[rows, :] = (jnp.where(lane < HD, dqs[0], dqs[1]) * SCALE).astype(BF16)
    own_ref[0] = dk[0] * SCALE
    own_ref[1] = dv[0]
    far_ref[0] = (dk[1] * SCALE).astype(BF16)
    far_ref[1] = dv[1].astype(BF16)


def attend_back(perm, lens, p, kv, do, logs):
    rows = p.shape[0]
    block = lambda first: pl.BlockSpec((rows, PAIR), lambda h, m, n: (0, first + h))
    both = pl.BlockSpec((2, rows, PAIR), lambda h, m, n: (0, 0, h))
    return pl.pallas_call(
        attend_back_kernel,
        grid_spec=pltpu.PrefetchScalarGridSpec(
            num_scalar_prefetch=2,
            grid=(PAIRS,),
            in_specs=[
                block(0),
                block(PAIRS),
                block(0),
                block(2 * PAIRS),
                block(PAIRS),
                pl.BlockSpec((rows, PAIR), lambda h, m, n: (0, m[8 + h])),
                block(0),
            ],
            out_specs=[block(0), both, both],
        ),
        out_shape=[
            jax.ShapeDtypeStruct((rows, D), BF16),
            jax.ShapeDtypeStruct((2, rows, D), F32),
            jax.ShapeDtypeStruct((2, rows, D), BF16),
        ],
        compiler_params=params(VMEM),
        cost_estimate=pl.CostEstimate(
            flops=20 * rows * rows * D,
            bytes_accessed=28 * rows * D,
            transcendentals=2 * rows * rows * HEADS,
        ),
        name="attend_back",
    )(perm, lens, p, p, kv, p, kv, do, logs)


def iota(shape, dim):
    return lax.broadcasted_iota(jnp.int32, shape, dim)


def render_kernel(
    views_ref, inv_ref, z_ref, zx_ref, rd_ref, mc_ref, dz_ref, dzx_ref, loss_ref,
    tf_ref, both_ref, o_ref, wm_ref, a_ref, dt_ref, tok_ref, edge_ref, zs_ref,
):
    width = 256
    pixels = rd_ref.shape[-1]
    kg = 8

    lanes = 128
    parts = z_ref.shape[1] // lanes
    for i in range(parts):
        zs_ref[i] = z_ref[:, i * lanes : (i + 1) * lanes]
    zs_ref[parts] = zx_ref[...]

    def values(i):
        return [zs_ref[i, pl.ds(v, NG, stride=GV), :] for v in range(GV)]

    def shade(z):
        colour = [jax.nn.sigmoid(z[i]) for i in range(3)]
        gate = jax.nn.sigmoid(z[3])
        square = z[4] * z[4]
        for i in range(5, GV):
            square = square + z[i] * z[i]
        opacity = gate * jnp.exp(-0.5 * (square / (GV - 4)))
        return colour, gate, opacity

    own_group = iota((NG, width), 0) % 16 == iota((NG, width), 1) // 16

    def spread(base):
        return (iota((128, width), 0) == base + iota((128, width), 1) % 16).astype(F32)

    def rim_rows(table, base):
        wide = lax.dot_general(
            table, spread(base), (((1,), (0,)), ((), ())), precision=HIGHEST,
            preferred_element_type=F32,
        )
        return jnp.sum(jnp.where(own_group, wide, 0.0).reshape(4, 16, width), axis=1)

    def rim_back(rows, base):
        wide = jnp.concatenate(
            [jnp.broadcast_to(rows[j : j + 1, :], (16, width)) for j in range(4)], axis=0
        )
        return lax.dot_general(
            jnp.where(own_group, wide, 0.0), spread(base), (((1,), (1,)), ((), ())),
            precision=HIGHEST, preferred_element_type=F32,
        )

    def place(i):
        if i == parts:
            return edge_ref, slice(0, lanes)
        return tok_ref, slice(i * lanes, (i + 1) * lanes)

    for i in range(parts + 1):
        out_ref, cols = place(i)
        colour, gate, opacity = shade(values(i))
        for ch in range(3):
            out_ref[ch * NG : (ch + 1) * NG, cols] = colour[ch] * opacity
        out_ref[3 * NG : 4 * NG, cols] = opacity

    for ch in range(4):
        rows = slice(ch * NG, (ch + 1) * NG)
        at = ch * TABLE
        tf_ref[0, at : at + NG, :] = tok_ref[rows, 0:width]
        tf_ref[1, at : at + NG, :] = tok_ref[rows, width : 2 * width]
        tf_ref[0, at + NG : at + NG + 4, :] = rim_rows(edge_ref[rows, :], 0)
        tf_ref[0, at + NG + 4 : at + NG + 8, :] = rim_rows(tok_ref[rows, width : width + 128], 0)
        tf_ref[1, at + NG : at + NG + 4, :] = rim_rows(tok_ref[rows, width - 128 : width], 112)
        tf_ref[1, at + NG + 4 : at + NG + 8, :] = rim_rows(edge_ref[rows, :], 16)
    for block in range(2):
        table = tf_ref[block]
        high = table.astype(BF16)
        both_ref[block, : 4 * TABLE] = high
        both_ref[block, 4 * TABLE :] = (table - high.astype(F32)).astype(BF16)
    dt_ref[...] = jnp.zeros_like(dt_ref)
    inverse = inv_ref[0]
    row_hi = iota((width, pixels), 0).astype(F32).astype(BF16)
    row_lo = iota((TABLE, pixels), 0)
    one_low, zero_low = jnp.ones((), BF16), jnp.zeros((), BF16)

    def features(c):
        return jnp.tanh(mc_ref[0] * c[0] + mc_ref[1] * c[1] + mc_ref[2] * c[2])

    def view(t, loss):
        for block in range(2):
            r = rd_ref[block, t, 0:kg, :].astype(jnp.int32)
            weight = rd_ref[block, t, kg : 2 * kg, :]
            token = lax.shift_right_logical(r, 6)
            g = jnp.bitwise_and(r, NG - 1)
            after = token >= HT + width
            inside = jnp.logical_and(token >= HT, jnp.logical_not(after))
            rim = jnp.where(after, token - (HT + width), token)
            high = jnp.where(inside, token - HT, jnp.bitwise_and(g, 15) * 16 + rim)
            low = jnp.where(
                inside, g, NG + lax.shift_right_logical(g, 4) + jnp.where(after, 4, 0)
            )
            sums = [jnp.zeros((8, pixels), F32) for _ in range(4)]
            high = high.astype(F32).astype(BF16)
            table = both_ref[block]
            for k in range(kg):
                cols = slice(k * pixels, (k + 1) * pixels)
                one = jnp.where(row_hi == high[k : k + 1, :], one_low, zero_low)
                o_ref[block, :, cols] = one
                wm = jnp.where(row_lo == low[k : k + 1, :], weight[k : k + 1, :], 0.0)
                wm_ref[block, :, cols] = wm
                picked = nn(table, one)
                picked = picked[: 4 * TABLE] + picked[4 * TABLE :]
                for ch in range(4):
                    part = picked[ch * TABLE : (ch + 1) * TABLE, :] * wm
                    sums[ch] = sums[ch] + jnp.sum(part.reshape(TABLE // 8, 8, pixels), axis=0)
            sums = [jnp.sum(s, axis=0, keepdims=True) for s in sums]
            scale = 1.0 / (1.0 + sums[3])
            seen = [sums[i] * scale for i in range(3)]
            goal = [rd_ref[block, t, 2 * kg + i : 2 * kg + i + 1, :] for i in range(3)]
            f_seen = features(seen)
            gap = f_seen - features(goal)
            diff = [seen[i] - goal[i] for i in range(3)]
            loss = loss + diff[0] * diff[0] + diff[1] * diff[1] + diff[2] * diff[2]
            loss = loss + 0.5 * jnp.sum(gap * gap, axis=0, keepdims=True)
            pull = gap * (1.0 - f_seen * f_seen)
            d_seen = [
                inverse * (2.0 * diff[i] + jnp.sum(pull * mc_ref[i], axis=0, keepdims=True))
                for i in range(3)
            ]
            d_sum = [d * scale for d in d_seen]
            d_sum.append(
                -(d_seen[0] * seen[0] + d_seen[1] * seen[1] + d_seen[2] * seen[2]) * scale
            )
            for k in range(kg):
                cols = slice(k * pixels, (k + 1) * pixels)
                wm = wm_ref[block, :, cols]
                full = jnp.concatenate([wm * d_sum[ch] for ch in range(4)], axis=0)
                a_ref[block, :, cols] = full.astype(BF16)
            dt_ref[block] += nt(a_ref[block], o_ref[block])
        return loss

    loss = lax.fori_loop(0, views_ref[0], view, jnp.zeros((1, pixels), F32))
    loss_ref[...] = jnp.broadcast_to(jnp.sum(loss, axis=1, keepdims=True), loss_ref.shape)

    for ch in range(4):
        rows = slice(ch * NG, (ch + 1) * NG)
        at = ch * TABLE + NG
        tok_ref[rows, 0:width] = dt_ref[0, at - NG : at, :]
        tok_ref[rows, width : 2 * width] = dt_ref[1, at - NG : at, :]
        tok_ref[rows, width : width + 128] += rim_back(dt_ref[0, at + 4 : at + 8, :], 0)
        tok_ref[rows, width - 128 : width] += rim_back(dt_ref[1, at : at + 4, :], 112)
        edge_ref[rows, :] = rim_back(dt_ref[0, at : at + 4, :], 0) + rim_back(
            dt_ref[1, at + 4 : at + 8, :], 16
        )

    for part in range(parts + 1):
        grad_ref, cols = place(part)
        z = values(part)
        colour, gate, opacity = shade(z)
        d = [grad_ref[i * NG : (i + 1) * NG, cols] for i in range(4)]
        d_opacity = d[3]
        for i in range(3):
            d_opacity = d_opacity + d[i] * colour[i]
            zs_ref[part, pl.ds(i, NG, stride=GV), :] = d[i] * opacity * colour[i] * (1.0 - colour[i])
        both = d_opacity * opacity
        zs_ref[part, pl.ds(3, NG, stride=GV), :] = both * (1.0 - gate)
        for i in range(4, GV):
            zs_ref[part, pl.ds(i, NG, stride=GV), :] = both * z[i] * (-1.0 / (GV - 4))
    for i in range(parts):
        dz_ref[:, i * lanes : (i + 1) * lanes] = zs_ref[i]
    dzx_ref[...] = zs_ref[parts]


def render(views, inverse, zt, zx, rd):
    tokens = zt.shape[1]
    pixels = rd.shape[-1]
    slots = 8 * pixels
    counter = np.arange(48, dtype=np.float32).reshape(16, 3)
    mix = (np.float32(0.8) * np.cos(np.float32(1.7) * counter + np.float32(0.3))).astype(np.float32)
    mix = jnp.broadcast_to(jnp.asarray(mix.T)[:, :, None], (3, 16, pixels))
    whole = lambda x: pl.BlockSpec(x.shape, lambda: (0,) * x.ndim)
    smem = pl.BlockSpec(memory_space=pltpu.SMEM)
    shape = jax.ShapeDtypeStruct
    return pl.pallas_call(
        render_kernel,
        in_specs=[smem, smem, whole(zt), whole(zx), whole(rd), whole(mix)],
        out_specs=[whole(zt), whole(zx), pl.BlockSpec((8, 128), lambda: (0, 0))],
        out_shape=[shape(zt.shape, F32), shape(zx.shape, F32), shape((8, 128), F32)],
        scratch_shapes=[
            pltpu.VMEM((2, 4 * TABLE, 256), F32),
            pltpu.VMEM((2, 8 * TABLE, 256), BF16),
            pltpu.VMEM((2, 256, slots), BF16),
            pltpu.VMEM((2, TABLE, slots), F32),
            pltpu.VMEM((2, 4 * TABLE, slots), BF16),
            pltpu.VMEM((2, 4 * TABLE, 256), F32),
            pltpu.VMEM((4 * NG, tokens), F32),
            pltpu.VMEM((4 * NG, 128), F32),
            pltpu.VMEM((tokens // 128 + 1, POUT, 128), F32),
        ],
        compiler_params=pltpu.CompilerParams(vmem_limit_bytes=VMEM * VMEM_MB),
        cost_estimate=pl.CostEstimate(
            flops=24 * slots * 4 * TABLE * 256 * 6, bytes_accessed=4 * 1024 * 1024, transcendentals=0
        ),
        name="render",
    )(views, inverse, zt, zx, rd, mix)


def flip_pairs(n, bit):
    return [(i, i ^ bit) for i in range(n)]


def swap(x, axis, bit):
    return lax.ppermute(x, axis, flip_pairs(lax.axis_size(axis), bit))


def total_sum(x):
    for axis in ("scene", "rows"):
        bit = 1
        while bit < lax.axis_size(axis):
            x = x + swap(x, axis, bit)
            bit = 2 * bit
    return x


def gather_whole(shard):
    whole = lax.all_gather(shard, ("scene", "rows"), axis=0)
    return (whole.reshape((BLOCKS, 4) + shard.shape),) * 2


def scatter_whole(grad):
    part = lax.psum_scatter(grad[0], "scene", scatter_dimension=0)
    return lax.psum_scatter(part, "rows", scatter_dimension=0).astype(F32)


def gather_plain(shards, turned):
    parts = []
    for shard in shards:
        if turned:
            wide = lax.all_gather(shard, "rows", axis=0, tiled=True)
            full = lax.all_gather(wide, "scene", axis=1, tiled=True)
            parts.append(jnp.transpose(full.reshape(4, -1, BLOCKS, WIDE), (2, 0, 1, 3)))
        else:
            wide = lax.all_gather(shard, "rows", axis=1, tiled=True)
            full = lax.all_gather(wide, "scene", axis=0, tiled=True)
            blocks = full.reshape(BLOCKS, full.shape[0] // BLOCKS, 4, -1)
            parts.append(jnp.transpose(blocks, (0, 2, 1, 3)))
    chunk = jnp.concatenate(parts, axis=2 if turned else 3)
    return chunk[:4], chunk[4:]


def scatter_plain(grad, turned):
    both = jnp.concatenate(grad, axis=0)
    if turned:
        full = jnp.transpose(both, (1, 2, 0, 3)).reshape(-1, D)
    else:
        full = jnp.transpose(both, (0, 2, 1, 3)).reshape(both.shape[0] * both.shape[2], -1)
    part = lax.psum_scatter(full, "scene", scatter_dimension=int(turned), tiled=True)
    return lax.psum_scatter(part, "rows", scatter_dimension=1 - turned, tiled=True).astype(F32)


CORE, XBIT, YBIT = 1, 2, 4
PLACES = np.array([0, 2, 4, 6, 1, 3, 5, 7], np.int32)


def stack_kernel(*refs):
    *parts, out_ref = refs
    for i, ref in enumerate(parts):
        out_ref[i] = ref[...]


def stack(parts):
    shape = parts[0].shape
    lead = shape[:-2]
    steps = lead[0] if lead else 1
    block = (1,) * len(lead) + shape[-2:]
    rest = (0,) * (len(shape) - 1) if lead else (0, 0)
    place = lambda i: ((i,) + rest) if lead else rest
    return pl.pallas_call(
        stack_kernel,
        grid=(steps,),
        in_specs=[pl.BlockSpec(block, place)] * len(parts),
        out_specs=pl.BlockSpec((len(parts),) + block, lambda i: (0,) + place(i)),
        out_shape=jax.ShapeDtypeStruct((len(parts),) + shape, parts[0].dtype),
        compiler_params=params(VMEM),
        cost_estimate=pl.CostEstimate(
            flops=0, bytes_accessed=4 * len(parts) * parts[0].size, transcendentals=0
        ),
        name="stack",
    )(*parts)


def tie(x, *earlier):
    return lax.optimization_barrier((x,) + earlier)[0]


def share_rows(x):
    return lax.all_to_all(x, "rows", 0, 0)


class Gather:
    def __init__(self, shard, order):
        self.shard = shard
        self.first, self.second = (XBIT, YBIT) if order == "xy" else (YBIT, XBIT)

    def rows(self, *earlier):
        shard = tie(self.shard, *earlier)
        self.own = share_rows(jnp.broadcast_to(shard[None], (4,) + shard.shape))

    def near(self, *earlier):
        self.own = tie(self.own, *earlier)
        self.one = swap(self.own, "scene", self.first)
        self.two = swap(self.own, "scene", self.second)
        return self.own

    def cross(self, *earlier):
        self.one = tie(self.one, *earlier)
        self.both = swap(self.one, "scene", self.second)
        return self.one

    def core(self, *earlier):
        x, y = (self.one, self.two) if self.first == XBIT else (self.two, self.one)
        self.half = stack([tie(self.own, *earlier), x, y, self.both])
        return self.half

    def get(self):
        return self.half, swap(self.half, "scene", CORE)


class Scatter:
    def __init__(self, grad, streams):
        self.keep, send = grad
        self.streams = streams
        self.got = swap(send, "scene", CORE)

    def near(self, *earlier):
        keep = tie(self.keep, *earlier)
        shape = (2, 2) + keep.shape[1:]
        total = keep.reshape(shape).astype(F32) + self.got.reshape(shape).astype(F32)
        count = 4 // len(self.streams)
        self.sums, self.moved = [], []
        for i, order in enumerate(self.streams):
            part = total[:, :, i * count : (i + 1) * count]
            if order == "xy":
                near, far, bit = part[:, 0], part[:, 1], XBIT
            else:
                near, far, bit = part[0], part[1], YBIT
            self.sums.append(near)
            self.moved.append(swap(far.astype(BF16), "scene", bit))
        return self.moved[0]

    def cross(self, *earlier):
        for i, order in enumerate(self.streams):
            near = self.sums[i] + tie(self.moved[i], *earlier).astype(F32)
            self.sums[i] = near[0]
            self.moved[i] = swap(near[1].astype(BF16), "scene", YBIT if order == "xy" else XBIT)
        return self.moved[0]

    def rows(self, *earlier):
        mine = [
            (near + tie(moved, *earlier).astype(F32)).astype(BF16)
            for near, moved in zip(self.sums, self.moved)
        ]
        self.sums = share_rows(mine[0] if len(mine) == 1 else jnp.concatenate(mine, axis=0))
        return mine[0]

    def get(self, *earlier):
        return jnp.sum(tie(self.sums, *earlier).astype(F32), axis=0)


def weight_step(grad, factor, moment, master, average):
    clipped = grad * factor
    moment_new = MOMENTUM * moment + clipped
    weight_new = master - STEP_RATE * (clipped + MOMENTUM * moment_new)
    return moment_new, weight_new, AVERAGE_DECAY * average + (1.0 - AVERAGE_DECAY) * weight_new


def to_items(x):
    scenes, rows = lax.axis_size("scene"), lax.axis_size("rows")
    z = lax.axis_index("rows")
    pairs = [[], []]
    for s in range(scenes):
        for b in range(rows):
            for turn in range(2):
                m = (b % 2) ^ turn
                to = ((s // 2) * 2 + b // 2) * rows + 2 * m + s % 2
                pairs[turn].append((s * rows + b, to))
    even = z % 2 == 0
    first = lax.ppermute(jnp.where(even, x[0], x[1]), ("scene", "rows"), pairs[0])
    second = lax.ppermute(jnp.where(even, x[1], x[0]), ("scene", "rows"), pairs[1])
    early = z // 2 == 0
    return jnp.stack([jnp.where(early, first, second), jnp.where(early, second, first)])


def body(patches, scene_length, target_views, gauss_index, raster_weight, target_color, *state):
    masters, moments, averages = state[:7], state[7:14], state[14:]
    vectors = masters[6]
    scene, row = lax.axis_index("scene"), lax.axis_index("rows")
    side = scene % 2
    item_m, item_s = row // 2, (scene // 2) * 2 + row % 2
    block_rows = patches.shape[2]
    tokens = 2 * block_rows
    length = scene_length[item_m, item_s]
    views = target_views[item_m, item_s].reshape(1)
    lens = jnp.stack([length - side * tokens, length - (1 - side) * tokens])
    pixel_count = jnp.sum(target_views).astype(F32) * (
        raster_weight.shape[-1] * lax.axis_size("rows")
    )
    natural = jnp.arange(BLOCKS, dtype=jnp.int32)
    plain = jnp.concatenate([natural, natural, natural[:4]])
    placed = lax.axis_size("scene") == BLOCKS and lax.axis_size("rows") == 4
    if placed:
        apart = jnp.bitwise_xor(natural, scene.astype(jnp.int32))
        at = jnp.bitwise_xor(jnp.asarray(PLACES), scene.astype(jnp.int32))
        spots = jnp.bitwise_and(apart, 1) * 4 + lax.shift_right_logical(apart, 1)
        perm = jnp.concatenate([at, spots, natural[:4]])
    else:
        perm = plain

    gains = [vectors[None, i * D : (i + 1) * D] for i in range(9)]
    bias_up = vectors[None, 9 * D : 9 * D + FF]
    bias_gauss = vectors[9 * D + FF :]

    low = [w.astype(BF16) for w in masters[:6]]
    low[5] = low[5].T
    x_in = patches[:, 0]
    drawn = jnp.concatenate(
        [gauss_index[:, 0].astype(F32), raster_weight[:, 0], target_color[:, 0]], axis=1
    )
    drawn = jnp.transpose(drawn, (0, 2, 1, 3))
    if placed:
        side_w = Gather(jnp.concatenate([low[0], low[5]], axis=0), "yx")
        first_w = Gather(low[1], "xy")
        second_w = Gather(jnp.concatenate([low[3], low[2]], axis=1), "yx")
        side_w.rows()
        x = to_items(x_in)
        first_w.rows(side_w.own)
        own = side_w.near()
        one = side_w.cross(own, x)
        own = first_w.near(one)
        second_w.rows(own)
        w_third = gather_whole(tie(low[4], own))
        half = side_w.core(own)
        w_side = side_w.get()
        one = first_w.cross(half)
        x = tie(x, one)
    else:
        w_side = gather_plain([low[0], low[5]], True)
        w_first = gather_plain([low[1]], False)
        w_second = gather_plain([low[3], low[2]], False)
        w_third = gather_plain([low[4]], False)
    if not placed:
        x = to_items(x_in)
    x = x.reshape(tokens, -1)
    h0, a1 = embed(perm, x, w_side, gains[6], gains[0], gains[3])
    if placed:
        own = second_w.near(a1)
        first_w.core(own)
        w_first = first_w.get()
    p = joint(perm, a1, w_first)
    kv = swap(p[:, D:], "scene", 1)
    if placed:
        second_w.cross(p)
        drawn = tie(drawn, second_w.one)
    mixed, logs = attend(perm, lens, p, kv)
    if placed:
        second_w.core(mixed)
        w_second = second_w.get()
    rd = to_items(drawn)
    h1, a2 = project(perm, mixed, w_second, 4, h0, gains[7], gains[1], gains[4])
    u, act = up_project(plain, a2, w_second, bias_up)
    h2, a3 = project(perm, act, w_third, 0, h1, gains[8], gains[2], gains[5])
    zt = gauss(perm, a3, w_side, bias_gauss)
    rd = tie(rd, zt)

    edge = swap(jnp.where(side == 0, zt[:, tokens - HT :], zt[:, :HT]), "scene", 1)
    before = jnp.where(side == 0, 0.0, edge)
    after = jnp.where(side == 0, edge, 0.0)
    zx = jnp.concatenate([before, after, jnp.zeros((POUT, 128 - 2 * HT), F32)], axis=1)
    dzt, dzx, loss = render(views, (1.0 / pixel_count).reshape(1), zt, zx, rd)
    back = swap(jnp.where(side == 0, dzx[:, HT : 2 * HT], dzx[:, :HT]), "scene", 1)
    dzt = jnp.concatenate(
        [
            dzt[:, :HT] + jnp.where(side == 0, 0.0, back),
            dzt[:, HT : tokens - HT],
            dzt[:, tokens - HT :] + jnp.where(side == 0, back, 0.0),
        ],
        axis=1,
    )
    d_bias_gauss = jnp.sum(dzt, axis=1)
    dz = dzt.astype(BF16)

    streams = ("xy", "yx")
    dw_gauss = side_grad(perm, dz, a3, placed)
    if placed:
        r_gauss = scatter_whole(dw_gauss)
        dz = tie(dz, dw_gauss[0])
    dh2, dh2_low, sums3 = norm_back(perm, dz, w_side, True, h2, gains[2], None, False)
    dw_down = weight_grad(plain, act, dh2_low, placed)
    d_low = dh2_low
    if placed:
        r_down = scatter_whole(dw_down)
        d_low = tie(dh2_low, dw_down[0])
    du, d_bias_up = down_back(plain, d_low, w_third, u)
    dw_up = weight_grad(perm, a2, du)
    if placed:
        su = Scatter(dw_up, streams)
        du = tie(du, dw_up[0])
    dh1, dh1_low, sums2 = norm_back(perm, du, w_second, False, h1, gains[1], dh2, False)
    d_low = dh1_low
    if placed:
        su.near(dh1_low)
        d_low = tie(dh1_low, su.sums[0])
    dw_out = weight_grad(perm, mixed, d_low)
    if placed:
        so = Scatter(dw_out, ("xy",))
        d_low = tie(dh1_low, dw_out[0])
    do = out_back(perm, d_low, w_second)
    dq, own, far = attend_back(perm, lens, p, kv, do, logs)
    got = swap(far, "scene", 1)
    if placed:
        su.cross(dq)
        so.near(su.sums[0])
        got = tie(got, so.sums[0])
    dkv = (own + got.astype(F32)).astype(BF16)
    dp = jnp.concatenate([dq, dkv[0], dkv[1]], axis=1)
    dw_joint = weight_grad(perm, a1, dp)
    dp_last = dp
    if placed:
        sj = Scatter(dw_joint, streams)
        dp_last = tie(dp, dw_joint[0])
    dh0_low, sums1 = norm_back(perm, dp_last, w_first, False, h0, gains[0], dh1, True)
    d_low = dh0_low
    if placed:
        sj.near(dh0_low)
        d_low = tie(dh0_low, sj.sums[0])
    dw_patch = side_grad(perm, x.T, d_low)
    if placed:
        sp = Scatter(dw_patch, ("yx",))
        so.cross(dw_patch[0], r_gauss)
        moved = su.rows(so.sums[0])
        sp.near(moved)
        sj.cross(sp.sums[0], r_down)
        moved = so.rows(sj.sums[0])
        sp.cross(moved)
        moved = sj.rows(sp.sums[0])
        sp.rows(moved)
        reduced = [t.get() for t in (sp, sj, so, su)] + [r_down, r_gauss]
    else:
        grads = [dw_patch, dw_joint, dw_out, dw_up, dw_down, dw_gauss]
        reduced = [scatter_plain(g, i in (0, 5)) for i, g in enumerate(grads)]
    reduced[5] = reduced[5].T
    vector_part = jnp.concatenate(
        [sums1[0], sums2[0], sums3[0], sums1[1], sums2[1], sums3[1], sums1[2], sums2[2], sums3[2]]
        + [d_bias_up[0], d_bias_gauss, loss[0]]
    )
    squares = sum(jnp.sum(item * item) for item in reduced)
    totals = total_sum(jnp.concatenate([vector_part, jnp.broadcast_to(squares, (128,))]).reshape(-1, 128))
    totals = totals.reshape(-1)
    vec = vectors.shape[0]
    vector_grad, loss_sum, square_sum = totals[:vec], totals[vec], totals[vec + 128]
    grad_norm = jnp.sqrt(square_sum + jnp.sum(vector_grad * vector_grad))
    factor = jnp.minimum(1.0, CLIP_NORM / (grad_norm + 1e-06))
    next_moments, next_weights, next_averages = ([], [], [])
    for grad, moment, master, average in zip(reduced + [vector_grad], moments, masters, averages):
        moment, weight, mean = weight_step(grad, factor, moment, master, average)
        next_moments.append(moment)
        next_weights.append(weight)
        next_averages.append(mean)
    return (loss_sum, pixel_count, grad_norm, *next_moments, *next_weights, *next_averages)


def solution(mesh):
    item = P(None, "scene", None, None, "rows")
    weight_specs = (P("rows", "scene"),) + (P("scene", "rows"),) * 5 + (P(),)
    in_specs = (P(None, "scene", "rows", None), P(), P(), item, item, item) + 3 * weight_specs
    out_specs = (P(), P(), P()) + 3 * weight_specs
    return jax.shard_map(body, mesh=mesh, in_specs=in_specs, out_specs=out_specs, check_vma=False)
```

```python
import functools

import jax
import jax.numpy as jnp
import numpy as np
from jax import lax
from jax.experimental import pallas as pl
from jax.experimental.pallas import tpu as pltpu
from jax.sharding import PartitionSpec as P

D = 1024
HEADS = 16
HD = 64
FF = 4096
POUT = 768
HT = 16
GV = 12
NG = POUT // GV

EPSILON = 1e-05
CLIP_NORM = 0.002
STEP_RATE = 1250.0
MOMENTUM = 0.9
AVERAGE_DECAY = 0.9

F32 = jnp.float32
BF16 = jnp.bfloat16
HIGHEST = lax.Precision.HIGHEST
BLOCKS = 8
WIDE = D // BLOCKS
VMEM_MB = 1024 * 1024
VMEM = 28
WIDE_VMEM = 56
TABLE = NG + 8


def nn(a, b):
    return lax.dot_general(a, b, (((1,), (0,)), ((), ())), preferred_element_type=F32)


def nt(a, b):
    return lax.dot_general(a, b, (((1,), (1,)), ((), ())), preferred_element_type=F32)


def tn(a, b):
    return lax.dot_general(a, b, (((0,), (0,)), ((), ())), preferred_element_type=F32)


def params(mb, n=1):
    return pltpu.CompilerParams(
        vmem_limit_bytes=mb * VMEM_MB, dimension_semantics=("arbitrary",) * n
    )


def lane_block(index, width):
    return pl.ds(pl.multiple_of(index * width, width), width)


PATCH = 144
GAUSS = POUT // 4


def side_rows(w_ref, place, first, count):
    return jnp.concatenate(
        [w_ref[j, place, first : first + count, :] for j in range(4)], axis=1
    )


def norm_store(perm, h_ref, g_ref, s_ref, a_ref, chunk):
    def step(i, carry):
        rows = pl.ds(pl.multiple_of(i * chunk, chunk), chunk)
        h = h_ref[rows, :]
        c = h - jnp.mean(h, axis=1, keepdims=True)
        var = jnp.mean(c * c, axis=1, keepdims=True)
        a = (c * lax.rsqrt(var + EPSILON) * g_ref[...] + s_ref[...]).astype(BF16)
        for b in range(BLOCKS):
            a_ref[rows, lane_block(perm[8 + b], WIDE)] = a[:, b * WIDE : (b + 1) * WIDE]
        return carry

    lax.fori_loop(0, h_ref.shape[0] // chunk, step, 0)


def rows_of(w_ref, z, width):
    block = w_ref[:, z]
    if block.shape[-1] != width:
        block = block[:, :, :width]
    return block.reshape(block.shape[0] * block.shape[1], width)


def embed_kernel(perm, x_ref, w0_ref, w1_ref, b_ref, g_ref, s_ref, h_ref, a_ref):
    x = x_ref[...]
    for i, w_ref in enumerate((w0_ref, w1_ref)):
        weight = jnp.concatenate(
            [side_rows(w_ref, perm[16 + z], 0, PATCH) for z in range(4)], axis=0
        )
        hr = nn(x, weight)
        for j in range(BLOCKS // 2):
            cols = lane_block(perm[i * BLOCKS // 2 + j], WIDE)
            h_ref[:, cols] = hr[:, j * WIDE : (j + 1) * WIDE] + b_ref[:, cols]
    norm_store(perm, h_ref, g_ref, s_ref, a_ref, 32)


def embed(perm, x, chunk, b, g, s):
    rows = x.shape[0]
    part = 256
    full = lambda shape: pl.BlockSpec(shape, lambda i, p: (0, 0))
    tile = lambda n: pl.BlockSpec((part, n), lambda i, p: (i, 0))
    weight = pl.BlockSpec((4, 4, PATCH + GAUSS, WIDE), lambda i, p: (0, 0, 0, 0))
    return pl.pallas_call(
        embed_kernel,
        grid_spec=pltpu.PrefetchScalarGridSpec(
            num_scalar_prefetch=1,
            grid=(rows // part,),
            in_specs=[tile(x.shape[1]), weight, weight]
            + [full((1, D))] * 3,
            out_specs=[tile(D), tile(D)],
        ),
        out_shape=[jax.ShapeDtypeStruct((rows, D), F32), jax.ShapeDtypeStruct((rows, D), BF16)],
        compiler_params=params(VMEM),
        cost_estimate=pl.CostEstimate(
            flops=2 * rows * D * 576, bytes_accessed=rows * D * 6 + 4 * D * 576, transcendentals=0
        ),
        name="embed_norm",
    )(perm, x, *chunk, b, g, s)


def first_of(chunk):
    return (0, 0) if chunk[0].shape[0] == 4 else (0, 1)


def project_kernel(perm, a_ref, w0_ref, w1_ref, r_ref, b_ref, g_ref, s_ref, h_ref, n_ref):
    z = pl.program_id(0)
    middle = a_ref.shape[1] // 2
    width = D // 4
    cols = lane_block(z, width)
    h_ref[:, cols] = (
        r_ref[...]
        + b_ref[...]
        + nn(a_ref[:, :middle], rows_of(w0_ref, 0, width))
        + nn(a_ref[:, middle:], rows_of(w1_ref, 0, width))
    )

    @pl.when(z == pl.num_programs(0) - 1)
    def _():
        norm_store(perm, h_ref, g_ref, s_ref, n_ref, 32)


def project(perm, a, chunk, at, res, b, g, s, grant=VMEM):
    rows, depth = a.shape
    width = D // 4
    full = lambda shape: pl.BlockSpec(shape, lambda z, p: (0, 0))
    weights = [
        pl.BlockSpec((4, 1, depth // 8, width), lambda z, p, i=i: (i, p[16 + z], 0, at))
        for i in first_of(chunk)
    ]
    return pl.pallas_call(
        project_kernel,
        grid_spec=pltpu.PrefetchScalarGridSpec(
            num_scalar_prefetch=1,
            grid=(4,),
            in_specs=[
                full((rows, depth)),
                *weights,
                pl.BlockSpec((rows, width), lambda z, p: (0, z)),
                pl.BlockSpec((1, width), lambda z, p: (0, z)),
                full((1, D)),
                full((1, D)),
            ],
            out_specs=[full((rows, D)), full((rows, D))],
        ),
        out_shape=[jax.ShapeDtypeStruct((rows, D), F32), jax.ShapeDtypeStruct((rows, D), BF16)],
        compiler_params=params(grant),
        cost_estimate=pl.CostEstimate(
            flops=2 * rows * D * depth,
            bytes_accessed=rows * D * 10 + 2 * D * depth + 2 * rows * depth,
            transcendentals=0,
        ),
        name="project_norm",
    )(perm, a, *chunk, res, b, g, s)


def halves(a_ref, w0_ref, w1_ref, width):
    middle = a_ref.shape[1] // 2
    return nn(a_ref[:, :middle], rows_of(w0_ref, 0, width)) + nn(
        a_ref[:, middle:], rows_of(w1_ref, 0, width)
    )


def joint_kernel(perm, a_ref, w0_ref, w1_ref, p_ref):
    p_ref[...] = halves(a_ref, w0_ref, w1_ref, p_ref.shape[1]).astype(BF16)


def joint(perm, a, chunk):
    rows = a.shape[0]
    part = 3 * D // 4
    weight = pl.BlockSpec((4, 1, WIDE, part), lambda z, p: (0, p[16 + z], 0, 0))
    return pl.pallas_call(
        joint_kernel,
        grid_spec=pltpu.PrefetchScalarGridSpec(
            num_scalar_prefetch=1,
            grid=(4,),
            in_specs=[pl.BlockSpec((rows, D), lambda z, p: (0, 0)), weight, weight],
            out_specs=pl.BlockSpec((rows, part), lambda z, p: (0, z)),
        ),
        out_shape=jax.ShapeDtypeStruct((rows, 3 * D), BF16),
        compiler_params=params(VMEM),
        cost_estimate=pl.CostEstimate(
            flops=6 * rows * D * D, bytes_accessed=rows * D * 8 + 6 * D * D, transcendentals=0
        ),
        name="joint",
    )(perm, a, *chunk)


def gauss_kernel(perm, a_ref, w0_ref, w1_ref, b_ref, z_ref):
    half = D // 2
    z_ref[...] = (
        nt(side_rows(w0_ref, 0, PATCH, GAUSS), a_ref[:, :half])
        + nt(side_rows(w1_ref, 0, PATCH, GAUSS), a_ref[:, half:])
        + b_ref[...]
    )


def gauss(perm, a, chunk, b):
    rows = a.shape[0]
    weight = pl.BlockSpec((4, 1, PATCH + GAUSS, WIDE), lambda z, p: (0, p[16 + z], 0, 0))
    return pl.pallas_call(
        gauss_kernel,
        grid_spec=pltpu.PrefetchScalarGridSpec(
            num_scalar_prefetch=1,
            grid=(4,),
            in_specs=[
                pl.BlockSpec((rows, D), lambda z, p: (0, 0)),
                weight,
                weight,
                pl.BlockSpec((GAUSS, 1), lambda z, p: (z, 0)),
            ],
            out_specs=pl.BlockSpec((GAUSS, rows), lambda z, p: (z, 0)),
        ),
        out_shape=jax.ShapeDtypeStruct((POUT, rows), F32),
        compiler_params=params(VMEM),
        cost_estimate=pl.CostEstimate(
            flops=2 * rows * D * POUT, bytes_accessed=rows * D * 5 + 2 * D * POUT, transcendentals=0
        ),
        name="gauss",
    )(perm, a, *chunk, b[:, None])


def out_back_kernel(perm, d_ref, w0_ref, w1_ref, o_ref):
    width = D // 4
    for i, w_ref in enumerate((w0_ref, w1_ref)):
        total = sum(
            nt(d_ref[:, z * width : (z + 1) * width], rows_of(w_ref, perm[16 + z], width))
            for z in range(4)
        )
        o_ref[:, i * D // 2 : (i + 1) * D // 2] = total.astype(BF16)


def out_back(perm, d, chunk):
    rows = d.shape[0]
    part = 256
    weight = pl.BlockSpec((4, 4, WIDE, D // 4), lambda i, p: (0, 0, 0, 4))
    tile = pl.BlockSpec((part, D), lambda i, p: (i, 0))
    return pl.pallas_call(
        out_back_kernel,
        grid_spec=pltpu.PrefetchScalarGridSpec(
            num_scalar_prefetch=1,
            grid=(rows // part,),
            in_specs=[tile, weight, weight],
            out_specs=tile,
        ),
        out_shape=jax.ShapeDtypeStruct((rows, D), BF16),
        compiler_params=params(VMEM),
        cost_estimate=pl.CostEstimate(
            flops=2 * rows * D * D, bytes_accessed=rows * D * 4 + 2 * D * D, transcendentals=0
        ),
        name="out_back",
    )(perm, d, *chunk)


def grad_kernel(perm, a_ref, d_ref, *refs):
    *outs, turned_ref = refs
    middle = a_ref.shape[1] // 2

    @pl.when(pl.program_id(0) == 0)
    def _():
        turned_ref[...] = a_ref[...].T

    for i in (1, 0):
        g = nn(turned_ref[i * middle : (i + 1) * middle, :], d_ref[...]).astype(BF16)
        g = g.reshape(4, 1, middle // 4, g.shape[1])
        if len(outs) == 2:
            outs[i][...] = g
        else:
            for j in range(4):
                outs[0][perm[4 * i + j]] = g[j]


def weight_grad(perm, a, d, whole=False):
    tokens, depth = a.shape
    n = d.shape[1] // 4
    right = pl.BlockSpec((tokens, n), lambda z, p: (0, z))
    count = 8 if whole else 4
    out = pl.BlockSpec((count, 1, depth // 8, n), lambda z, p: (0, p[16 + z], 0, 0))
    shape = jax.ShapeDtypeStruct((count, 4, depth // 8, n), BF16)
    return pl.pallas_call(
        grad_kernel,
        grid_spec=pltpu.PrefetchScalarGridSpec(
            num_scalar_prefetch=1,
            grid=(4,),
            in_specs=[pl.BlockSpec((tokens, depth), lambda z, p: (0, 0)), right],
            out_specs=[out] * (8 // count),
            scratch_shapes=[pltpu.VMEM((depth, tokens), BF16)],
        ),
        out_shape=[shape] * (8 // count),
        compiler_params=params(VMEM),
        cost_estimate=pl.CostEstimate(
            flops=8 * tokens * depth * n,
            bytes_accessed=2 * tokens * (depth + 4 * n) + 8 * depth * n,
            transcendentals=0,
        ),
        name="weight_grad",
    )(perm, a, d)


def side_grad_kernel(perm, d_ref, a_ref, *outs):
    g = nn(d_ref[...], a_ref[...]).astype(BF16)
    for j in range(BLOCKS):
        block = g[:, j * WIDE : (j + 1) * WIDE]
        if len(outs) == 2:
            outs[j // 4][j % 4, 0] = block
        else:
            outs[0][perm[j], 0] = block


def side_grad(perm, d, a, whole=False):
    tokens = a.shape[0]
    n = d.shape[0] // 4
    count = 8 if whole else 4
    out = pl.BlockSpec((count, 1, n, WIDE), lambda z, p: (0, p[16 + z], 0, 0))
    shape = jax.ShapeDtypeStruct((count, 4, n, WIDE), BF16)
    return pl.pallas_call(
        side_grad_kernel,
        grid_spec=pltpu.PrefetchScalarGridSpec(
            num_scalar_prefetch=1,
            grid=(4,),
            in_specs=[
                pl.BlockSpec((n, tokens), lambda z, p: (z, 0)),
                pl.BlockSpec((tokens, D), lambda z, p: (0, 0)),
            ],
            out_specs=[out] * (8 // count),
        ),
        out_shape=[shape] * (8 // count),
        compiler_params=params(VMEM),
        cost_estimate=pl.CostEstimate(
            flops=8 * tokens * D * n, bytes_accessed=2 * tokens * D + 16 * D * n, transcendentals=0
        ),
        name="side_grad",
    )(perm, d, a)


GELU_C = float(np.sqrt(2.0 / np.pi))


def up_kernel(perm, a_ref, w0_ref, w1_ref, b_ref, u_ref, g_ref):
    u = halves(a_ref, w0_ref, w1_ref, u_ref.shape[1]) + b_ref[...]
    u_ref[...] = u
    t = jnp.tanh(GELU_C * (u + 0.044715 * (u * u * u)))
    g_ref[...] = (u * (0.5 * (1.0 + t))).astype(BF16)


def up_project(perm, a, chunk, b):
    rows = a.shape[0]
    part = FF // BLOCKS
    weight = pl.BlockSpec((4, 1, WIDE, part), lambda n, p: (0, p[16 + n // 2], 0, n % 2))
    return pl.pallas_call(
        up_kernel,
        grid_spec=pltpu.PrefetchScalarGridSpec(
            num_scalar_prefetch=1,
            grid=(BLOCKS,),
            in_specs=[
                pl.BlockSpec((rows, D), lambda n, p: (0, 0)),
                weight,
                weight,
                pl.BlockSpec((1, part), lambda n, p: (0, n)),
            ],
            out_specs=[
                pl.BlockSpec((rows, part), lambda n, p: (0, n)),
                pl.BlockSpec((rows, part), lambda n, p: (0, p[8 + n])),
            ],
        ),
        out_shape=[jax.ShapeDtypeStruct((rows, FF), F32), jax.ShapeDtypeStruct((rows, FF), BF16)],
        compiler_params=params(VMEM),
        cost_estimate=pl.CostEstimate(
            flops=2 * rows * D * FF, bytes_accessed=rows * FF * 6 + 2 * D * FF, transcendentals=rows * FF
        ),
        name="up_gelu",
    )(perm, a, *chunk, b)


def down_back_kernel(perm, d_ref, w0_ref, w1_ref, u_ref, du_ref, sum_ref, dg_ref):
    width = D // 4

    def product(w_ref):
        dg_ref[...] = sum(
            nt(d_ref[:, z * width : (z + 1) * width], rows_of(w_ref, perm[16 + z], width))
            for z in range(4)
        )

    first = pl.program_id(0) < pl.num_programs(0) // 2
    pl.when(first)(lambda: product(w0_ref))
    pl.when(jnp.logical_not(first))(lambda: product(w1_ref))
    dg = dg_ref[...]
    u = u_ref[...]
    u2 = u * u
    t = jnp.tanh(GELU_C * (u + 0.044715 * (u2 * u)))
    slope = 0.5 * (1.0 + t) + (0.5 * GELU_C) * u * (1.0 - t * t) * (1.0 + (3 * 0.044715) * u2)
    du = slope * dg
    du_ref[...] = du.astype(BF16)
    sum_ref[...] = jnp.sum(du, axis=0, keepdims=True)


def down_back(perm, d, chunk, u):
    rows = d.shape[0]
    second = 4 * first_of(chunk)[1]
    part = FF // BLOCKS
    return pl.pallas_call(
        down_back_kernel,
        grid_spec=pltpu.PrefetchScalarGridSpec(
            num_scalar_prefetch=1,
            grid=(BLOCKS,),
            in_specs=[
                pl.BlockSpec((rows, D), lambda j, p: (0, 0)),
                pl.BlockSpec((1, 4, part, D // 4), lambda j, p: (jnp.minimum(j, 3), 0, 0, 0)),
                pl.BlockSpec(
                    (1, 4, part, D // 4), lambda j, p: (jnp.maximum(j - 4, 0) + second, 0, 0, 0)
                ),
                pl.BlockSpec((rows, part), lambda j, p: (0, p[j])),
            ],
            out_specs=[
                pl.BlockSpec((rows, part), lambda j, p: (0, p[j])),
                pl.BlockSpec((1, part), lambda j, p: (0, p[j])),
            ],
            scratch_shapes=[pltpu.VMEM((rows, part), F32)],
        ),
        out_shape=[jax.ShapeDtypeStruct((rows, FF), BF16), jax.ShapeDtypeStruct((1, FF), F32)],
        compiler_params=params(WIDE_VMEM),
        cost_estimate=pl.CostEstimate(
            flops=2 * rows * D * FF, bytes_accessed=rows * FF * 6 + 2 * D * FF, transcendentals=rows * FF
        ),
        name="down_back_gelu",
    )(perm, d, *chunk, u)


def back_kernel(has_res, placed, turned, perm, *refs):
    if has_res:
        d_ref, w0_ref, w1_ref, h_ref, g_ref, r_ref, *outs = refs
    else:
        d_ref, w0_ref, w1_ref, h_ref, g_ref, *outs = refs
        r_ref = None
    if placed:
        low_ref, sums_ref, acc_ref, part_ref = outs
        dh_ref = None
    else:
        dh_ref, low_ref, sums_ref, acc_ref, part_ref = outs
    n = pl.program_id(0)

    if turned:
        d = d_ref[...].T
        for i, w_ref in enumerate((w0_ref, w1_ref)):
            weight = jnp.concatenate(
                [side_rows(w_ref, perm[16 + z], PATCH, GAUSS) for z in range(4)], axis=0
            )
            acc_ref[:, i * D // 2 : (i + 1) * D // 2] = nn(d, weight)
    else:
        d = d_ref[...]
        width = d.shape[1]

        @pl.when(n == 0)
        def _():
            acc_ref[:, : D // 2] = nt(d, rows_of(w0_ref, 0, width))
            acc_ref[:, D // 2 :] = nt(d, rows_of(w1_ref, 0, width))

        @pl.when(n > 0)
        def _():
            acc_ref[:, : D // 2] += nt(d, rows_of(w0_ref, 0, width))
            acc_ref[:, D // 2 :] += nt(d, rows_of(w1_ref, 0, width))

    @pl.when(n == pl.num_programs(0) - 1)
    def _():
        chunk = 32
        part_ref[...] = jnp.zeros_like(part_ref)

        def fold(x):
            return jnp.sum(x.reshape(chunk // 8, 8, D), axis=0)

        def step(i, carry):
            rows = pl.ds(pl.multiple_of(i * chunk, chunk), chunk)
            h = h_ref[rows, :]
            c = h - jnp.mean(h, axis=1, keepdims=True)
            var = jnp.mean(c * c, axis=1, keepdims=True)
            rstd = lax.rsqrt(var + EPSILON)
            xh = c * rstd
            da = jnp.concatenate(
                [acc_ref[rows, lane_block(perm[8 + b], WIDE)] for b in range(BLOCKS)], axis=1
            )
            dxh = da * xh
            part_ref[0] += fold(dxh)
            part_ref[1] += fold(da)
            dy = da * g_ref[...]
            first = jnp.mean(dy, axis=1, keepdims=True)
            second = jnp.mean(dy * xh, axis=1, keepdims=True)
            dh = rstd * (dy - first - xh * second)
            if has_res:
                dh = dh + r_ref[rows, :]
            part_ref[2] += fold(dh)
            low = dh.astype(BF16)
            if placed:
                for b in range(BLOCKS):
                    low_ref[rows, lane_block(perm[8 + b], WIDE)] = low[:, b * WIDE : (b + 1) * WIDE]
            else:
                dh_ref[rows, :] = dh
                low_ref[rows, :] = low
            return carry

        lax.fori_loop(0, h_ref.shape[0] // chunk, step, 0)
        sums_ref[...] = jnp.concatenate(
            [jnp.sum(part_ref[i], axis=0, keepdims=True) for i in range(3)]
            + [jnp.zeros((5, D), F32)],
            axis=0,
        )


def norm_back(perm, d, chunk, turned, h, g, res, placed):
    full = lambda shape: pl.BlockSpec(shape, lambda n, p: (0, 0))
    rows = h.shape[0]
    wide = d.size // rows
    if turned:
        left = full(d.shape)
        weight = pl.BlockSpec((4, 4, PATCH + GAUSS, WIDE), lambda n, p: (0, 0, 0, 0))
    else:
        part = wide // 4
        left = pl.BlockSpec((rows, part), lambda n, p: (0, n))
        weight = pl.BlockSpec((4, 1, WIDE, part), lambda n, p: (0, p[16 + n], 0, 0))
    args = [d, *chunk, h, g]
    specs = [left, weight, weight, full((rows, D)), full((1, D))]
    if res is not None:
        args.append(res)
        specs.append(full((rows, D)))
    out_specs = [full((rows, D)), full((8, D))]
    out_shape = [jax.ShapeDtypeStruct((rows, D), BF16), jax.ShapeDtypeStruct((8, D), F32)]
    if not placed:
        out_specs = [full((rows, D))] + out_specs
        out_shape = [jax.ShapeDtypeStruct((rows, D), F32)] + out_shape
    return pl.pallas_call(
        functools.partial(back_kernel, res is not None, placed, turned),
        grid_spec=pltpu.PrefetchScalarGridSpec(
            num_scalar_prefetch=1,
            grid=(1 if turned else 4,),
            in_specs=specs,
            out_specs=out_specs,
            scratch_shapes=[pltpu.VMEM((rows, D), F32), pltpu.VMEM((3, 8, D), F32)],
        ),
        out_shape=out_shape,
        compiler_params=params(VMEM),
        cost_estimate=pl.CostEstimate(
            flops=2 * rows * D * wide,
            bytes_accessed=rows * D * 14 + 2 * D * wide + 2 * rows * wide,
            transcendentals=0,
        ),
        name="norm_back",
    )(perm, *args)


SCALE = HD ** (-0.5)
PAIR = 2 * HD
PAIRS = HEADS // 2


def lanes_of(side):
    lane = lax.broadcasted_iota(jnp.int32, (1, PAIR), 1)
    mine = (lane < HD) == (side == 0)
    return lane, mine, HD * (1 - side)


def masked_keys(keys, first, length, extra):
    lane, mine, free = first
    spot = lax.broadcasted_iota(jnp.int32, (keys.shape[0], 1), 0)
    hidden = jnp.where(spot < length, 0.0, -1e30).astype(BF16)
    rest = jnp.where(lane == free, hidden, 0.0).astype(BF16)
    if extra:
        ones = jnp.logical_and(lane > free, lane <= free + extra)
        rest = jnp.where(ones, 1.0, rest).astype(BF16)
    return jnp.where(mine, keys, rest)


def attend_kernel(perm, lens, q_ref, k0_ref, k1_ref, v0_ref, v1_ref, o_ref, l_ref, f_ref):
    v0, v1 = v0_ref[...], v1_ref[...]
    sides = [lanes_of(side) for side in range(2)]
    keys = [
        [masked_keys(ref[...], where, lens[j], 0) for j, ref in enumerate((k0_ref, k1_ref))]
        for where in sides
    ]
    chunk = 256
    for i in range(q_ref.shape[0] // chunk):
        rows = slice(i * chunk, (i + 1) * chunk)
        q = (q_ref[rows, :] * SCALE).astype(BF16)
        outs = []
        logs = []
        for (lane, mine, free), (k0, k1) in zip(sides, keys):
            qm = jnp.where(mine, q, jnp.where(lane == free, 1.0, 0.0).astype(BF16))
            s0 = nt(qm, k0)
            s1 = nt(qm, k1)
            top = jnp.max(jnp.maximum(s0, s1), axis=1, keepdims=True)
            e0 = jnp.exp(s0 - top)
            e1 = jnp.exp(s1 - top)
            total = jnp.sum(e0 + e1, axis=1, keepdims=True)
            outs.append((nn(e0.astype(BF16), v0) + nn(e1.astype(BF16), v1)) * (1.0 / total))
            logs.append(top + jnp.log(total))
        lane = sides[0][0]
        mixed = jnp.where(lane < HD, outs[0], outs[1])
        o_ref[rows, :] = mixed.astype(BF16)
        f_ref[rows, :] = mixed
        l_ref[rows, :] = jnp.where(lane < HD, logs[1], logs[0])


def attend(perm, lens, p, kv):
    rows = p.shape[0]
    block = lambda first: pl.BlockSpec((rows, PAIR), lambda h, m, n: (0, first + h))
    return pl.pallas_call(
        attend_kernel,
        grid_spec=pltpu.PrefetchScalarGridSpec(
            num_scalar_prefetch=2,
            grid=(PAIRS,),
            in_specs=[block(0), block(PAIRS), block(0), block(2 * PAIRS), block(PAIRS)],
            out_specs=[
                pl.BlockSpec((rows, PAIR), lambda h, m, n: (0, m[8 + h])),
                block(0),
                block(0),
            ],
        ),
        out_shape=[
            jax.ShapeDtypeStruct((rows, D), BF16),
            jax.ShapeDtypeStruct((rows, D), F32),
            jax.ShapeDtypeStruct((rows, D), F32),
        ],
        compiler_params=params(VMEM),
        cost_estimate=pl.CostEstimate(
            flops=8 * rows * rows * D,
            bytes_accessed=12 * rows * D,
            transcendentals=2 * rows * rows * HEADS,
        ),
        name="attend",
    )(perm, lens, p, p, kv, p, kv)


def attend_back_kernel(
    perm, lens, q_ref, k0_ref, k1_ref, v0_ref, v1_ref, do_ref, l_ref, f_ref, dq_ref, own_ref, far_ref
):
    values = []
    for side in range(2):
        lane, mine, free = lanes_of(side)
        ones = jnp.logical_and(lane >= free, lane < free + 3)
        rest = jnp.where(ones, 1.0, 0.0).astype(BF16)
        values.append([jnp.where(mine, ref[...], rest) for ref in (v0_ref, v1_ref)])
    q_all, do_all = q_ref[...], do_ref[...]
    sides = [lanes_of(side) for side in range(2)]
    keys = [
        [masked_keys(ref[...], where, lens[j], 3) for j, ref in enumerate((k0_ref, k1_ref))]
        for where in sides
    ]
    turned = [[k.T for k in pair] for pair in keys]
    chunk = 256
    dk = [None, None]
    dv = [None, None]
    for i in range(q_ref.shape[0] // chunk):
        rows = slice(i * chunk, (i + 1) * chunk)

        def thirds(x):
            first = x.astype(BF16)
            left = x - first.astype(F32)
            second = left.astype(BF16)
            return first, second, (left - second.astype(F32)).astype(BF16)

        logs = thirds(l_ref[rows, :])
        flow = do_all[rows, :].astype(F32) * f_ref[rows, :]
        dqs = []
        for (lane, mine, free), (k0, k1), vs, across in zip(sides, keys, values, turned):
            qm = jnp.where(mine, q_all[rows, :], 0.0).astype(BF16)
            dom = jnp.where(mine, do_all[rows, :], 0.0).astype(BF16)
            rest = jnp.where(lane == free, 1.0, 0.0).astype(BF16)
            for at, part in enumerate(logs):
                rest = jnp.where(lane == free + 1 + at, -part, rest)
            qs = jnp.where(mine, (q_all[rows, :] * SCALE).astype(BF16), rest)
            probs = [jnp.exp(nt(k, qs)) for k in (k0, k1)]
            delta = jnp.sum(jnp.where(mine, flow, 0.0), axis=1, keepdims=True)
            less = dom
            for at, part in enumerate(thirds(delta)):
                less = jnp.where(lane == free + at, -part, less)
            da = [nt(v, less) for v in vs]
            dq = None
            for j in range(2):
                ds = (probs[j] * da[j]).astype(BF16)
                term = nn(across[j], ds)
                dq = term if dq is None else dq + term
                term = nn(ds, qm)
                dk[j] = term if dk[j] is None else dk[j] + term
                term = nn(probs[j].astype(BF16), dom)
                dv[j] = term if dv[j] is None else dv[j] + term
            dqs.append(dq)
        dq = jnp.concatenate([dqs[0][:HD], dqs[1][HD:]], axis=0) * SCALE
        dq_ref[rows, :] = dq.T.astype(BF16)
    own_ref[0] = dk[0] * SCALE
    own_ref[1] = dv[0]
    far_ref[0] = (dk[1] * SCALE).astype(BF16)
    far_ref[1] = dv[1].astype(BF16)


def attend_back(perm, lens, p, kv, do, logs, flat):
    rows = p.shape[0]
    block = lambda first: pl.BlockSpec((rows, PAIR), lambda h, m, n: (0, first + h))
    both = pl.BlockSpec((2, rows, PAIR), lambda h, m, n: (0, 0, h))
    return pl.pallas_call(
        attend_back_kernel,
        grid_spec=pltpu.PrefetchScalarGridSpec(
            num_scalar_prefetch=2,
            grid=(PAIRS,),
            in_specs=[
                block(0),
                block(PAIRS),
                block(0),
                block(2 * PAIRS),
                block(PAIRS),
                pl.BlockSpec((rows, PAIR), lambda h, m, n: (0, m[8 + h])),
                block(0),
                block(0),
            ],
            out_specs=[block(0), both, both],
        ),
        out_shape=[
            jax.ShapeDtypeStruct((rows, D), BF16),
            jax.ShapeDtypeStruct((2, rows, D), F32),
            jax.ShapeDtypeStruct((2, rows, D), BF16),
        ],
        compiler_params=params(VMEM),
        cost_estimate=pl.CostEstimate(
            flops=20 * rows * rows * D,
            bytes_accessed=28 * rows * D,
            transcendentals=2 * rows * rows * HEADS,
        ),
        name="attend_back",
    )(perm, lens, p, p, kv, p, kv, do, logs, flat)


def iota(shape, dim):
    return lax.broadcasted_iota(jnp.int32, shape, dim)


def render_kernel(
    views_ref, inv_ref, z_ref, zx_ref, rd_ref, mc_ref, dz_ref, dzx_ref, loss_ref,
    tf_ref, both_ref, o_ref, wm_ref, a_ref, dt_ref, tok_ref, edge_ref, zs_ref,
):
    width = 256
    pixels = rd_ref.shape[-1]
    kg = 8

    lanes = 128
    parts = z_ref.shape[1] // lanes
    for i in range(parts):
        zs_ref[i] = z_ref[:, i * lanes : (i + 1) * lanes]
    zs_ref[parts] = zx_ref[...]

    def values(i):
        return [zs_ref[i, pl.ds(v, NG, stride=GV), :] for v in range(GV)]

    def shade(z):
        colour = [jax.nn.sigmoid(z[i]) for i in range(3)]
        gate = jax.nn.sigmoid(z[3])
        square = z[4] * z[4]
        for i in range(5, GV):
            square = square + z[i] * z[i]
        opacity = gate * jnp.exp(-0.5 * (square / (GV - 4)))
        return colour, gate, opacity

    own_group = iota((NG, width), 0) % 16 == iota((NG, width), 1) // 16

    def spread(base):
        return (iota((128, width), 0) == base + iota((128, width), 1) % 16).astype(F32)

    def rim_rows(table, base):
        wide = lax.dot_general(
            table, spread(base), (((1,), (0,)), ((), ())), precision=HIGHEST,
            preferred_element_type=F32,
        )
        return jnp.sum(jnp.where(own_group, wide, 0.0).reshape(4, 16, width), axis=1)

    def rim_back(rows, base):
        wide = jnp.concatenate(
            [jnp.broadcast_to(rows[j : j + 1, :], (16, width)) for j in range(4)], axis=0
        )
        return lax.dot_general(
            jnp.where(own_group, wide, 0.0), spread(base), (((1,), (1,)), ((), ())),
            precision=HIGHEST, preferred_element_type=F32,
        )

    def place(i):
        if i == parts:
            return edge_ref, slice(0, lanes)
        return tok_ref, slice(i * lanes, (i + 1) * lanes)

    for i in range(parts + 1):
        out_ref, cols = place(i)
        colour, gate, opacity = shade(values(i))
        for ch in range(3):
            out_ref[ch * NG : (ch + 1) * NG, cols] = colour[ch] * opacity
        out_ref[3 * NG : 4 * NG, cols] = opacity

    for ch in range(4):
        rows = slice(ch * NG, (ch + 1) * NG)
        at = ch * TABLE
        tf_ref[0, at : at + NG, :] = tok_ref[rows, 0:width]
        tf_ref[1, at : at + NG, :] = tok_ref[rows, width : 2 * width]
        tf_ref[0, at + NG : at + NG + 4, :] = rim_rows(edge_ref[rows, :], 0)
        tf_ref[0, at + NG + 4 : at + NG + 8, :] = rim_rows(tok_ref[rows, width : width + 128], 0)
        tf_ref[1, at + NG : at + NG + 4, :] = rim_rows(tok_ref[rows, width - 128 : width], 112)
        tf_ref[1, at + NG + 4 : at + NG + 8, :] = rim_rows(edge_ref[rows, :], 16)
    for block in range(2):
        table = tf_ref[block]
        high = table.astype(BF16)
        both_ref[block, : 4 * TABLE] = high
        both_ref[block, 4 * TABLE :] = (table - high.astype(F32)).astype(BF16)
    dt_ref[...] = jnp.zeros_like(dt_ref)
    inverse = inv_ref[0]
    row_hi = iota((width, pixels), 0).astype(F32).astype(BF16)
    row_lo = iota((TABLE, pixels), 0)
    one_low, zero_low = jnp.ones((), BF16), jnp.zeros((), BF16)

    def features(c):
        return jnp.tanh(mc_ref[0] * c[0] + mc_ref[1] * c[1] + mc_ref[2] * c[2])

    def view(t, loss):
        for block in range(2):
            r = rd_ref[block, t, 0:kg, :].astype(jnp.int32)
            weight = rd_ref[block, t, kg : 2 * kg, :]
            token = lax.shift_right_logical(r, 6)
            g = jnp.bitwise_and(r, NG - 1)
            after = token >= HT + width
            inside = jnp.logical_and(token >= HT, jnp.logical_not(after))
            rim = jnp.where(after, token - (HT + width), token)
            high = jnp.where(inside, token - HT, jnp.bitwise_and(g, 15) * 16 + rim)
            low = jnp.where(
                inside, g, NG + lax.shift_right_logical(g, 4) + jnp.where(after, 4, 0)
            )
            sums = [jnp.zeros((8, pixels), F32) for _ in range(4)]
            high = high.astype(F32).astype(BF16)
            table = both_ref[block]
            for k in range(kg):
                cols = slice(k * pixels, (k + 1) * pixels)
                one = jnp.where(row_hi == high[k : k + 1, :], one_low, zero_low)
                o_ref[block, :, cols] = one
                wm = jnp.where(row_lo == low[k : k + 1, :], weight[k : k + 1, :], 0.0)
                wm_ref[block, :, cols] = wm
                picked = nn(table, one)
                picked = picked[: 4 * TABLE] + picked[4 * TABLE :]
                for ch in range(4):
                    part = picked[ch * TABLE : (ch + 1) * TABLE, :] * wm
                    sums[ch] = sums[ch] + jnp.sum(part.reshape(TABLE // 8, 8, pixels), axis=0)
            sums = [jnp.sum(s, axis=0, keepdims=True) for s in sums]
            scale = 1.0 / (1.0 + sums[3])
            seen = [sums[i] * scale for i in range(3)]
            goal = [rd_ref[block, t, 2 * kg + i : 2 * kg + i + 1, :] for i in range(3)]
            f_seen = features(seen)
            gap = f_seen - features(goal)
            diff = [seen[i] - goal[i] for i in range(3)]
            loss = loss + diff[0] * diff[0] + diff[1] * diff[1] + diff[2] * diff[2]
            loss = loss + 0.5 * jnp.sum(gap * gap, axis=0, keepdims=True)
            pull = gap * (1.0 - f_seen * f_seen)
            d_seen = [
                inverse * (2.0 * diff[i] + jnp.sum(pull * mc_ref[i], axis=0, keepdims=True))
                for i in range(3)
            ]
            d_sum = [d * scale for d in d_seen]
            d_sum.append(
                -(d_seen[0] * seen[0] + d_seen[1] * seen[1] + d_seen[2] * seen[2]) * scale
            )
            for k in range(kg):
                cols = slice(k * pixels, (k + 1) * pixels)
                wm = wm_ref[block, :, cols]
                full = jnp.concatenate([wm * d_sum[ch] for ch in range(4)], axis=0)
                a_ref[block, :, cols] = full.astype(BF16)
            dt_ref[block] += nt(a_ref[block], o_ref[block])
        return loss

    loss = lax.fori_loop(0, views_ref[0], view, jnp.zeros((1, pixels), F32))
    loss_ref[...] = jnp.broadcast_to(jnp.sum(loss, axis=1, keepdims=True), loss_ref.shape)

    for ch in range(4):
        rows = slice(ch * NG, (ch + 1) * NG)
        at = ch * TABLE + NG
        tok_ref[rows, 0:width] = dt_ref[0, at - NG : at, :]
        tok_ref[rows, width : 2 * width] = dt_ref[1, at - NG : at, :]
        tok_ref[rows, width : width + 128] += rim_back(dt_ref[0, at + 4 : at + 8, :], 0)
        tok_ref[rows, width - 128 : width] += rim_back(dt_ref[1, at : at + 4, :], 112)
        edge_ref[rows, :] = rim_back(dt_ref[0, at : at + 4, :], 0) + rim_back(
            dt_ref[1, at + 4 : at + 8, :], 16
        )

    for part in range(parts + 1):
        grad_ref, cols = place(part)
        z = values(part)
        colour, gate, opacity = shade(z)
        d = [grad_ref[i * NG : (i + 1) * NG, cols] for i in range(4)]
        d_opacity = d[3]
        for i in range(3):
            d_opacity = d_opacity + d[i] * colour[i]
            zs_ref[part, pl.ds(i, NG, stride=GV), :] = d[i] * opacity * colour[i] * (1.0 - colour[i])
        both = d_opacity * opacity
        zs_ref[part, pl.ds(3, NG, stride=GV), :] = both * (1.0 - gate)
        for i in range(4, GV):
            zs_ref[part, pl.ds(i, NG, stride=GV), :] = both * z[i] * (-1.0 / (GV - 4))
    for i in range(parts):
        dz_ref[:, i * lanes : (i + 1) * lanes] = zs_ref[i]
    dzx_ref[...] = zs_ref[parts]


def render(views, inverse, zt, zx, rd):
    tokens = zt.shape[1]
    pixels = rd.shape[-1]
    slots = 8 * pixels
    counter = np.arange(48, dtype=np.float32).reshape(16, 3)
    mix = (np.float32(0.8) * np.cos(np.float32(1.7) * counter + np.float32(0.3))).astype(np.float32)
    mix = jnp.broadcast_to(jnp.asarray(mix.T)[:, :, None], (3, 16, pixels))
    whole = lambda x: pl.BlockSpec(x.shape, lambda: (0,) * x.ndim)
    smem = pl.BlockSpec(memory_space=pltpu.SMEM)
    shape = jax.ShapeDtypeStruct
    return pl.pallas_call(
        render_kernel,
        in_specs=[smem, smem, whole(zt), whole(zx), whole(rd), whole(mix)],
        out_specs=[whole(zt), whole(zx), pl.BlockSpec((8, 128), lambda: (0, 0))],
        out_shape=[shape(zt.shape, F32), shape(zx.shape, F32), shape((8, 128), F32)],
        scratch_shapes=[
            pltpu.VMEM((2, 4 * TABLE, 256), F32),
            pltpu.VMEM((2, 8 * TABLE, 256), BF16),
            pltpu.VMEM((2, 256, slots), BF16),
            pltpu.VMEM((2, TABLE, slots), F32),
            pltpu.VMEM((2, 4 * TABLE, slots), BF16),
            pltpu.VMEM((2, 4 * TABLE, 256), F32),
            pltpu.VMEM((4 * NG, tokens), F32),
            pltpu.VMEM((4 * NG, 128), F32),
            pltpu.VMEM((tokens // 128 + 1, POUT, 128), F32),
        ],
        compiler_params=pltpu.CompilerParams(vmem_limit_bytes=VMEM * VMEM_MB),
        cost_estimate=pl.CostEstimate(
            flops=24 * slots * 4 * TABLE * 256 * 6, bytes_accessed=4 * 1024 * 1024, transcendentals=0
        ),
        name="render",
    )(views, inverse, zt, zx, rd, mix)


def flip_pairs(n, bit):
    return [(i, i ^ bit) for i in range(n)]


def swap(x, axis, bit):
    return lax.ppermute(x, axis, flip_pairs(lax.axis_size(axis), bit))


CORE, XBIT, YBIT = 1, 2, 4
PLACES = np.array([0, 2, 4, 6, 1, 3, 5, 7], np.int32)


def total_sum(x):
    if lax.axis_size("scene") == BLOCKS and lax.axis_size("rows") == 4:
        x = x + swap(x, "scene", CORE)
        near, far, both = (swap(x, "scene", bit) for bit in (XBIT, YBIT, XBIT | YBIT))
        x = (x + near) + (far + both)
        near, far, both = (swap(x, "rows", bit) for bit in (1, 2, 3))
        return (x + near) + (far + both)
    for axis in ("scene", "rows"):
        bit = 1
        while bit < lax.axis_size(axis):
            x = x + swap(x, axis, bit)
            bit = 2 * bit
    return x


def gather_whole(shard):
    whole = lax.all_gather(shard, ("scene", "rows"), axis=0)
    return (whole.reshape((BLOCKS, 4) + shard.shape),) * 2


def gather_plain(shards, turned):
    parts = []
    for shard in shards:
        if turned:
            wide = lax.all_gather(shard, "rows", axis=0, tiled=True)
            full = lax.all_gather(wide, "scene", axis=1, tiled=True)
            parts.append(jnp.transpose(full.reshape(4, -1, BLOCKS, WIDE), (2, 0, 1, 3)))
        else:
            wide = lax.all_gather(shard, "rows", axis=1, tiled=True)
            full = lax.all_gather(wide, "scene", axis=0, tiled=True)
            blocks = full.reshape(BLOCKS, full.shape[0] // BLOCKS, 4, -1)
            parts.append(jnp.transpose(blocks, (0, 2, 1, 3)))
    chunk = jnp.concatenate(parts, axis=2 if turned else 3)
    return chunk[:4], chunk[4:]


def scatter_plain(grad, turned):
    both = jnp.concatenate(grad, axis=0)
    if turned:
        full = jnp.transpose(both, (1, 2, 0, 3)).reshape(-1, D)
    else:
        full = jnp.transpose(both, (0, 2, 1, 3)).reshape(both.shape[0] * both.shape[2], -1)
    part = lax.psum_scatter(full, "scene", scatter_dimension=int(turned), tiled=True)
    return lax.psum_scatter(part, "rows", scatter_dimension=1 - turned, tiled=True).astype(F32)


def stack_kernel(*refs):
    own, x, y, *both, out_ref = refs
    for i, ref in enumerate((own, x, y)):
        out_ref[i] = ref[...]
    if len(both) == 1:
        out_ref[3] = both[0][...]
    else:
        early = pl.program_id(0) < 2
        for ref, now in zip(both, (early, jnp.logical_not(early))):

            @pl.when(now)
            def _(ref=ref):
                out_ref[3] = ref[...]


def stack(parts, both):
    both = both if isinstance(both, list) else [both]
    shape = parts[0].shape
    block = (1,) + shape[1:]
    places = [lambda i: (i, 0, 0)] * 4
    if len(both) == 2:
        places[3:] = [lambda i: (jnp.minimum(i, 1), 0, 0), lambda i: (jnp.maximum(i - 2, 0), 0, 0)]
    return pl.pallas_call(
        stack_kernel,
        grid=(4,),
        in_specs=[pl.BlockSpec(block, place) for place in places],
        out_specs=pl.BlockSpec((4,) + block, lambda i: (0, i, 0, 0)),
        out_shape=jax.ShapeDtypeStruct((4,) + shape, parts[0].dtype),
        compiler_params=params(VMEM),
        cost_estimate=pl.CostEstimate(
            flops=0, bytes_accessed=16 * parts[0].size, transcendentals=0
        ),
        name="stack",
    )(*parts, *both)


def together(*arrays):
    return lax.optimization_barrier(arrays)


def share_rows(x):
    return lax.all_to_all(x, "rows", 0, 0)


class Gather:
    def __init__(self, shard, order):
        self.shard = shard
        self.first, self.second = (XBIT, YBIT) if order == "xy" else (YBIT, XBIT)

    def rows(self):
        self.own = share_rows(jnp.broadcast_to(self.shard[None], (4,) + self.shard.shape))

    def near(self):
        self.one = swap(self.own, "scene", self.first)
        self.two = swap(self.own, "scene", self.second)

    def cross(self):
        self.both = swap(self.one, "scene", self.second)

    def cross_halves(self):
        self.both = [
            swap(self.one[:2], "scene", self.second),
            swap(self.two[2:], "scene", self.first),
        ]

    def get(self):
        x, y = (self.one, self.two) if self.first == XBIT else (self.two, self.one)
        half = stack([self.own, x, y], self.both)
        return half, swap(half, "scene", CORE)


class Scatter:
    def __init__(self, grad, streams):
        self.keep, send = grad
        self.streams = streams
        self.got = swap(send, "scene", CORE)

    def near(self):
        shape = (2, 2) + self.keep.shape[1:]
        keep, got = self.keep.reshape(shape), self.got.reshape(shape)
        count = 4 // len(self.streams)
        self.sums, self.away = [], []
        for i, order in enumerate(self.streams):
            zs = slice(i * count, (i + 1) * count)

            def part(place):
                pick = (slice(None), place, zs) if order == "xy" else (place, slice(None), zs)
                return keep[pick].astype(F32) + got[pick].astype(F32)

            self.sums.append(part(0))
            self.away.append(part(1).astype(BF16))

    def send(self, step):
        bits = {"xy": (XBIT, YBIT), "yx": (YBIT, XBIT)}
        self.moved = [
            swap(away, "scene", bits[order][step])
            for away, order in zip(self.away, self.streams)
        ]

    def cross(self):
        whole = [near + moved.astype(F32) for near, moved in zip(self.sums, self.moved)]
        self.sums = [part[0] for part in whole]
        self.away = [part[1].astype(BF16) for part in whole]

    def last(self):
        mine = [
            (near + moved.astype(F32)).astype(BF16) for near, moved in zip(self.sums, self.moved)
        ]
        self.away = [mine[0] if len(mine) == 1 else jnp.concatenate(mine, axis=0)]

    def rows(self):
        self.total = share_rows(self.away[0])

    def rows_apart(self):
        z = lax.axis_index("rows")
        block = lambda k: lax.dynamic_index_in_dim(self.away[0], z ^ k, 0, keepdims=False)
        self.total = jnp.stack([block(0)] + [swap(block(k), "rows", k) for k in (1, 2, 3)])

    def get(self):
        return jnp.sum(self.total.astype(F32), axis=0)


def settle(scatters, *arrays):
    flat = [a for t in scatters for a in t.away]
    out = list(together(*flat, *arrays))
    for t in scatters:
        t.away = [out.pop(0) for _ in t.away]
    return out[0] if len(out) == 1 else out


def weight_step(grad, factor, moment, master, average):
    clipped = grad * factor
    moment_new = MOMENTUM * moment + clipped
    weight_new = master - STEP_RATE * (clipped + MOMENTUM * moment_new)
    return moment_new, weight_new, AVERAGE_DECAY * average + (1.0 - AVERAGE_DECAY) * weight_new


def items_sent(x):
    scenes, rows = lax.axis_size("scene"), lax.axis_size("rows")
    z = lax.axis_index("rows")
    pairs = [[], []]
    for s in range(scenes):
        for b in range(rows):
            for turn in range(2):
                m = (b % 2) ^ turn
                to = ((s // 2) * 2 + b // 2) * rows + 2 * m + s % 2
                pairs[turn].append((s * rows + b, to))
    even = z % 2 == 0
    first = lax.ppermute(jnp.where(even, x[0], x[1]), ("scene", "rows"), pairs[0])
    second = lax.ppermute(jnp.where(even, x[1], x[0]), ("scene", "rows"), pairs[1])
    return first, second


def items_placed(parts):
    first, second = parts
    early = lax.axis_index("rows") // 2 == 0
    return jnp.stack([jnp.where(early, first, second), jnp.where(early, second, first)])


def body(patches, scene_length, target_views, gauss_index, raster_weight, target_color, *state):
    masters, moments, averages = state[:7], state[7:14], state[14:]
    vectors = masters[6]
    scene, row = lax.axis_index("scene"), lax.axis_index("rows")
    side = scene % 2
    item_m, item_s = row // 2, (scene // 2) * 2 + row % 2
    block_rows = patches.shape[2]
    tokens = 2 * block_rows
    length = scene_length[item_m, item_s]
    views = target_views[item_m, item_s].reshape(1)
    lens = jnp.stack([length - side * tokens, length - (1 - side) * tokens])
    pixel_count = jnp.sum(target_views).astype(F32) * (
        raster_weight.shape[-1] * lax.axis_size("rows")
    )
    natural = jnp.arange(BLOCKS, dtype=jnp.int32)
    plain = jnp.concatenate([natural, natural, natural[:4]])
    placed = lax.axis_size("scene") == BLOCKS and lax.axis_size("rows") == 4
    if placed:
        apart = jnp.bitwise_xor(natural, scene.astype(jnp.int32))
        at = jnp.bitwise_xor(jnp.asarray(PLACES), scene.astype(jnp.int32))
        spots = jnp.bitwise_and(apart, 1) * 4 + lax.shift_right_logical(apart, 1)
        perm = jnp.concatenate([at, spots, natural[:4]])
    else:
        perm = plain

    gains = [vectors[None, i * D : (i + 1) * D] for i in range(9)]
    bias_up = vectors[None, 9 * D : 9 * D + FF]
    bias_gauss = vectors[9 * D + FF :]

    low = [w.astype(BF16) for w in masters[:6]]
    low[5] = low[5].T
    x_in = patches[:, 0]
    drawn = jnp.concatenate(
        [gauss_index[:, 0].astype(F32), raster_weight[:, 0], target_color[:, 0]], axis=1
    )
    drawn = jnp.transpose(drawn, (0, 2, 1, 3))
    if placed:
        side_w = Gather(jnp.concatenate([low[0], low[5]], axis=0), "yx")
        first_w = Gather(low[1], "xy")
        second_w = Gather(jnp.concatenate([low[3], low[2]], axis=1), "yx")
        side_w.rows()
        side_w.own, first_w.shard = together(side_w.own, first_w.shard)
        first_w.rows()
        side_w.near()
        first_w.own, side_w.one, side_w.two, x_in = together(
            first_w.own, side_w.one, side_w.two, x_in
        )
        first_w.near()
        side_w.cross()
        x = items_sent(x_in)
        second_w.shard, *x = together(second_w.shard, *x)
        second_w.rows()
        first_w.one, first_w.two, side_w.both = together(
            first_w.one, first_w.two, side_w.both
        )
        first_w.cross()
        w_side = side_w.get()
        x = items_placed(x)
    else:
        w_side = gather_plain([low[0], low[5]], True)
        w_first = gather_plain([low[1]], False)
        w_second = gather_plain([low[3], low[2]], False)
        w_third = gather_plain([low[4]], False)
    if not placed:
        x = items_placed(items_sent(x_in))
    x = x.reshape(tokens, -1)
    h0, a1 = embed(perm, x, w_side, gains[6], gains[0], gains[3])
    if placed:
        second_w.own, a1, first_w.both, shard = together(second_w.own, a1, first_w.both, low[4])
        second_w.near()
        w_third = gather_whole(shard)
        w_first = first_w.get()
    p = joint(perm, a1, w_first)
    kv = swap(p[:, D:], "scene", 1)
    mixed, logs, flat = attend(perm, lens, p, kv)
    if placed:
        mixed, logs, second_w.one, second_w.two = together(
            mixed, logs, second_w.one, second_w.two
        )
        second_w.cross_halves()
        w_second = second_w.get()
    rd = items_sent(drawn)
    h1, a2 = project(perm, mixed, w_second, 4, h0, gains[7], gains[1], gains[4])
    u, act = up_project(plain, a2, w_second, bias_up)
    h2, a3 = project(perm, act, w_third, 0, h1, gains[8], gains[2], gains[5], WIDE_VMEM)
    zt = gauss(perm, a3, w_side, bias_gauss)
    zt, *rd = together(zt, *rd)
    rd = items_placed(rd)

    edge = swap(jnp.where(side == 0, zt[:, tokens - HT :], zt[:, :HT]), "scene", 1)
    before = jnp.where(side == 0, 0.0, edge)
    after = jnp.where(side == 0, edge, 0.0)
    zx = jnp.concatenate([before, after, jnp.zeros((POUT, 128 - 2 * HT), F32)], axis=1)
    dzt, dzx, loss = render(views, (1.0 / pixel_count).reshape(1), zt, zx, rd)
    back = swap(jnp.where(side == 0, dzx[:, HT : 2 * HT], dzx[:, :HT]), "scene", 1)
    dzt = jnp.concatenate(
        [
            dzt[:, :HT] + jnp.where(side == 0, 0.0, back),
            dzt[:, HT : tokens - HT],
            dzt[:, tokens - HT :] + jnp.where(side == 0, back, 0.0),
        ],
        axis=1,
    )
    d_bias_gauss = jnp.sum(dzt, axis=1)
    dz = dzt.astype(BF16)

    streams = ("xy", "yx")
    dw_gauss = side_grad(perm, dz, a3)
    if placed:
        sg = Scatter(dw_gauss, ("yx",))
        sg.keep, dz = together(sg.keep, dz)
    dh2, dh2_low, sums3 = norm_back(perm, dz, w_side, True, h2, gains[2], None, False)
    dw_down = weight_grad(plain, act, dh2_low, placed)
    d_low = dh2_low
    if placed:
        whole_down, d_low = together(dw_down[0], d_low)
        part_down = lax.psum_scatter(whole_down, "scene", scatter_dimension=0)
        sg.near()
        d_low = settle([sg], d_low)
        sg.send(0)
    du, d_bias_up = down_back(plain, d_low, w_third, u)
    if placed:
        du, *sg.moved = together(du, *sg.moved)
        sg.cross()
        du = settle([sg], du)
        sg.send(1)
    dw_up = weight_grad(perm, a2, du)
    if placed:
        su = Scatter(dw_up, streams)
        su.keep, du = together(su.keep, du)
    dh1, dh1_low, sums2 = norm_back(perm, du, w_second, False, h1, gains[1], dh2, False)
    if placed:
        dh1_low, su.got, *sg.moved = together(dh1_low, su.got, *sg.moved)
        su.near()
        sg.last()
        dh1_low = settle([su, sg], dh1_low)
        su.send(0)
        sg.rows()
    dw_out = weight_grad(perm, mixed, dh1_low)
    if placed:
        so = Scatter(dw_out, ("xy",))
        so.keep, dh1_low = together(so.keep, dh1_low)
    do = out_back(perm, dh1_low, w_second)
    dq, own, far = attend_back(perm, lens, p, kv, do, logs, flat)
    if placed:
        dq, own, far, so.got, sg.total, part_down, *su.moved = together(
            dq, own, far, so.got, sg.total, part_down, *su.moved
        )
        r_down = lax.psum_scatter(part_down, "rows", scatter_dimension=0)
    got = swap(far, "scene", 1)
    if placed:
        su.cross()
        so.near()
        got = settle([su, so], got)
        su.send(1)
        so.send(0)
    dkv = (own + got.astype(F32)).astype(BF16)
    dp = jnp.concatenate([dq, dkv[0], dkv[1]], axis=1)
    dw_joint = weight_grad(perm, a1, dp)
    if placed:
        sj = Scatter(dw_joint, streams)
        sj.keep, dp, *su.moved = together(sj.keep, dp, *su.moved)
        su.last()
        dp = settle([su], dp)
        su.rows()
    dh0_low, sums1 = norm_back(perm, dp, w_first, False, h0, gains[0], dh1, True)
    if placed:
        dh0_low, sj.got, su.total, r_down, *so.moved = together(
            dh0_low, sj.got, su.total, r_down, *so.moved
        )
        r_down = r_down.astype(F32)
        sj.near()
        so.cross()
        dh0_low = settle([sj, so], dh0_low)
        sj.send(0)
        so.send(1)
    dw_patch = side_grad(perm, x.T, dh0_low)
    if placed:
        sp = Scatter(dw_patch, ("yx",))
        sp.keep, *moved = together(sp.keep, *sj.moved, *so.moved)
        sj.moved, so.moved = moved[:2], moved[2:]
        so.last()
        sj.cross()
        settle([sj])
        sj.send(1)
        sp.near()
        sp.send(0)
        sj.last()
        wide = sj.away[0].shape[-1]
        sj.away = [jnp.concatenate([sj.away[0], so.away[0]], axis=-1)]
        sj.rows()
        sj.total, so.total = sj.total[..., :wide], sj.total[..., wide:]
        sp.cross()
        sp.send(1)
        sp.last()
        sp.rows_apart()
        reduced = [t.get() for t in (sp, sj, so, su)] + [r_down, sg.get()]
    else:
        grads = [dw_patch, dw_joint, dw_out, dw_up, dw_down, dw_gauss]
        reduced = [scatter_plain(g, i in (0, 5)) for i, g in enumerate(grads)]
    reduced[5] = reduced[5].T
    vector_part = jnp.concatenate(
        [sums1[0], sums2[0], sums3[0], sums1[1], sums2[1], sums3[1], sums1[2], sums2[2], sums3[2]]
        + [d_bias_up[0], d_bias_gauss, loss[0]]
    )
    squares = sum(jnp.sum(item * item) for item in reduced)
    totals = total_sum(jnp.concatenate([vector_part, jnp.broadcast_to(squares, (128,))]).reshape(-1, 128))
    totals = totals.reshape(-1)
    vec = vectors.shape[0]
    vector_grad, loss_sum, square_sum = totals[:vec], totals[vec], totals[vec + 128]
    grad_norm = jnp.sqrt(square_sum + jnp.sum(vector_grad * vector_grad))
    factor = jnp.minimum(1.0, CLIP_NORM / (grad_norm + 1e-06))
    next_moments, next_weights, next_averages = ([], [], [])
    for grad, moment, master, average in zip(reduced + [vector_grad], moments, masters, averages):
        moment, weight, mean = weight_step(grad, factor, moment, master, average)
        next_moments.append(moment)
        next_weights.append(weight)
        next_averages.append(mean)
    return (loss_sum, pixel_count, grad_norm, *next_moments, *next_weights, *next_averages)


def solution(mesh):
    item = P(None, "scene", None, None, "rows")
    weight_specs = (P("rows", "scene"),) + (P("scene", "rows"),) * 5 + (P(),)
    in_specs = (P(None, "scene", "rows", None), P(), P(), item, item, item) + 3 * weight_specs
    out_specs = (P(), P(), P()) + 3 * weight_specs
    return jax.shard_map(body, mesh=mesh, in_specs=in_specs, out_specs=out_specs, check_vma=False)
```

```python
import functools

import jax
import jax.numpy as jnp
import numpy as np
from jax import lax
from jax.experimental import pallas as pl
from jax.experimental.pallas import tpu as pltpu
from jax.sharding import PartitionSpec as P

D = 1024
HEADS = 16
HD = 64
FF = 4096
POUT = 768
HT = 16
GV = 12
NG = POUT // GV

EPSILON = 1e-05
CLIP_NORM = 0.002
STEP_RATE = 1250.0
MOMENTUM = 0.9
AVERAGE_DECAY = 0.9

F32 = jnp.float32
BF16 = jnp.bfloat16
HIGHEST = lax.Precision.HIGHEST
BLOCKS = 8
WIDE = D // BLOCKS
VMEM_MB = 1024 * 1024
VMEM = 28
WIDE_VMEM = 56
TABLE = NG + 8


def nn(a, b):
    return lax.dot_general(a, b, (((1,), (0,)), ((), ())), preferred_element_type=F32)


def nt(a, b):
    return lax.dot_general(a, b, (((1,), (1,)), ((), ())), preferred_element_type=F32)


def tn(a, b):
    return lax.dot_general(a, b, (((0,), (0,)), ((), ())), preferred_element_type=F32)


def params(mb, n=1):
    return pltpu.CompilerParams(
        vmem_limit_bytes=mb * VMEM_MB, dimension_semantics=("arbitrary",) * n
    )


def lane_block(index, width):
    return pl.ds(pl.multiple_of(index * width, width), width)


PATCH = 144
GAUSS = POUT // 4


def side_rows(w_ref, place, first, count):
    return jnp.concatenate(
        [w_ref[j, place, first : first + count, :] for j in range(4)], axis=1
    )


def norm_store(perm, h_ref, g_ref, s_ref, a_ref, chunk):
    def step(i, carry):
        rows = pl.ds(pl.multiple_of(i * chunk, chunk), chunk)
        h = h_ref[rows, :]
        c = h - jnp.mean(h, axis=1, keepdims=True)
        var = jnp.mean(c * c, axis=1, keepdims=True)
        a = (c * lax.rsqrt(var + EPSILON) * g_ref[...] + s_ref[...]).astype(BF16)
        for b in range(BLOCKS):
            a_ref[rows, lane_block(perm[8 + b], WIDE)] = a[:, b * WIDE : (b + 1) * WIDE]
        return carry

    lax.fori_loop(0, h_ref.shape[0] // chunk, step, 0)


def rows_of(w_ref, z, width):
    block = w_ref[:, z]
    if block.shape[-1] != width:
        block = block[:, :, :width]
    return block.reshape(block.shape[0] * block.shape[1], width)


def embed_kernel(perm, x_ref, w0_ref, w1_ref, b_ref, g_ref, s_ref, h_ref, a_ref):
    x = x_ref[...]
    for i, w_ref in enumerate((w0_ref, w1_ref)):
        weight = jnp.concatenate(
            [side_rows(w_ref, perm[16 + z], 0, PATCH) for z in range(4)], axis=0
        )
        hr = nn(x, weight)
        for j in range(BLOCKS // 2):
            cols = lane_block(perm[i * BLOCKS // 2 + j], WIDE)
            h_ref[:, cols] = hr[:, j * WIDE : (j + 1) * WIDE] + b_ref[:, cols]
    norm_store(perm, h_ref, g_ref, s_ref, a_ref, 128)


def embed(perm, x, chunk, b, g, s):
    rows = x.shape[0]
    part = 256
    full = lambda shape: pl.BlockSpec(shape, lambda i, p: (0, 0))
    tile = lambda n: pl.BlockSpec((part, n), lambda i, p: (i, 0))
    weight = pl.BlockSpec((4, 4, PATCH + GAUSS, WIDE), lambda i, p: (0, 0, 0, 0))
    return pl.pallas_call(
        embed_kernel,
        grid_spec=pltpu.PrefetchScalarGridSpec(
            num_scalar_prefetch=1,
            grid=(rows // part,),
            in_specs=[tile(x.shape[1]), weight, weight]
            + [full((1, D))] * 3,
            out_specs=[tile(D), tile(D)],
        ),
        out_shape=[jax.ShapeDtypeStruct((rows, D), F32), jax.ShapeDtypeStruct((rows, D), BF16)],
        compiler_params=params(VMEM),
        cost_estimate=pl.CostEstimate(
            flops=2 * rows * D * 576, bytes_accessed=rows * D * 6 + 4 * D * 576, transcendentals=0
        ),
        name="embed_norm",
    )(perm, x, *chunk, b, g, s)


def first_of(chunk):
    return (0, 0) if chunk[0].shape[0] == 4 else (0, 1)


def project_kernel(perm, a_ref, w0_ref, w1_ref, r_ref, b_ref, g_ref, s_ref, h_ref, n_ref):
    z = pl.program_id(0)
    middle = a_ref.shape[1] // 2
    width = D // 4
    cols = lane_block(z, width)
    h_ref[:, cols] = (
        r_ref[...]
        + b_ref[...]
        + nn(a_ref[:, :middle], rows_of(w0_ref, 0, width))
        + nn(a_ref[:, middle:], rows_of(w1_ref, 0, width))
    )

    @pl.when(z == pl.num_programs(0) - 1)
    def _():
        norm_store(perm, h_ref, g_ref, s_ref, n_ref, 128)


def project(perm, a, chunk, at, res, b, g, s, grant=VMEM):
    rows, depth = a.shape
    width = D // 4
    full = lambda shape: pl.BlockSpec(shape, lambda z, p: (0, 0))
    weights = [
        pl.BlockSpec((4, 1, depth // 8, width), lambda z, p, i=i: (i, p[16 + z], 0, at))
        for i in first_of(chunk)
    ]
    return pl.pallas_call(
        project_kernel,
        grid_spec=pltpu.PrefetchScalarGridSpec(
            num_scalar_prefetch=1,
            grid=(4,),
            in_specs=[
                full((rows, depth)),
                *weights,
                pl.BlockSpec((rows, width), lambda z, p: (0, z)),
                pl.BlockSpec((1, width), lambda z, p: (0, z)),
                full((1, D)),
                full((1, D)),
            ],
            out_specs=[full((rows, D)), full((rows, D))],
        ),
        out_shape=[jax.ShapeDtypeStruct((rows, D), F32), jax.ShapeDtypeStruct((rows, D), BF16)],
        compiler_params=params(grant),
        cost_estimate=pl.CostEstimate(
            flops=2 * rows * D * depth,
            bytes_accessed=rows * D * 10 + 2 * D * depth + 2 * rows * depth,
            transcendentals=0,
        ),
        name="project_norm",
    )(perm, a, *chunk, res, b, g, s)


def halves(a_ref, w0_ref, w1_ref, width):
    middle = a_ref.shape[1] // 2
    return nn(a_ref[:, :middle], rows_of(w0_ref, 0, width)) + nn(
        a_ref[:, middle:], rows_of(w1_ref, 0, width)
    )


def joint_kernel(perm, a_ref, w0_ref, w1_ref, p_ref):
    p_ref[...] = halves(a_ref, w0_ref, w1_ref, p_ref.shape[1]).astype(BF16)


def joint(perm, a, chunk):
    rows = a.shape[0]
    part = 3 * D // 4
    weight = pl.BlockSpec((4, 1, WIDE, part), lambda z, p: (0, p[16 + z], 0, 0))
    return pl.pallas_call(
        joint_kernel,
        grid_spec=pltpu.PrefetchScalarGridSpec(
            num_scalar_prefetch=1,
            grid=(4,),
            in_specs=[pl.BlockSpec((rows, D), lambda z, p: (0, 0)), weight, weight],
            out_specs=pl.BlockSpec((rows, part), lambda z, p: (0, z)),
        ),
        out_shape=jax.ShapeDtypeStruct((rows, 3 * D), BF16),
        compiler_params=params(VMEM),
        cost_estimate=pl.CostEstimate(
            flops=6 * rows * D * D, bytes_accessed=rows * D * 8 + 6 * D * D, transcendentals=0
        ),
        name="joint",
    )(perm, a, *chunk)


def gauss_kernel(perm, a_ref, w0_ref, w1_ref, b_ref, z_ref):
    half = D // 2
    z_ref[...] = (
        nt(side_rows(w0_ref, 0, PATCH, GAUSS), a_ref[:, :half])
        + nt(side_rows(w1_ref, 0, PATCH, GAUSS), a_ref[:, half:])
        + b_ref[...]
    )


def gauss(perm, a, chunk, b):
    rows = a.shape[0]
    weight = pl.BlockSpec((4, 1, PATCH + GAUSS, WIDE), lambda z, p: (0, p[16 + z], 0, 0))
    return pl.pallas_call(
        gauss_kernel,
        grid_spec=pltpu.PrefetchScalarGridSpec(
            num_scalar_prefetch=1,
            grid=(4,),
            in_specs=[
                pl.BlockSpec((rows, D), lambda z, p: (0, 0)),
                weight,
                weight,
                pl.BlockSpec((GAUSS, 1), lambda z, p: (z, 0)),
            ],
            out_specs=pl.BlockSpec((GAUSS, rows), lambda z, p: (z, 0)),
        ),
        out_shape=jax.ShapeDtypeStruct((POUT, rows), F32),
        compiler_params=params(VMEM),
        cost_estimate=pl.CostEstimate(
            flops=2 * rows * D * POUT, bytes_accessed=rows * D * 5 + 2 * D * POUT, transcendentals=0
        ),
        name="gauss",
    )(perm, a, *chunk, b[:, None])


def out_back_kernel(perm, d_ref, w0_ref, w1_ref, o_ref):
    width = D // 4
    for i, w_ref in enumerate((w0_ref, w1_ref)):
        total = sum(
            nt(d_ref[:, z * width : (z + 1) * width], rows_of(w_ref, perm[16 + z], width))
            for z in range(4)
        )
        o_ref[:, i * D // 2 : (i + 1) * D // 2] = total.astype(BF16)


def out_back(perm, d, chunk):
    rows = d.shape[0]
    part = 256
    weight = pl.BlockSpec((4, 4, WIDE, D // 4), lambda i, p: (0, 0, 0, 4))
    tile = pl.BlockSpec((part, D), lambda i, p: (i, 0))
    return pl.pallas_call(
        out_back_kernel,
        grid_spec=pltpu.PrefetchScalarGridSpec(
            num_scalar_prefetch=1,
            grid=(rows // part,),
            in_specs=[tile, weight, weight],
            out_specs=tile,
        ),
        out_shape=jax.ShapeDtypeStruct((rows, D), BF16),
        compiler_params=params(VMEM),
        cost_estimate=pl.CostEstimate(
            flops=2 * rows * D * D, bytes_accessed=rows * D * 4 + 2 * D * D, transcendentals=0
        ),
        name="out_back",
    )(perm, d, *chunk)


def grad_kernel(perm, a_ref, d_ref, *refs):
    *outs, turned_ref = refs
    middle = a_ref.shape[1] // 2

    @pl.when(pl.program_id(0) == 0)
    def _():
        turned_ref[...] = a_ref[...].T

    for i in (1, 0):
        g = nn(turned_ref[i * middle : (i + 1) * middle, :], d_ref[...]).astype(BF16)
        g = g.reshape(4, 1, middle // 4, g.shape[1])
        if len(outs) == 2:
            outs[i][...] = g
        else:
            for j in range(4):
                outs[0][perm[4 * i + j]] = g[j]


def weight_grad(perm, a, d, whole=False):
    tokens, depth = a.shape
    n = d.shape[1] // 4
    right = pl.BlockSpec((tokens, n), lambda z, p: (0, z))
    count = 8 if whole else 4
    out = pl.BlockSpec((count, 1, depth // 8, n), lambda z, p: (0, p[16 + z], 0, 0))
    shape = jax.ShapeDtypeStruct((count, 4, depth // 8, n), BF16)
    return pl.pallas_call(
        grad_kernel,
        grid_spec=pltpu.PrefetchScalarGridSpec(
            num_scalar_prefetch=1,
            grid=(4,),
            in_specs=[pl.BlockSpec((tokens, depth), lambda z, p: (0, 0)), right],
            out_specs=[out] * (8 // count),
            scratch_shapes=[pltpu.VMEM((depth, tokens), BF16)],
        ),
        out_shape=[shape] * (8 // count),
        compiler_params=params(VMEM),
        cost_estimate=pl.CostEstimate(
            flops=8 * tokens * depth * n,
            bytes_accessed=2 * tokens * (depth + 4 * n) + 8 * depth * n,
            transcendentals=0,
        ),
        name="weight_grad",
    )(perm, a, d)


def side_grad_kernel(perm, d_ref, a_ref, *outs):
    g = nn(d_ref[...], a_ref[...]).astype(BF16)
    for j in range(BLOCKS):
        block = g[:, j * WIDE : (j + 1) * WIDE]
        if len(outs) == 2:
            outs[j // 4][j % 4, 0] = block
        else:
            outs[0][perm[j], 0] = block


def side_grad(perm, d, a, whole=False):
    tokens = a.shape[0]
    n = d.shape[0] // 4
    count = 8 if whole else 4
    out = pl.BlockSpec((count, 1, n, WIDE), lambda z, p: (0, p[16 + z], 0, 0))
    shape = jax.ShapeDtypeStruct((count, 4, n, WIDE), BF16)
    return pl.pallas_call(
        side_grad_kernel,
        grid_spec=pltpu.PrefetchScalarGridSpec(
            num_scalar_prefetch=1,
            grid=(4,),
            in_specs=[
                pl.BlockSpec((n, tokens), lambda z, p: (z, 0)),
                pl.BlockSpec((tokens, D), lambda z, p: (0, 0)),
            ],
            out_specs=[out] * (8 // count),
        ),
        out_shape=[shape] * (8 // count),
        compiler_params=params(VMEM),
        cost_estimate=pl.CostEstimate(
            flops=8 * tokens * D * n, bytes_accessed=2 * tokens * D + 16 * D * n, transcendentals=0
        ),
        name="side_grad",
    )(perm, d, a)


GELU_C = float(np.sqrt(2.0 / np.pi))


def up_kernel(perm, a_ref, w0_ref, w1_ref, b_ref, u_ref, g_ref):
    u = halves(a_ref, w0_ref, w1_ref, u_ref.shape[1]) + b_ref[...]
    u_ref[...] = u
    t = jnp.tanh(GELU_C * (u + 0.044715 * (u * u * u)))
    g_ref[...] = (u * (0.5 * (1.0 + t))).astype(BF16)


def up_project(perm, a, chunk, b):
    rows = a.shape[0]
    part = FF // BLOCKS
    weight = pl.BlockSpec((4, 1, WIDE, part), lambda n, p: (0, p[16 + n // 2], 0, n % 2))
    return pl.pallas_call(
        up_kernel,
        grid_spec=pltpu.PrefetchScalarGridSpec(
            num_scalar_prefetch=1,
            grid=(BLOCKS,),
            in_specs=[
                pl.BlockSpec((rows, D), lambda n, p: (0, 0)),
                weight,
                weight,
                pl.BlockSpec((1, part), lambda n, p: (0, n)),
            ],
            out_specs=[
                pl.BlockSpec((rows, part), lambda n, p: (0, n)),
                pl.BlockSpec((rows, part), lambda n, p: (0, p[8 + n])),
            ],
        ),
        out_shape=[jax.ShapeDtypeStruct((rows, FF), F32), jax.ShapeDtypeStruct((rows, FF), BF16)],
        compiler_params=params(WIDE_VMEM),
        cost_estimate=pl.CostEstimate(
            flops=2 * rows * D * FF, bytes_accessed=rows * FF * 6 + 2 * D * FF, transcendentals=rows * FF
        ),
        name="up_gelu",
    )(perm, a, *chunk, b)


def down_back_kernel(perm, d_ref, w0_ref, w1_ref, u_ref, du_ref, sum_ref, dg_ref):
    width = D // 4

    def product(w_ref):
        dg_ref[...] = sum(
            nt(d_ref[:, z * width : (z + 1) * width], rows_of(w_ref, perm[16 + z], width))
            for z in range(4)
        )

    first = pl.program_id(0) < pl.num_programs(0) // 2
    pl.when(first)(lambda: product(w0_ref))
    pl.when(jnp.logical_not(first))(lambda: product(w1_ref))
    dg = dg_ref[...]
    u = u_ref[...]
    u2 = u * u
    t = jnp.tanh(GELU_C * (u + 0.044715 * (u2 * u)))
    slope = 0.5 * (1.0 + t) + (0.5 * GELU_C) * u * (1.0 - t * t) * (1.0 + (3 * 0.044715) * u2)
    du = slope * dg
    du_ref[...] = du.astype(BF16)
    sum_ref[...] = jnp.sum(du, axis=0, keepdims=True)


def down_back(perm, d, chunk, u):
    rows = d.shape[0]
    second = 4 * first_of(chunk)[1]
    part = FF // BLOCKS
    return pl.pallas_call(
        down_back_kernel,
        grid_spec=pltpu.PrefetchScalarGridSpec(
            num_scalar_prefetch=1,
            grid=(BLOCKS,),
            in_specs=[
                pl.BlockSpec((rows, D), lambda j, p: (0, 0)),
                pl.BlockSpec((1, 4, part, D // 4), lambda j, p: (jnp.minimum(j, 3), 0, 0, 0)),
                pl.BlockSpec(
                    (1, 4, part, D // 4), lambda j, p: (jnp.maximum(j - 4, 0) + second, 0, 0, 0)
                ),
                pl.BlockSpec((rows, part), lambda j, p: (0, p[j])),
            ],
            out_specs=[
                pl.BlockSpec((rows, part), lambda j, p: (0, p[j])),
                pl.BlockSpec((1, part), lambda j, p: (0, p[j])),
            ],
            scratch_shapes=[pltpu.VMEM((rows, part), F32)],
        ),
        out_shape=[jax.ShapeDtypeStruct((rows, FF), BF16), jax.ShapeDtypeStruct((1, FF), F32)],
        compiler_params=params(WIDE_VMEM),
        cost_estimate=pl.CostEstimate(
            flops=2 * rows * D * FF, bytes_accessed=rows * FF * 6 + 2 * D * FF, transcendentals=rows * FF
        ),
        name="down_back_gelu",
    )(perm, d, *chunk, u)


def back_kernel(has_res, placed, turned, perm, *refs):
    if has_res:
        d_ref, w0_ref, w1_ref, h_ref, g_ref, r_ref, *outs = refs
    else:
        d_ref, w0_ref, w1_ref, h_ref, g_ref, *outs = refs
        r_ref = None
    if placed:
        low_ref, sums_ref, acc_ref, part_ref = outs
        dh_ref = None
    else:
        dh_ref, low_ref, sums_ref, acc_ref, part_ref = outs
    n = pl.program_id(0)

    if turned:
        d = d_ref[...].T
        for i, w_ref in enumerate((w0_ref, w1_ref)):
            weight = jnp.concatenate(
                [side_rows(w_ref, perm[16 + z], PATCH, GAUSS) for z in range(4)], axis=0
            )
            acc_ref[:, i * D // 2 : (i + 1) * D // 2] = nn(d, weight)
    else:
        d = d_ref[...]
        width = d.shape[1]

        @pl.when(n == 0)
        def _():
            acc_ref[:, : D // 2] = nt(d, rows_of(w0_ref, 0, width))
            acc_ref[:, D // 2 :] = nt(d, rows_of(w1_ref, 0, width))

        @pl.when(n > 0)
        def _():
            acc_ref[:, : D // 2] += nt(d, rows_of(w0_ref, 0, width))
            acc_ref[:, D // 2 :] += nt(d, rows_of(w1_ref, 0, width))

    @pl.when(n == pl.num_programs(0) - 1)
    def _():
        chunk = 128
        part_ref[...] = jnp.zeros_like(part_ref)

        def fold(x):
            return jnp.sum(x.reshape(chunk // 8, 8, D), axis=0)

        def step(i, carry):
            rows = pl.ds(pl.multiple_of(i * chunk, chunk), chunk)
            h = h_ref[rows, :]
            c = h - jnp.mean(h, axis=1, keepdims=True)
            var = jnp.mean(c * c, axis=1, keepdims=True)
            rstd = lax.rsqrt(var + EPSILON)
            xh = c * rstd
            da = jnp.concatenate(
                [acc_ref[rows, lane_block(perm[8 + b], WIDE)] for b in range(BLOCKS)], axis=1
            )
            dxh = da * xh
            part_ref[0] += fold(dxh)
            part_ref[1] += fold(da)
            dy = da * g_ref[...]
            first = jnp.mean(dy, axis=1, keepdims=True)
            second = jnp.mean(dy * xh, axis=1, keepdims=True)
            dh = rstd * (dy - first - xh * second)
            if has_res:
                dh = dh + r_ref[rows, :]
            part_ref[2] += fold(dh)
            low = dh.astype(BF16)
            if placed:
                for b in range(BLOCKS):
                    low_ref[rows, lane_block(perm[8 + b], WIDE)] = low[:, b * WIDE : (b + 1) * WIDE]
            else:
                dh_ref[rows, :] = dh
                low_ref[rows, :] = low
            return carry

        lax.fori_loop(0, h_ref.shape[0] // chunk, step, 0)
        sums_ref[...] = jnp.concatenate(
            [jnp.sum(part_ref[i], axis=0, keepdims=True) for i in range(3)]
            + [jnp.zeros((5, D), F32)],
            axis=0,
        )


def norm_back(perm, d, chunk, turned, h, g, res, placed):
    full = lambda shape: pl.BlockSpec(shape, lambda n, p: (0, 0))
    rows = h.shape[0]
    wide = d.size // rows
    if turned:
        left = full(d.shape)
        weight = pl.BlockSpec((4, 4, PATCH + GAUSS, WIDE), lambda n, p: (0, 0, 0, 0))
    else:
        part = wide // 4
        left = pl.BlockSpec((rows, part), lambda n, p: (0, n))
        weight = pl.BlockSpec((4, 1, WIDE, part), lambda n, p: (0, p[16 + n], 0, 0))
    args = [d, *chunk, h, g]
    specs = [left, weight, weight, full((rows, D)), full((1, D))]
    if res is not None:
        args.append(res)
        specs.append(full((rows, D)))
    out_specs = [full((rows, D)), full((8, D))]
    out_shape = [jax.ShapeDtypeStruct((rows, D), BF16), jax.ShapeDtypeStruct((8, D), F32)]
    if not placed:
        out_specs = [full((rows, D))] + out_specs
        out_shape = [jax.ShapeDtypeStruct((rows, D), F32)] + out_shape
    return pl.pallas_call(
        functools.partial(back_kernel, res is not None, placed, turned),
        grid_spec=pltpu.PrefetchScalarGridSpec(
            num_scalar_prefetch=1,
            grid=(1 if turned else 4,),
            in_specs=specs,
            out_specs=out_specs,
            scratch_shapes=[pltpu.VMEM((rows, D), F32), pltpu.VMEM((3, 8, D), F32)],
        ),
        out_shape=out_shape,
        compiler_params=params(WIDE_VMEM if placed else VMEM),
        cost_estimate=pl.CostEstimate(
            flops=2 * rows * D * wide,
            bytes_accessed=rows * D * 14 + 2 * D * wide + 2 * rows * wide,
            transcendentals=0,
        ),
        name="norm_back",
    )(perm, *args)


SCALE = HD ** (-0.5)
PAIR = 2 * HD
PAIRS = HEADS // 2


def lanes_of(side):
    lane = lax.broadcasted_iota(jnp.int32, (1, PAIR), 1)
    mine = (lane < HD) == (side == 0)
    return lane, mine, HD * (1 - side)


def masked_keys(keys, first, length, extra):
    lane, mine, free = first
    spot = lax.broadcasted_iota(jnp.int32, (keys.shape[0], 1), 0)
    hidden = jnp.where(spot < length, 0.0, -1e30).astype(BF16)
    rest = jnp.where(lane == free, hidden, 0.0).astype(BF16)
    if extra:
        ones = jnp.logical_and(lane > free, lane <= free + extra)
        rest = jnp.where(ones, 1.0, rest).astype(BF16)
    return jnp.where(mine, keys, rest)


def attend_kernel(perm, lens, q_ref, k0_ref, k1_ref, v0_ref, v1_ref, o_ref, l_ref, f_ref):
    v0, v1 = v0_ref[...], v1_ref[...]
    sides = [lanes_of(side) for side in range(2)]
    keys = [
        [masked_keys(ref[...], where, lens[j], 0) for j, ref in enumerate((k0_ref, k1_ref))]
        for where in sides
    ]
    chunk = 256
    for i in range(q_ref.shape[0] // chunk):
        rows = slice(i * chunk, (i + 1) * chunk)
        q = (q_ref[rows, :] * SCALE).astype(BF16)
        outs = []
        logs = []
        for (lane, mine, free), (k0, k1) in zip(sides, keys):
            qm = jnp.where(mine, q, jnp.where(lane == free, 1.0, 0.0).astype(BF16))
            s0 = nt(qm, k0)
            s1 = nt(qm, k1)
            top = jnp.max(jnp.maximum(s0, s1), axis=1, keepdims=True)
            e0 = jnp.exp(s0 - top)
            e1 = jnp.exp(s1 - top)
            total = jnp.sum(e0 + e1, axis=1, keepdims=True)
            outs.append((nn(e0.astype(BF16), v0) + nn(e1.astype(BF16), v1)) * (1.0 / total))
            logs.append(top + jnp.log(total))
        lane = sides[0][0]
        mixed = jnp.where(lane < HD, outs[0], outs[1])
        o_ref[rows, :] = mixed.astype(BF16)
        f_ref[rows, :] = mixed
        l_ref[rows, :] = jnp.where(lane < HD, logs[1], logs[0])


def attend(perm, lens, p, kv):
    rows = p.shape[0]
    block = lambda first: pl.BlockSpec((rows, PAIR), lambda h, m, n: (0, first + h))
    return pl.pallas_call(
        attend_kernel,
        grid_spec=pltpu.PrefetchScalarGridSpec(
            num_scalar_prefetch=2,
            grid=(PAIRS,),
            in_specs=[block(0), block(PAIRS), block(0), block(2 * PAIRS), block(PAIRS)],
            out_specs=[
                pl.BlockSpec((rows, PAIR), lambda h, m, n: (0, m[8 + h])),
                block(0),
                block(0),
            ],
        ),
        out_shape=[
            jax.ShapeDtypeStruct((rows, D), BF16),
            jax.ShapeDtypeStruct((rows, D), F32),
            jax.ShapeDtypeStruct((rows, D), F32),
        ],
        compiler_params=params(VMEM),
        cost_estimate=pl.CostEstimate(
            flops=8 * rows * rows * D,
            bytes_accessed=12 * rows * D,
            transcendentals=2 * rows * rows * HEADS,
        ),
        name="attend",
    )(perm, lens, p, p, kv, p, kv)


def attend_back_kernel(
    perm, lens, q_ref, k0_ref, k1_ref, v0_ref, v1_ref, do_ref, l_ref, f_ref, dq_ref, own_ref, far_ref
):
    values = []
    for side in range(2):
        lane, mine, free = lanes_of(side)
        ones = jnp.logical_and(lane >= free, lane < free + 3)
        rest = jnp.where(ones, 1.0, 0.0).astype(BF16)
        values.append([jnp.where(mine, ref[...], rest) for ref in (v0_ref, v1_ref)])
    q_all, do_all = q_ref[...], do_ref[...]
    sides = [lanes_of(side) for side in range(2)]
    keys = [
        [masked_keys(ref[...], where, lens[j], 3) for j, ref in enumerate((k0_ref, k1_ref))]
        for where in sides
    ]
    turned = [[k.T for k in pair] for pair in keys]
    chunk = 256
    dk = [None, None]
    dv = [None, None]
    for i in range(q_ref.shape[0] // chunk):
        rows = slice(i * chunk, (i + 1) * chunk)

        def thirds(x):
            first = x.astype(BF16)
            left = x - first.astype(F32)
            second = left.astype(BF16)
            return first, second, (left - second.astype(F32)).astype(BF16)

        logs = thirds(l_ref[rows, :])
        flow = do_all[rows, :].astype(F32) * f_ref[rows, :]
        dqs = []
        for (lane, mine, free), (k0, k1), vs, across in zip(sides, keys, values, turned):
            qm = jnp.where(mine, q_all[rows, :], 0.0).astype(BF16)
            dom = jnp.where(mine, do_all[rows, :], 0.0).astype(BF16)
            rest = jnp.where(lane == free, 1.0, 0.0).astype(BF16)
            for at, part in enumerate(logs):
                rest = jnp.where(lane == free + 1 + at, -part, rest)
            qs = jnp.where(mine, (q_all[rows, :] * SCALE).astype(BF16), rest)
            probs = [jnp.exp(nt(k, qs)) for k in (k0, k1)]
            delta = jnp.sum(jnp.where(mine, flow, 0.0), axis=1, keepdims=True)
            less = dom
            for at, part in enumerate(thirds(delta)):
                less = jnp.where(lane == free + at, -part, less)
            da = [nt(v, less) for v in vs]
            dq = None
            for j in range(2):
                ds = (probs[j] * da[j]).astype(BF16)
                term = nn(across[j], ds)
                dq = term if dq is None else dq + term
                term = nn(ds, qm)
                dk[j] = term if dk[j] is None else dk[j] + term
                term = nn(probs[j].astype(BF16), dom)
                dv[j] = term if dv[j] is None else dv[j] + term
            dqs.append(dq)
        dq = jnp.concatenate([dqs[0][:HD], dqs[1][HD:]], axis=0) * SCALE
        dq_ref[rows, :] = dq.T.astype(BF16)
    own_ref[0] = dk[0] * SCALE
    own_ref[1] = dv[0]
    far_ref[0] = (dk[1] * SCALE).astype(BF16)
    far_ref[1] = dv[1].astype(BF16)


def attend_back(perm, lens, p, kv, do, logs, flat):
    rows = p.shape[0]
    block = lambda first: pl.BlockSpec((rows, PAIR), lambda h, m, n: (0, first + h))
    both = pl.BlockSpec((2, rows, PAIR), lambda h, m, n: (0, 0, h))
    return pl.pallas_call(
        attend_back_kernel,
        grid_spec=pltpu.PrefetchScalarGridSpec(
            num_scalar_prefetch=2,
            grid=(PAIRS,),
            in_specs=[
                block(0),
                block(PAIRS),
                block(0),
                block(2 * PAIRS),
                block(PAIRS),
                pl.BlockSpec((rows, PAIR), lambda h, m, n: (0, m[8 + h])),
                block(0),
                block(0),
            ],
            out_specs=[block(0), both, both],
        ),
        out_shape=[
            jax.ShapeDtypeStruct((rows, D), BF16),
            jax.ShapeDtypeStruct((2, rows, D), F32),
            jax.ShapeDtypeStruct((2, rows, D), BF16),
        ],
        compiler_params=params(VMEM),
        cost_estimate=pl.CostEstimate(
            flops=20 * rows * rows * D,
            bytes_accessed=28 * rows * D,
            transcendentals=2 * rows * rows * HEADS,
        ),
        name="attend_back",
    )(perm, lens, p, p, kv, p, kv, do, logs, flat)


def iota(shape, dim):
    return lax.broadcasted_iota(jnp.int32, shape, dim)


def render_kernel(
    views_ref, inv_ref, z_ref, zx_ref, rd_ref, mc_ref, dz_ref, dzx_ref, loss_ref,
    tf_ref, both_ref, o_ref, wm_ref, a_ref, dt_ref, tok_ref, edge_ref, zs_ref,
):
    width = 256
    pixels = rd_ref.shape[-1]
    kg = 8

    lanes = 128
    parts = z_ref.shape[1] // lanes
    for i in range(parts):
        zs_ref[i] = z_ref[:, i * lanes : (i + 1) * lanes]
    zs_ref[parts] = zx_ref[...]

    def values(i):
        return [zs_ref[i, pl.ds(v, NG, stride=GV), :] for v in range(GV)]

    def shade(z):
        colour = [jax.nn.sigmoid(z[i]) for i in range(3)]
        gate = jax.nn.sigmoid(z[3])
        square = z[4] * z[4]
        for i in range(5, GV):
            square = square + z[i] * z[i]
        opacity = gate * jnp.exp(-0.5 * (square / (GV - 4)))
        return colour, gate, opacity

    own_group = iota((NG, width), 0) % 16 == iota((NG, width), 1) // 16

    def spread(base):
        return (iota((128, width), 0) == base + iota((128, width), 1) % 16).astype(F32)

    def rim_rows(table, base):
        wide = lax.dot_general(
            table, spread(base), (((1,), (0,)), ((), ())), precision=HIGHEST,
            preferred_element_type=F32,
        )
        return jnp.sum(jnp.where(own_group, wide, 0.0).reshape(4, 16, width), axis=1)

    def rim_back(rows, base):
        wide = jnp.concatenate(
            [jnp.broadcast_to(rows[j : j + 1, :], (16, width)) for j in range(4)], axis=0
        )
        return lax.dot_general(
            jnp.where(own_group, wide, 0.0), spread(base), (((1,), (1,)), ((), ())),
            precision=HIGHEST, preferred_element_type=F32,
        )

    def place(i):
        if i == parts:
            return edge_ref, slice(0, lanes)
        return tok_ref, slice(i * lanes, (i + 1) * lanes)

    for i in range(parts + 1):
        out_ref, cols = place(i)
        colour, gate, opacity = shade(values(i))
        for ch in range(3):
            out_ref[ch * NG : (ch + 1) * NG, cols] = colour[ch] * opacity
        out_ref[3 * NG : 4 * NG, cols] = opacity

    for ch in range(4):
        rows = slice(ch * NG, (ch + 1) * NG)
        at = ch * TABLE
        tf_ref[0, at : at + NG, :] = tok_ref[rows, 0:width]
        tf_ref[1, at : at + NG, :] = tok_ref[rows, width : 2 * width]
        tf_ref[0, at + NG : at + NG + 4, :] = rim_rows(edge_ref[rows, :], 0)
        tf_ref[0, at + NG + 4 : at + NG + 8, :] = rim_rows(tok_ref[rows, width : width + 128], 0)
        tf_ref[1, at + NG : at + NG + 4, :] = rim_rows(tok_ref[rows, width - 128 : width], 112)
        tf_ref[1, at + NG + 4 : at + NG + 8, :] = rim_rows(edge_ref[rows, :], 16)
    for block in range(2):
        table = tf_ref[block]
        high = table.astype(BF16)
        both_ref[block, : 4 * TABLE] = high
        both_ref[block, 4 * TABLE :] = (table - high.astype(F32)).astype(BF16)
    dt_ref[...] = jnp.zeros_like(dt_ref)
    inverse = inv_ref[0]
    row_hi = iota((width, pixels), 0).astype(F32).astype(BF16)
    row_lo = iota((TABLE, pixels), 0)
    one_low, zero_low = jnp.ones((), BF16), jnp.zeros((), BF16)

    def features(c):
        return jnp.tanh(mc_ref[0] * c[0] + mc_ref[1] * c[1] + mc_ref[2] * c[2])

    def view(t, loss):
        for block in range(2):
            r = rd_ref[block, t, 0:kg, :].astype(jnp.int32)
            weight = rd_ref[block, t, kg : 2 * kg, :]
            token = lax.shift_right_logical(r, 6)
            g = jnp.bitwise_and(r, NG - 1)
            after = token >= HT + width
            inside = jnp.logical_and(token >= HT, jnp.logical_not(after))
            rim = jnp.where(after, token - (HT + width), token)
            high = jnp.where(inside, token - HT, jnp.bitwise_and(g, 15) * 16 + rim)
            low = jnp.where(
                inside, g, NG + lax.shift_right_logical(g, 4) + jnp.where(after, 4, 0)
            )
            sums = [jnp.zeros((8, pixels), F32) for _ in range(4)]
            high = high.astype(F32).astype(BF16)
            table = both_ref[block]
            for k in range(kg):
                cols = slice(k * pixels, (k + 1) * pixels)
                one = jnp.where(row_hi == high[k : k + 1, :], one_low, zero_low)
                o_ref[block, :, cols] = one
                wm = jnp.where(row_lo == low[k : k + 1, :], weight[k : k + 1, :], 0.0)
                wm_ref[block, :, cols] = wm
                picked = nn(table, one)
                picked = picked[: 4 * TABLE] + picked[4 * TABLE :]
                for ch in range(4):
                    part = picked[ch * TABLE : (ch + 1) * TABLE, :] * wm
                    sums[ch] = sums[ch] + jnp.sum(part.reshape(TABLE // 8, 8, pixels), axis=0)
            sums = [jnp.sum(s, axis=0, keepdims=True) for s in sums]
            scale = 1.0 / (1.0 + sums[3])
            seen = [sums[i] * scale for i in range(3)]
            goal = [rd_ref[block, t, 2 * kg + i : 2 * kg + i + 1, :] for i in range(3)]
            f_seen = features(seen)
            gap = f_seen - features(goal)
            diff = [seen[i] - goal[i] for i in range(3)]
            loss = loss + diff[0] * diff[0] + diff[1] * diff[1] + diff[2] * diff[2]
            loss = loss + 0.5 * jnp.sum(gap * gap, axis=0, keepdims=True)
            pull = gap * (1.0 - f_seen * f_seen)
            d_seen = [
                inverse * (2.0 * diff[i] + jnp.sum(pull * mc_ref[i], axis=0, keepdims=True))
                for i in range(3)
            ]
            d_sum = [d * scale for d in d_seen]
            d_sum.append(
                -(d_seen[0] * seen[0] + d_seen[1] * seen[1] + d_seen[2] * seen[2]) * scale
            )
            for k in range(kg):
                cols = slice(k * pixels, (k + 1) * pixels)
                wm = wm_ref[block, :, cols]
                full = jnp.concatenate([wm * d_sum[ch] for ch in range(4)], axis=0)
                a_ref[block, :, cols] = full.astype(BF16)
            dt_ref[block] += nt(a_ref[block], o_ref[block])
        return loss

    loss = lax.fori_loop(0, views_ref[0], view, jnp.zeros((1, pixels), F32))
    loss_ref[...] = jnp.broadcast_to(jnp.sum(loss, axis=1, keepdims=True), loss_ref.shape)

    for ch in range(4):
        rows = slice(ch * NG, (ch + 1) * NG)
        at = ch * TABLE + NG
        tok_ref[rows, 0:width] = dt_ref[0, at - NG : at, :]
        tok_ref[rows, width : 2 * width] = dt_ref[1, at - NG : at, :]
        tok_ref[rows, width : width + 128] += rim_back(dt_ref[0, at + 4 : at + 8, :], 0)
        tok_ref[rows, width - 128 : width] += rim_back(dt_ref[1, at : at + 4, :], 112)
        edge_ref[rows, :] = rim_back(dt_ref[0, at : at + 4, :], 0) + rim_back(
            dt_ref[1, at + 4 : at + 8, :], 16
        )

    for part in range(parts + 1):
        grad_ref, cols = place(part)
        z = values(part)
        colour, gate, opacity = shade(z)
        d = [grad_ref[i * NG : (i + 1) * NG, cols] for i in range(4)]
        d_opacity = d[3]
        for i in range(3):
            d_opacity = d_opacity + d[i] * colour[i]
            zs_ref[part, pl.ds(i, NG, stride=GV), :] = d[i] * opacity * colour[i] * (1.0 - colour[i])
        both = d_opacity * opacity
        zs_ref[part, pl.ds(3, NG, stride=GV), :] = both * (1.0 - gate)
        for i in range(4, GV):
            zs_ref[part, pl.ds(i, NG, stride=GV), :] = both * z[i] * (-1.0 / (GV - 4))
    for i in range(parts):
        dz_ref[:, i * lanes : (i + 1) * lanes] = zs_ref[i]
    dzx_ref[...] = zs_ref[parts]


def render(views, inverse, zt, zx, rd):
    tokens = zt.shape[1]
    pixels = rd.shape[-1]
    slots = 8 * pixels
    counter = np.arange(48, dtype=np.float32).reshape(16, 3)
    mix = (np.float32(0.8) * np.cos(np.float32(1.7) * counter + np.float32(0.3))).astype(np.float32)
    mix = jnp.broadcast_to(jnp.asarray(mix.T)[:, :, None], (3, 16, pixels))
    whole = lambda x: pl.BlockSpec(x.shape, lambda: (0,) * x.ndim)
    smem = pl.BlockSpec(memory_space=pltpu.SMEM)
    shape = jax.ShapeDtypeStruct
    return pl.pallas_call(
        render_kernel,
        in_specs=[smem, smem, whole(zt), whole(zx), whole(rd), whole(mix)],
        out_specs=[whole(zt), whole(zx), pl.BlockSpec((8, 128), lambda: (0, 0))],
        out_shape=[shape(zt.shape, F32), shape(zx.shape, F32), shape((8, 128), F32)],
        scratch_shapes=[
            pltpu.VMEM((2, 4 * TABLE, 256), F32),
            pltpu.VMEM((2, 8 * TABLE, 256), BF16),
            pltpu.VMEM((2, 256, slots), BF16),
            pltpu.VMEM((2, TABLE, slots), F32),
            pltpu.VMEM((2, 4 * TABLE, slots), BF16),
            pltpu.VMEM((2, 4 * TABLE, 256), F32),
            pltpu.VMEM((4 * NG, tokens), F32),
            pltpu.VMEM((4 * NG, 128), F32),
            pltpu.VMEM((tokens // 128 + 1, POUT, 128), F32),
        ],
        compiler_params=pltpu.CompilerParams(vmem_limit_bytes=VMEM * VMEM_MB),
        cost_estimate=pl.CostEstimate(
            flops=24 * slots * 4 * TABLE * 256 * 6, bytes_accessed=4 * 1024 * 1024, transcendentals=0
        ),
        name="render",
    )(views, inverse, zt, zx, rd, mix)


def flip_pairs(n, bit):
    return [(i, i ^ bit) for i in range(n)]


def swap(x, axis, bit):
    return lax.ppermute(x, axis, flip_pairs(lax.axis_size(axis), bit))


CORE, XBIT, YBIT = 1, 2, 4
PLACES = np.array([0, 2, 4, 6, 1, 3, 5, 7], np.int32)


def total_sum(x):
    if lax.axis_size("scene") == BLOCKS and lax.axis_size("rows") == 4:
        x = x + swap(x, "scene", CORE)
        near, far, both = (swap(x, "scene", bit) for bit in (XBIT, YBIT, XBIT | YBIT))
        x = (x + near) + (far + both)
        near, far, both = (swap(x, "rows", bit) for bit in (1, 2, 3))
        return (x + near) + (far + both)
    for axis in ("scene", "rows"):
        bit = 1
        while bit < lax.axis_size(axis):
            x = x + swap(x, axis, bit)
            bit = 2 * bit
    return x


def gather_whole(shard):
    whole = lax.all_gather(shard, ("scene", "rows"), axis=0)
    return (whole.reshape((BLOCKS, 4) + shard.shape),) * 2


def gather_plain(shards, turned):
    parts = []
    for shard in shards:
        if turned:
            wide = lax.all_gather(shard, "rows", axis=0, tiled=True)
            full = lax.all_gather(wide, "scene", axis=1, tiled=True)
            parts.append(jnp.transpose(full.reshape(4, -1, BLOCKS, WIDE), (2, 0, 1, 3)))
        else:
            wide = lax.all_gather(shard, "rows", axis=1, tiled=True)
            full = lax.all_gather(wide, "scene", axis=0, tiled=True)
            blocks = full.reshape(BLOCKS, full.shape[0] // BLOCKS, 4, -1)
            parts.append(jnp.transpose(blocks, (0, 2, 1, 3)))
    chunk = jnp.concatenate(parts, axis=2 if turned else 3)
    return chunk[:4], chunk[4:]


def scatter_plain(grad, turned):
    both = jnp.concatenate(grad, axis=0)
    if turned:
        full = jnp.transpose(both, (1, 2, 0, 3)).reshape(-1, D)
    else:
        full = jnp.transpose(both, (0, 2, 1, 3)).reshape(both.shape[0] * both.shape[2], -1)
    part = lax.psum_scatter(full, "scene", scatter_dimension=int(turned), tiled=True)
    return lax.psum_scatter(part, "rows", scatter_dimension=1 - turned, tiled=True).astype(F32)


def stack_kernel(*refs):
    own, x, y, *both, out_ref = refs
    for i, ref in enumerate((own, x, y)):
        out_ref[i] = ref[...]
    if len(both) == 1:
        out_ref[3] = both[0][...]
    else:
        early = pl.program_id(0) < 2
        for ref, now in zip(both, (early, jnp.logical_not(early))):

            @pl.when(now)
            def _(ref=ref):
                out_ref[3] = ref[...]


def stack(parts, both):
    both = both if isinstance(both, list) else [both]
    shape = parts[0].shape
    block = (1,) + shape[1:]
    places = [lambda i: (i, 0, 0)] * 4
    if len(both) == 2:
        places[3:] = [lambda i: (jnp.minimum(i, 1), 0, 0), lambda i: (jnp.maximum(i - 2, 0), 0, 0)]
    return pl.pallas_call(
        stack_kernel,
        grid=(4,),
        in_specs=[pl.BlockSpec(block, place) for place in places],
        out_specs=pl.BlockSpec((4,) + block, lambda i: (0, i, 0, 0)),
        out_shape=jax.ShapeDtypeStruct((4,) + shape, parts[0].dtype),
        compiler_params=params(VMEM),
        cost_estimate=pl.CostEstimate(
            flops=0, bytes_accessed=16 * parts[0].size, transcendentals=0
        ),
        name="stack",
    )(*parts, *both)


def together(*arrays):
    return lax.optimization_barrier(arrays)


def share_rows(x):
    return lax.all_to_all(x, "rows", 0, 0)


class Gather:
    def __init__(self, shard, order):
        self.shard = shard
        self.first, self.second = (XBIT, YBIT) if order == "xy" else (YBIT, XBIT)

    def rows(self):
        self.own = share_rows(jnp.broadcast_to(self.shard[None], (4,) + self.shard.shape))

    def near(self):
        self.one = swap(self.own, "scene", self.first)
        self.two = swap(self.own, "scene", self.second)

    def cross(self):
        self.both = swap(self.one, "scene", self.second)

    def cross_halves(self):
        self.both = [
            swap(self.one[:2], "scene", self.second),
            swap(self.two[2:], "scene", self.first),
        ]

    def get(self):
        x, y = (self.one, self.two) if self.first == XBIT else (self.two, self.one)
        half = stack([self.own, x, y], self.both)
        return half, swap(half, "scene", CORE)


class Scatter:
    def __init__(self, grad, streams):
        self.keep, send = grad
        self.streams = streams
        self.got = swap(send, "scene", CORE)

    def near(self):
        shape = (2, 2) + self.keep.shape[1:]
        keep, got = self.keep.reshape(shape), self.got.reshape(shape)
        count = 4 // len(self.streams)
        self.sums, self.away = [], []
        for i, order in enumerate(self.streams):
            zs = slice(i * count, (i + 1) * count)

            def part(place):
                pick = (slice(None), place, zs) if order == "xy" else (place, slice(None), zs)
                return keep[pick].astype(F32) + got[pick].astype(F32)

            self.sums.append(part(0))
            self.away.append(part(1).astype(BF16))

    def send(self, step):
        bits = {"xy": (XBIT, YBIT), "yx": (YBIT, XBIT)}
        self.moved = [
            swap(away, "scene", bits[order][step])
            for away, order in zip(self.away, self.streams)
        ]

    def cross(self):
        whole = [near + moved.astype(F32) for near, moved in zip(self.sums, self.moved)]
        self.sums = [part[0] for part in whole]
        self.away = [part[1].astype(BF16) for part in whole]

    def last(self):
        mine = [
            (near + moved.astype(F32)).astype(BF16) for near, moved in zip(self.sums, self.moved)
        ]
        self.away = [mine[0] if len(mine) == 1 else jnp.concatenate(mine, axis=0)]

    def rows(self):
        self.total = share_rows(self.away[0])

    def rows_apart(self):
        z = lax.axis_index("rows")
        block = lambda k: lax.dynamic_index_in_dim(self.away[0], z ^ k, 0, keepdims=False)
        self.total = jnp.stack([block(0)] + [swap(block(k), "rows", k) for k in (1, 2, 3)])

    def get(self):
        return jnp.sum(self.total.astype(F32), axis=0)


def settle(scatters, *arrays):
    flat = [a for t in scatters for a in t.away]
    out = list(together(*flat, *arrays))
    for t in scatters:
        t.away = [out.pop(0) for _ in t.away]
    return out[0] if len(out) == 1 else out


def weight_step(grad, factor, moment, master, average):
    clipped = grad * factor
    moment_new = MOMENTUM * moment + clipped
    weight_new = master - STEP_RATE * (clipped + MOMENTUM * moment_new)
    return moment_new, weight_new, AVERAGE_DECAY * average + (1.0 - AVERAGE_DECAY) * weight_new


def items_sent(x):
    scenes, rows = lax.axis_size("scene"), lax.axis_size("rows")
    z = lax.axis_index("rows")
    pairs = [[], []]
    for s in range(scenes):
        for b in range(rows):
            for turn in range(2):
                m = (b % 2) ^ turn
                to = ((s // 2) * 2 + b // 2) * rows + 2 * m + s % 2
                pairs[turn].append((s * rows + b, to))
    even = z % 2 == 0
    first = lax.ppermute(jnp.where(even, x[0], x[1]), ("scene", "rows"), pairs[0])
    second = lax.ppermute(jnp.where(even, x[1], x[0]), ("scene", "rows"), pairs[1])
    return first, second


def items_placed(parts):
    first, second = parts
    early = lax.axis_index("rows") // 2 == 0
    return jnp.stack([jnp.where(early, first, second), jnp.where(early, second, first)])


def body(patches, scene_length, target_views, gauss_index, raster_weight, target_color, *state):
    masters, moments, averages = state[:7], state[7:14], state[14:]
    vectors = masters[6]
    scene, row = lax.axis_index("scene"), lax.axis_index("rows")
    side = scene % 2
    item_m, item_s = row // 2, (scene // 2) * 2 + row % 2
    block_rows = patches.shape[2]
    tokens = 2 * block_rows
    length = scene_length[item_m, item_s]
    views = target_views[item_m, item_s].reshape(1)
    lens = jnp.stack([length - side * tokens, length - (1 - side) * tokens])
    pixel_count = jnp.sum(target_views).astype(F32) * (
        raster_weight.shape[-1] * lax.axis_size("rows")
    )
    natural = jnp.arange(BLOCKS, dtype=jnp.int32)
    plain = jnp.concatenate([natural, natural, natural[:4]])
    placed = lax.axis_size("scene") == BLOCKS and lax.axis_size("rows") == 4
    if placed:
        apart = jnp.bitwise_xor(natural, scene.astype(jnp.int32))
        at = jnp.bitwise_xor(jnp.asarray(PLACES), scene.astype(jnp.int32))
        spots = jnp.bitwise_and(apart, 1) * 4 + lax.shift_right_logical(apart, 1)
        perm = jnp.concatenate([at, spots, natural[:4]])
    else:
        perm = plain

    gains = [vectors[None, i * D : (i + 1) * D] for i in range(9)]
    bias_up = vectors[None, 9 * D : 9 * D + FF]
    bias_gauss = vectors[9 * D + FF :]

    low = [w.astype(BF16) for w in masters[:6]]
    low[5] = low[5].T
    x_in = patches[:, 0]
    drawn = jnp.concatenate(
        [gauss_index[:, 0].astype(F32), raster_weight[:, 0], target_color[:, 0]], axis=1
    )
    drawn = jnp.transpose(drawn, (0, 2, 1, 3))
    if placed:
        side_w = Gather(jnp.concatenate([low[0], low[5]], axis=0), "yx")
        first_w = Gather(low[1], "xy")
        second_w = Gather(jnp.concatenate([low[3], low[2]], axis=1), "yx")
        side_w.rows()
        side_w.own, first_w.shard = together(side_w.own, first_w.shard)
        first_w.rows()
        side_w.near()
        first_w.own, side_w.one, side_w.two, x_in = together(
            first_w.own, side_w.one, side_w.two, x_in
        )
        first_w.near()
        side_w.cross()
        x = items_sent(x_in)
        second_w.shard, *x = together(second_w.shard, *x)
        second_w.rows()
        first_w.one, first_w.two, side_w.both = together(
            first_w.one, first_w.two, side_w.both
        )
        first_w.cross()
        w_side = side_w.get()
        x = items_placed(x)
    else:
        w_side = gather_plain([low[0], low[5]], True)
        w_first = gather_plain([low[1]], False)
        w_second = gather_plain([low[3], low[2]], False)
        w_third = gather_plain([low[4]], False)
    if not placed:
        x = items_placed(items_sent(x_in))
    x = x.reshape(tokens, -1)
    h0, a1 = embed(perm, x, w_side, gains[6], gains[0], gains[3])
    if placed:
        second_w.own, a1, first_w.both, shard = together(second_w.own, a1, first_w.both, low[4])
        second_w.near()
        w_third = gather_whole(shard)
        w_first = first_w.get()
    p = joint(perm, a1, w_first)
    kv = swap(p[:, D:], "scene", 1)
    mixed, logs, flat = attend(perm, lens, p, kv)
    if placed:
        mixed, logs, second_w.one, second_w.two = together(
            mixed, logs, second_w.one, second_w.two
        )
        second_w.cross_halves()
        w_second = second_w.get()
    rd = items_sent(drawn)
    h1, a2 = project(perm, mixed, w_second, 4, h0, gains[7], gains[1], gains[4])
    u, act = up_project(plain, a2, w_second, bias_up)
    h2, a3 = project(perm, act, w_third, 0, h1, gains[8], gains[2], gains[5], WIDE_VMEM)
    zt = gauss(perm, a3, w_side, bias_gauss)
    zt, *rd = together(zt, *rd)
    rd = items_placed(rd)

    edge = swap(jnp.where(side == 0, zt[:, tokens - HT :], zt[:, :HT]), "scene", 1)
    before = jnp.where(side == 0, 0.0, edge)
    after = jnp.where(side == 0, edge, 0.0)
    zx = jnp.concatenate([before, after, jnp.zeros((POUT, 128 - 2 * HT), F32)], axis=1)
    dzt, dzx, loss = render(views, (1.0 / pixel_count).reshape(1), zt, zx, rd)
    back = swap(jnp.where(side == 0, dzx[:, HT : 2 * HT], dzx[:, :HT]), "scene", 1)
    dzt = jnp.concatenate(
        [
            dzt[:, :HT] + jnp.where(side == 0, 0.0, back),
            dzt[:, HT : tokens - HT],
            dzt[:, tokens - HT :] + jnp.where(side == 0, back, 0.0),
        ],
        axis=1,
    )
    d_bias_gauss = jnp.sum(dzt, axis=1)
    dz = dzt.astype(BF16)

    streams = ("xy", "yx")
    dw_gauss = side_grad(perm, dz, a3)
    if placed:
        sg = Scatter(dw_gauss, ("yx",))
        sg.keep, dz = together(sg.keep, dz)
    dh2, dh2_low, sums3 = norm_back(perm, dz, w_side, True, h2, gains[2], None, False)
    dw_down = weight_grad(plain, act, dh2_low, placed)
    d_low = dh2_low
    if placed:
        whole_down, d_low = together(dw_down[0], d_low)
        part_down = lax.psum_scatter(whole_down, "scene", scatter_dimension=0)
        sg.near()
        d_low = settle([sg], d_low)
        sg.send(0)
    du, d_bias_up = down_back(plain, d_low, w_third, u)
    if placed:
        du, *sg.moved = together(du, *sg.moved)
        sg.cross()
        du = settle([sg], du)
        sg.send(1)
    dw_up = weight_grad(perm, a2, du)
    if placed:
        su = Scatter(dw_up, streams)
        su.keep, du = together(su.keep, du)
    dh1, dh1_low, sums2 = norm_back(perm, du, w_second, False, h1, gains[1], dh2, False)
    if placed:
        dh1_low, su.got, *sg.moved = together(dh1_low, su.got, *sg.moved)
        su.near()
        sg.last()
        dh1_low = settle([su, sg], dh1_low)
        su.send(0)
        sg.rows()
    dw_out = weight_grad(perm, mixed, dh1_low)
    if placed:
        so = Scatter(dw_out, ("xy",))
        so.keep, dh1_low = together(so.keep, dh1_low)
    do = out_back(perm, dh1_low, w_second)
    dq, own, far = attend_back(perm, lens, p, kv, do, logs, flat)
    if placed:
        dq, own, far, so.got, sg.total, part_down, *su.moved = together(
            dq, own, far, so.got, sg.total, part_down, *su.moved
        )
        r_down = lax.psum_scatter(part_down, "rows", scatter_dimension=0)
    got = swap(far, "scene", 1)
    if placed:
        su.cross()
        so.near()
        got = settle([su, so], got)
        su.send(1)
        so.send(0)
    dkv = (own + got.astype(F32)).astype(BF16)
    dp = jnp.concatenate([dq, dkv[0], dkv[1]], axis=1)
    dw_joint = weight_grad(perm, a1, dp)
    if placed:
        sj = Scatter(dw_joint, streams)
        sj.keep, dp = together(sj.keep, dp)
    dh0_low, sums1 = norm_back(perm, dp, w_first, False, h0, gains[0], dh1, True)
    if placed:
        dh0_low, sj.got, *su.moved = together(dh0_low, sj.got, *su.moved)
        sj.near()
        su.last()
        dh0_low = settle([sj, su], dh0_low)
        sj.send(0)
        su.rows()
    dw_patch = side_grad(perm, x.T, dh0_low)
    if placed:
        sp = Scatter(dw_patch, ("yx",))
        sp.keep, r_down, *moved = together(sp.keep, r_down, *sj.moved, *so.moved)
        sj.moved, so.moved = moved[:2], moved[2:]
        r_down = r_down.astype(F32)
        so.cross()
        sj.cross()
        settle([sj, so])
        sj.send(1)
        so.send(1)
        sp.near()
        sp.send(0)
        sj.last()
        so.last()
        wide = sj.away[0].shape[-1]
        sj.away = [jnp.concatenate([sj.away[0], so.away[0]], axis=-1)]
        sj.rows()
        sj.total, so.total = sj.total[..., :wide], sj.total[..., wide:]
        sp.cross()
        sp.send(1)
        sp.last()
        sp.rows_apart()
        reduced = [t.get() for t in (sp, sj, so, su)] + [r_down, sg.get()]
    else:
        grads = [dw_patch, dw_joint, dw_out, dw_up, dw_down, dw_gauss]
        reduced = [scatter_plain(g, i in (0, 5)) for i, g in enumerate(grads)]
    reduced[5] = reduced[5].T
    vector_part = jnp.concatenate(
        [sums1[0], sums2[0], sums3[0], sums1[1], sums2[1], sums3[1], sums1[2], sums2[2], sums3[2]]
        + [d_bias_up[0], d_bias_gauss, loss[0]]
    )
    squares = sum(jnp.sum(item * item) for item in reduced)
    totals = total_sum(jnp.concatenate([vector_part, jnp.broadcast_to(squares, (128,))]).reshape(-1, 128))
    totals = totals.reshape(-1)
    vec = vectors.shape[0]
    vector_grad, loss_sum, square_sum = totals[:vec], totals[vec], totals[vec + 128]
    grad_norm = jnp.sqrt(square_sum + jnp.sum(vector_grad * vector_grad))
    factor = jnp.minimum(1.0, CLIP_NORM / (grad_norm + 1e-06))
    next_moments, next_weights, next_averages = ([], [], [])
    for grad, moment, master, average in zip(reduced + [vector_grad], moments, masters, averages):
        moment, weight, mean = weight_step(grad, factor, moment, master, average)
        next_moments.append(moment)
        next_weights.append(weight)
        next_averages.append(mean)
    return (loss_sum, pixel_count, grad_norm, *next_moments, *next_weights, *next_averages)


def solution(mesh):
    item = P(None, "scene", None, None, "rows")
    weight_specs = (P("rows", "scene"),) + (P("scene", "rows"),) * 5 + (P(),)
    in_specs = (P(None, "scene", "rows", None), P(), P(), item, item, item) + 3 * weight_specs
    out_specs = (P(), P(), P()) + 3 * weight_specs
    return jax.shard_map(body, mesh=mesh, in_specs=in_specs, out_specs=out_specs, check_vma=False)
```

```python
import functools

import jax
import jax.numpy as jnp
import numpy as np
from jax import lax
from jax.experimental import pallas as pl
from jax.experimental.pallas import tpu as pltpu
from jax.sharding import PartitionSpec as P

D = 1024
HEADS = 16
HD = 64
FF = 4096
POUT = 768
HT = 16
GV = 12
NG = POUT // GV

EPSILON = 1e-05
CLIP_NORM = 0.002
STEP_RATE = 1250.0
MOMENTUM = 0.9
AVERAGE_DECAY = 0.9

F32 = jnp.float32
BF16 = jnp.bfloat16
HIGHEST = lax.Precision.HIGHEST
BLOCKS = 8
WIDE = D // BLOCKS
VMEM_MB = 1024 * 1024
VMEM = 28
WIDE_VMEM = 56
TABLE = NG + 8


def nn(a, b):
    return lax.dot_general(a, b, (((1,), (0,)), ((), ())), preferred_element_type=F32)


def nt(a, b):
    return lax.dot_general(a, b, (((1,), (1,)), ((), ())), preferred_element_type=F32)


def tn(a, b):
    return lax.dot_general(a, b, (((0,), (0,)), ((), ())), preferred_element_type=F32)


def params(mb, n=1):
    return pltpu.CompilerParams(
        vmem_limit_bytes=mb * VMEM_MB, dimension_semantics=("arbitrary",) * n
    )


def lane_block(index, width):
    return pl.ds(pl.multiple_of(index * width, width), width)


PATCH = 144
GAUSS = POUT // 4


def side_rows(w_ref, place, first, count):
    return jnp.concatenate(
        [w_ref[j, place, first : first + count, :] for j in range(4)], axis=1
    )


def norm_store(perm, h_ref, g_ref, s_ref, a_ref, chunk):
    def step(i, carry):
        rows = pl.ds(pl.multiple_of(i * chunk, chunk), chunk)
        h = h_ref[rows, :]
        c = h - jnp.mean(h, axis=1, keepdims=True)
        var = jnp.mean(c * c, axis=1, keepdims=True)
        a = (c * lax.rsqrt(var + EPSILON) * g_ref[...] + s_ref[...]).astype(BF16)
        for b in range(BLOCKS):
            a_ref[rows, lane_block(perm[8 + b], WIDE)] = a[:, b * WIDE : (b + 1) * WIDE]
        return carry

    lax.fori_loop(0, h_ref.shape[0] // chunk, step, 0)


def rows_of(w_ref, z, width):
    block = w_ref[:, z]
    if block.shape[-1] != width:
        block = block[:, :, :width]
    return block.reshape(block.shape[0] * block.shape[1], width)


def embed_kernel(perm, x_ref, w0_ref, w1_ref, b_ref, g_ref, s_ref, h_ref, a_ref):
    x = x_ref[...]
    for i, w_ref in enumerate((w0_ref, w1_ref)):
        weight = jnp.concatenate(
            [side_rows(w_ref, perm[16 + z], 0, PATCH) for z in range(4)], axis=0
        )
        hr = nn(x, weight)
        for j in range(BLOCKS // 2):
            cols = lane_block(perm[i * BLOCKS // 2 + j], WIDE)
            h_ref[:, cols] = hr[:, j * WIDE : (j + 1) * WIDE] + b_ref[:, cols]
    norm_store(perm, h_ref, g_ref, s_ref, a_ref, 128)


def embed(perm, x, chunk, b, g, s):
    rows = x.shape[0]
    part = 256
    full = lambda shape: pl.BlockSpec(shape, lambda i, p: (0, 0))
    tile = lambda n: pl.BlockSpec((part, n), lambda i, p: (i, 0))
    weight = pl.BlockSpec((4, 4, PATCH + GAUSS, WIDE), lambda i, p: (0, 0, 0, 0))
    return pl.pallas_call(
        embed_kernel,
        grid_spec=pltpu.PrefetchScalarGridSpec(
            num_scalar_prefetch=1,
            grid=(rows // part,),
            in_specs=[tile(x.shape[1]), weight, weight]
            + [full((1, D))] * 3,
            out_specs=[tile(D), tile(D)],
        ),
        out_shape=[jax.ShapeDtypeStruct((rows, D), F32), jax.ShapeDtypeStruct((rows, D), BF16)],
        compiler_params=params(VMEM),
        cost_estimate=pl.CostEstimate(
            flops=2 * rows * D * 576, bytes_accessed=rows * D * 6 + 4 * D * 576, transcendentals=0
        ),
        name="embed_norm",
    )(perm, x, *chunk, b, g, s)


def first_of(chunk):
    return (0, 0) if chunk[0].shape[0] == 4 else (0, 1)


def project_kernel(perm, a_ref, w0_ref, w1_ref, r_ref, b_ref, g_ref, s_ref, h_ref, n_ref):
    z = pl.program_id(0)
    middle = a_ref.shape[1] // 2
    width = D // 4
    cols = lane_block(z, width)
    h_ref[:, cols] = (
        r_ref[...]
        + b_ref[...]
        + nn(a_ref[:, :middle], rows_of(w0_ref, 0, width))
        + nn(a_ref[:, middle:], rows_of(w1_ref, 0, width))
    )

    @pl.when(z == pl.num_programs(0) - 1)
    def _():
        norm_store(perm, h_ref, g_ref, s_ref, n_ref, 128)


def project(perm, a, chunk, at, res, b, g, s, grant=VMEM):
    rows, depth = a.shape
    width = D // 4
    full = lambda shape: pl.BlockSpec(shape, lambda z, p: (0, 0))
    weights = [
        pl.BlockSpec((4, 1, depth // 8, width), lambda z, p, i=i: (i, p[16 + z], 0, at))
        for i in first_of(chunk)
    ]
    return pl.pallas_call(
        project_kernel,
        grid_spec=pltpu.PrefetchScalarGridSpec(
            num_scalar_prefetch=1,
            grid=(4,),
            in_specs=[
                full((rows, depth)),
                *weights,
                pl.BlockSpec((rows, width), lambda z, p: (0, z)),
                pl.BlockSpec((1, width), lambda z, p: (0, z)),
                full((1, D)),
                full((1, D)),
            ],
            out_specs=[full((rows, D)), full((rows, D))],
        ),
        out_shape=[jax.ShapeDtypeStruct((rows, D), F32), jax.ShapeDtypeStruct((rows, D), BF16)],
        compiler_params=params(grant),
        cost_estimate=pl.CostEstimate(
            flops=2 * rows * D * depth,
            bytes_accessed=rows * D * 10 + 2 * D * depth + 2 * rows * depth,
            transcendentals=0,
        ),
        name="project_norm",
    )(perm, a, *chunk, res, b, g, s)


def halves(a_ref, w0_ref, w1_ref, width):
    middle = a_ref.shape[1] // 2
    return nn(a_ref[:, :middle], rows_of(w0_ref, 0, width)) + nn(
        a_ref[:, middle:], rows_of(w1_ref, 0, width)
    )


def joint_kernel(perm, a_ref, w0_ref, w1_ref, p_ref):
    p_ref[...] = halves(a_ref, w0_ref, w1_ref, p_ref.shape[1]).astype(BF16)


def joint(perm, a, chunk):
    rows = a.shape[0]
    part = 3 * D // 4
    weight = pl.BlockSpec((4, 1, WIDE, part), lambda z, p: (0, p[16 + z], 0, 0))
    return pl.pallas_call(
        joint_kernel,
        grid_spec=pltpu.PrefetchScalarGridSpec(
            num_scalar_prefetch=1,
            grid=(4,),
            in_specs=[pl.BlockSpec((rows, D), lambda z, p: (0, 0)), weight, weight],
            out_specs=pl.BlockSpec((rows, part), lambda z, p: (0, z)),
        ),
        out_shape=jax.ShapeDtypeStruct((rows, 3 * D), BF16),
        compiler_params=params(VMEM),
        cost_estimate=pl.CostEstimate(
            flops=6 * rows * D * D, bytes_accessed=rows * D * 8 + 6 * D * D, transcendentals=0
        ),
        name="joint",
    )(perm, a, *chunk)


def gauss_kernel(perm, a_ref, w0_ref, w1_ref, b_ref, z_ref):
    half = D // 2
    z_ref[...] = (
        nt(side_rows(w0_ref, 0, PATCH, GAUSS), a_ref[:, :half])
        + nt(side_rows(w1_ref, 0, PATCH, GAUSS), a_ref[:, half:])
        + b_ref[...]
    )


def gauss(perm, a, chunk, b):
    rows = a.shape[0]
    weight = pl.BlockSpec((4, 1, PATCH + GAUSS, WIDE), lambda z, p: (0, p[16 + z], 0, 0))
    return pl.pallas_call(
        gauss_kernel,
        grid_spec=pltpu.PrefetchScalarGridSpec(
            num_scalar_prefetch=1,
            grid=(4,),
            in_specs=[
                pl.BlockSpec((rows, D), lambda z, p: (0, 0)),
                weight,
                weight,
                pl.BlockSpec((GAUSS, 1), lambda z, p: (z, 0)),
            ],
            out_specs=pl.BlockSpec((GAUSS, rows), lambda z, p: (z, 0)),
        ),
        out_shape=jax.ShapeDtypeStruct((POUT, rows), F32),
        compiler_params=params(VMEM),
        cost_estimate=pl.CostEstimate(
            flops=2 * rows * D * POUT, bytes_accessed=rows * D * 5 + 2 * D * POUT, transcendentals=0
        ),
        name="gauss",
    )(perm, a, *chunk, b[:, None])


def out_back_kernel(perm, d_ref, w0_ref, w1_ref, o_ref):
    width = D // 4
    for i, w_ref in enumerate((w0_ref, w1_ref)):
        total = sum(
            nt(d_ref[:, z * width : (z + 1) * width], rows_of(w_ref, perm[16 + z], width))
            for z in range(4)
        )
        o_ref[:, i * D // 2 : (i + 1) * D // 2] = total.astype(BF16)


def out_back(perm, d, chunk):
    rows = d.shape[0]
    part = 256
    weight = pl.BlockSpec((4, 4, WIDE, D // 4), lambda i, p: (0, 0, 0, 4))
    tile = pl.BlockSpec((part, D), lambda i, p: (i, 0))
    return pl.pallas_call(
        out_back_kernel,
        grid_spec=pltpu.PrefetchScalarGridSpec(
            num_scalar_prefetch=1,
            grid=(rows // part,),
            in_specs=[tile, weight, weight],
            out_specs=tile,
        ),
        out_shape=jax.ShapeDtypeStruct((rows, D), BF16),
        compiler_params=params(VMEM),
        cost_estimate=pl.CostEstimate(
            flops=2 * rows * D * D, bytes_accessed=rows * D * 4 + 2 * D * D, transcendentals=0
        ),
        name="out_back",
    )(perm, d, *chunk)


def grad_kernel(perm, a_ref, d_ref, *refs):
    *outs, turned_ref = refs
    middle = a_ref.shape[1] // 2

    @pl.when(pl.program_id(0) == 0)
    def _():
        turned_ref[...] = a_ref[...].T

    for i in (1, 0):
        g = nn(turned_ref[i * middle : (i + 1) * middle, :], d_ref[...]).astype(BF16)
        g = g.reshape(4, 1, middle // 4, g.shape[1])
        if len(outs) == 2:
            outs[i][...] = g
        else:
            for j in range(4):
                outs[0][perm[4 * i + j]] = g[j]


def weight_grad(perm, a, d, whole=False):
    tokens, depth = a.shape
    n = d.shape[1] // 4
    right = pl.BlockSpec((tokens, n), lambda z, p: (0, z))
    count = 8 if whole else 4
    out = pl.BlockSpec((count, 1, depth // 8, n), lambda z, p: (0, p[16 + z], 0, 0))
    shape = jax.ShapeDtypeStruct((count, 4, depth // 8, n), BF16)
    return pl.pallas_call(
        grad_kernel,
        grid_spec=pltpu.PrefetchScalarGridSpec(
            num_scalar_prefetch=1,
            grid=(4,),
            in_specs=[pl.BlockSpec((tokens, depth), lambda z, p: (0, 0)), right],
            out_specs=[out] * (8 // count),
            scratch_shapes=[pltpu.VMEM((depth, tokens), BF16)],
        ),
        out_shape=[shape] * (8 // count),
        compiler_params=params(VMEM),
        cost_estimate=pl.CostEstimate(
            flops=8 * tokens * depth * n,
            bytes_accessed=2 * tokens * (depth + 4 * n) + 8 * depth * n,
            transcendentals=0,
        ),
        name="weight_grad",
    )(perm, a, d)


def side_grad_kernel(perm, d_ref, a_ref, *outs):
    g = nn(d_ref[...], a_ref[...]).astype(BF16)
    for j in range(BLOCKS):
        block = g[:, j * WIDE : (j + 1) * WIDE]
        if len(outs) == 2:
            outs[j // 4][j % 4, 0] = block
        else:
            outs[0][perm[j], 0] = block


def side_grad(perm, d, a, whole=False):
    tokens = a.shape[0]
    n = d.shape[0] // 4
    count = 8 if whole else 4
    out = pl.BlockSpec((count, 1, n, WIDE), lambda z, p: (0, p[16 + z], 0, 0))
    shape = jax.ShapeDtypeStruct((count, 4, n, WIDE), BF16)
    return pl.pallas_call(
        side_grad_kernel,
        grid_spec=pltpu.PrefetchScalarGridSpec(
            num_scalar_prefetch=1,
            grid=(4,),
            in_specs=[
                pl.BlockSpec((n, tokens), lambda z, p: (z, 0)),
                pl.BlockSpec((tokens, D), lambda z, p: (0, 0)),
            ],
            out_specs=[out] * (8 // count),
        ),
        out_shape=[shape] * (8 // count),
        compiler_params=params(VMEM),
        cost_estimate=pl.CostEstimate(
            flops=8 * tokens * D * n, bytes_accessed=2 * tokens * D + 16 * D * n, transcendentals=0
        ),
        name="side_grad",
    )(perm, d, a)


GELU_C = float(np.sqrt(2.0 / np.pi))


def up_kernel(perm, a_ref, w0_ref, w1_ref, b_ref, u_ref, g_ref):
    u = halves(a_ref, w0_ref, w1_ref, u_ref.shape[1]) + b_ref[...]
    u_ref[...] = u
    t = jnp.tanh(GELU_C * (u + 0.044715 * (u * u * u)))
    g_ref[...] = (u * (0.5 * (1.0 + t))).astype(BF16)


def up_project(perm, a, chunk, b):
    rows = a.shape[0]
    part = FF // BLOCKS
    weight = pl.BlockSpec((4, 1, WIDE, part), lambda n, p: (0, p[16 + n // 2], 0, n % 2))
    return pl.pallas_call(
        up_kernel,
        grid_spec=pltpu.PrefetchScalarGridSpec(
            num_scalar_prefetch=1,
            grid=(BLOCKS,),
            in_specs=[
                pl.BlockSpec((rows, D), lambda n, p: (0, 0)),
                weight,
                weight,
                pl.BlockSpec((1, part), lambda n, p: (0, n)),
            ],
            out_specs=[
                pl.BlockSpec((rows, part), lambda n, p: (0, n)),
                pl.BlockSpec((rows, part), lambda n, p: (0, p[8 + n])),
            ],
        ),
        out_shape=[jax.ShapeDtypeStruct((rows, FF), F32), jax.ShapeDtypeStruct((rows, FF), BF16)],
        compiler_params=params(WIDE_VMEM),
        cost_estimate=pl.CostEstimate(
            flops=2 * rows * D * FF, bytes_accessed=rows * FF * 6 + 2 * D * FF, transcendentals=rows * FF
        ),
        name="up_gelu",
    )(perm, a, *chunk, b)


def down_back_kernel(perm, d_ref, w0_ref, w1_ref, u_ref, du_ref, sum_ref, dg_ref):
    width = D // 4

    def product(w_ref):
        dg_ref[...] = sum(
            nt(d_ref[:, z * width : (z + 1) * width], rows_of(w_ref, perm[16 + z], width))
            for z in range(4)
        )

    first = pl.program_id(0) < pl.num_programs(0) // 2
    pl.when(first)(lambda: product(w0_ref))
    pl.when(jnp.logical_not(first))(lambda: product(w1_ref))
    dg = dg_ref[...]
    u = u_ref[...]
    u2 = u * u
    t = jnp.tanh(GELU_C * (u + 0.044715 * (u2 * u)))
    slope = 0.5 * (1.0 + t) + (0.5 * GELU_C) * u * (1.0 - t * t) * (1.0 + (3 * 0.044715) * u2)
    du = slope * dg
    du_ref[...] = du.astype(BF16)
    sum_ref[...] = jnp.sum(du, axis=0, keepdims=True)


def down_back(perm, d, chunk, u):
    rows = d.shape[0]
    second = 4 * first_of(chunk)[1]
    part = FF // BLOCKS
    return pl.pallas_call(
        down_back_kernel,
        grid_spec=pltpu.PrefetchScalarGridSpec(
            num_scalar_prefetch=1,
            grid=(BLOCKS,),
            in_specs=[
                pl.BlockSpec((rows, D), lambda j, p: (0, 0)),
                pl.BlockSpec((1, 4, part, D // 4), lambda j, p: (jnp.minimum(j, 3), 0, 0, 0)),
                pl.BlockSpec(
                    (1, 4, part, D // 4), lambda j, p: (jnp.maximum(j - 4, 0) + second, 0, 0, 0)
                ),
                pl.BlockSpec((rows, part), lambda j, p: (0, p[j])),
            ],
            out_specs=[
                pl.BlockSpec((rows, part), lambda j, p: (0, p[j])),
                pl.BlockSpec((1, part), lambda j, p: (0, p[j])),
            ],
            scratch_shapes=[pltpu.VMEM((rows, part), F32)],
        ),
        out_shape=[jax.ShapeDtypeStruct((rows, FF), BF16), jax.ShapeDtypeStruct((1, FF), F32)],
        compiler_params=params(WIDE_VMEM),
        cost_estimate=pl.CostEstimate(
            flops=2 * rows * D * FF, bytes_accessed=rows * FF * 6 + 2 * D * FF, transcendentals=rows * FF
        ),
        name="down_back_gelu",
    )(perm, d, *chunk, u)


def back_kernel(has_res, placed, turned, perm, *refs):
    if has_res:
        d_ref, w0_ref, w1_ref, h_ref, g_ref, r_ref, *outs = refs
    else:
        d_ref, w0_ref, w1_ref, h_ref, g_ref, *outs = refs
        r_ref = None
    if placed:
        low_ref, sums_ref, acc_ref, part_ref = outs
        dh_ref = None
    else:
        dh_ref, low_ref, sums_ref, acc_ref, part_ref = outs
    n = pl.program_id(0)

    if turned:
        d = d_ref[...].T
        for i, w_ref in enumerate((w0_ref, w1_ref)):
            weight = jnp.concatenate(
                [side_rows(w_ref, perm[16 + z], PATCH, GAUSS) for z in range(4)], axis=0
            )
            acc_ref[:, i * D // 2 : (i + 1) * D // 2] = nn(d, weight)
    else:
        d = d_ref[...]
        width = d.shape[1]

        @pl.when(n == 0)
        def _():
            acc_ref[:, : D // 2] = nt(d, rows_of(w0_ref, 0, width))
            acc_ref[:, D // 2 :] = nt(d, rows_of(w1_ref, 0, width))

        @pl.when(n > 0)
        def _():
            acc_ref[:, : D // 2] += nt(d, rows_of(w0_ref, 0, width))
            acc_ref[:, D // 2 :] += nt(d, rows_of(w1_ref, 0, width))

    @pl.when(n == pl.num_programs(0) - 1)
    def _():
        chunk = 128
        part_ref[...] = jnp.zeros_like(part_ref)

        def fold(x):
            return jnp.sum(x.reshape(chunk // 8, 8, D), axis=0)

        def step(i, carry):
            rows = pl.ds(pl.multiple_of(i * chunk, chunk), chunk)
            h = h_ref[rows, :]
            c = h - jnp.mean(h, axis=1, keepdims=True)
            var = jnp.mean(c * c, axis=1, keepdims=True)
            rstd = lax.rsqrt(var + EPSILON)
            xh = c * rstd
            da = jnp.concatenate(
                [acc_ref[rows, lane_block(perm[8 + b], WIDE)] for b in range(BLOCKS)], axis=1
            )
            dxh = da * xh
            part_ref[0] += fold(dxh)
            part_ref[1] += fold(da)
            dy = da * g_ref[...]
            first = jnp.mean(dy, axis=1, keepdims=True)
            second = jnp.mean(dy * xh, axis=1, keepdims=True)
            dh = rstd * (dy - first - xh * second)
            if has_res:
                dh = dh + r_ref[rows, :]
            part_ref[2] += fold(dh)
            low = dh.astype(BF16)
            if placed:
                for b in range(BLOCKS):
                    low_ref[rows, lane_block(perm[8 + b], WIDE)] = low[:, b * WIDE : (b + 1) * WIDE]
            else:
                dh_ref[rows, :] = dh
                low_ref[rows, :] = low
            return carry

        lax.fori_loop(0, h_ref.shape[0] // chunk, step, 0)
        sums_ref[...] = jnp.concatenate(
            [jnp.sum(part_ref[i], axis=0, keepdims=True) for i in range(3)]
            + [jnp.zeros((5, D), F32)],
            axis=0,
        )


def norm_back(perm, d, chunk, turned, h, g, res, placed):
    full = lambda shape: pl.BlockSpec(shape, lambda n, p: (0, 0))
    rows = h.shape[0]
    wide = d.size // rows
    if turned:
        left = full(d.shape)
        weight = pl.BlockSpec((4, 4, PATCH + GAUSS, WIDE), lambda n, p: (0, 0, 0, 0))
    else:
        part = wide // 4
        left = pl.BlockSpec((rows, part), lambda n, p: (0, n))
        weight = pl.BlockSpec((4, 1, WIDE, part), lambda n, p: (0, p[16 + n], 0, 0))
    args = [d, *chunk, h, g]
    specs = [left, weight, weight, full((rows, D)), full((1, D))]
    if res is not None:
        args.append(res)
        specs.append(full((rows, D)))
    out_specs = [full((rows, D)), full((8, D))]
    out_shape = [jax.ShapeDtypeStruct((rows, D), BF16), jax.ShapeDtypeStruct((8, D), F32)]
    if not placed:
        out_specs = [full((rows, D))] + out_specs
        out_shape = [jax.ShapeDtypeStruct((rows, D), F32)] + out_shape
    return pl.pallas_call(
        functools.partial(back_kernel, res is not None, placed, turned),
        grid_spec=pltpu.PrefetchScalarGridSpec(
            num_scalar_prefetch=1,
            grid=(1 if turned else 4,),
            in_specs=specs,
            out_specs=out_specs,
            scratch_shapes=[pltpu.VMEM((rows, D), F32), pltpu.VMEM((3, 8, D), F32)],
        ),
        out_shape=out_shape,
        compiler_params=params(WIDE_VMEM if placed else VMEM),
        cost_estimate=pl.CostEstimate(
            flops=2 * rows * D * wide,
            bytes_accessed=rows * D * 14 + 2 * D * wide + 2 * rows * wide,
            transcendentals=0,
        ),
        name="norm_back",
    )(perm, *args)


SCALE = HD ** (-0.5)
PAIR = 2 * HD
PAIRS = HEADS // 2


def lanes_of(side):
    lane = lax.broadcasted_iota(jnp.int32, (1, PAIR), 1)
    mine = (lane < HD) == (side == 0)
    return lane, mine, HD * (1 - side)


def masked_keys(keys, first, length, extra):
    lane, mine, free = first
    spot = lax.broadcasted_iota(jnp.int32, (keys.shape[0], 1), 0)
    hidden = jnp.where(spot < length, 0.0, -1e30).astype(BF16)
    rest = jnp.where(lane == free, hidden, 0.0).astype(BF16)
    if extra:
        ones = jnp.logical_and(lane > free, lane <= free + extra)
        rest = jnp.where(ones, 1.0, rest).astype(BF16)
    return jnp.where(mine, keys, rest)


def attend_kernel(perm, lens, q_ref, k0_ref, k1_ref, v0_ref, v1_ref, o_ref, l_ref, f_ref):
    v0, v1 = v0_ref[...], v1_ref[...]
    sides = [lanes_of(side) for side in range(2)]
    keys = [
        [masked_keys(ref[...], where, lens[j], 0) for j, ref in enumerate((k0_ref, k1_ref))]
        for where in sides
    ]
    chunk = 512
    for i in range(q_ref.shape[0] // chunk):
        rows = slice(i * chunk, (i + 1) * chunk)
        q = (q_ref[rows, :] * SCALE).astype(BF16)
        outs = []
        logs = []
        for (lane, mine, free), (k0, k1) in zip(sides, keys):
            qm = jnp.where(mine, q, jnp.where(lane == free, 1.0, 0.0).astype(BF16))
            s0 = nt(qm, k0)
            s1 = nt(qm, k1)
            top = jnp.max(jnp.maximum(s0, s1), axis=1, keepdims=True)
            e0 = jnp.exp(s0 - top)
            e1 = jnp.exp(s1 - top)
            total = jnp.sum(e0 + e1, axis=1, keepdims=True)
            outs.append((nn(e0.astype(BF16), v0) + nn(e1.astype(BF16), v1)) * (1.0 / total))
            logs.append(top + jnp.log(total))
        lane = sides[0][0]
        mixed = jnp.where(lane < HD, outs[0], outs[1])
        o_ref[rows, :] = mixed.astype(BF16)
        f_ref[rows, :] = mixed
        l_ref[rows, :] = jnp.where(lane < HD, logs[1], logs[0])


def attend(perm, lens, p, kv):
    rows = p.shape[0]
    block = lambda first: pl.BlockSpec((rows, PAIR), lambda h, m, n: (0, first + h))
    return pl.pallas_call(
        attend_kernel,
        grid_spec=pltpu.PrefetchScalarGridSpec(
            num_scalar_prefetch=2,
            grid=(PAIRS,),
            in_specs=[block(0), block(PAIRS), block(0), block(2 * PAIRS), block(PAIRS)],
            out_specs=[
                pl.BlockSpec((rows, PAIR), lambda h, m, n: (0, m[8 + h])),
                block(0),
                block(0),
            ],
        ),
        out_shape=[
            jax.ShapeDtypeStruct((rows, D), BF16),
            jax.ShapeDtypeStruct((rows, D), F32),
            jax.ShapeDtypeStruct((rows, D), F32),
        ],
        compiler_params=params(VMEM),
        cost_estimate=pl.CostEstimate(
            flops=8 * rows * rows * D,
            bytes_accessed=12 * rows * D,
            transcendentals=2 * rows * rows * HEADS,
        ),
        name="attend",
    )(perm, lens, p, p, kv, p, kv)


def attend_back_kernel(
    perm, lens, q_ref, k0_ref, k1_ref, v0_ref, v1_ref, do_ref, l_ref, f_ref, dq_ref, own_ref, far_ref
):
    values = []
    for side in range(2):
        lane, mine, free = lanes_of(side)
        ones = jnp.logical_and(lane >= free, lane < free + 3)
        rest = jnp.where(ones, 1.0, 0.0).astype(BF16)
        values.append([jnp.where(mine, ref[...], rest) for ref in (v0_ref, v1_ref)])
    q_all, do_all = q_ref[...], do_ref[...]
    sides = [lanes_of(side) for side in range(2)]
    keys = [
        [masked_keys(ref[...], where, lens[j], 3) for j, ref in enumerate((k0_ref, k1_ref))]
        for where in sides
    ]
    turned = [[k.T for k in pair] for pair in keys]
    chunk = 256
    dk = [None, None]
    dv = [None, None]
    for i in range(q_ref.shape[0] // chunk):
        rows = slice(i * chunk, (i + 1) * chunk)

        def thirds(x):
            first = x.astype(BF16)
            left = x - first.astype(F32)
            second = left.astype(BF16)
            return first, second, (left - second.astype(F32)).astype(BF16)

        logs = thirds(l_ref[rows, :])
        flow = do_all[rows, :].astype(F32) * f_ref[rows, :]
        dqs = []
        for (lane, mine, free), (k0, k1), vs, across in zip(sides, keys, values, turned):
            qm = jnp.where(mine, q_all[rows, :], 0.0).astype(BF16)
            dom = jnp.where(mine, do_all[rows, :], 0.0).astype(BF16)
            rest = jnp.where(lane == free, 1.0, 0.0).astype(BF16)
            for at, part in enumerate(logs):
                rest = jnp.where(lane == free + 1 + at, -part, rest)
            qs = jnp.where(mine, (q_all[rows, :] * SCALE).astype(BF16), rest)
            probs = [jnp.exp(nt(k, qs)) for k in (k0, k1)]
            delta = jnp.sum(jnp.where(mine, flow, 0.0), axis=1, keepdims=True)
            less = dom
            for at, part in enumerate(thirds(delta)):
                less = jnp.where(lane == free + at, -part, less)
            da = [nt(v, less) for v in vs]
            dq = None
            for j in range(2):
                ds = (probs[j] * da[j]).astype(BF16)
                term = nn(across[j], ds)
                dq = term if dq is None else dq + term
                term = nn(ds, qm)
                dk[j] = term if dk[j] is None else dk[j] + term
                term = nn(probs[j].astype(BF16), dom)
                dv[j] = term if dv[j] is None else dv[j] + term
            dqs.append(dq)
        dq = jnp.concatenate([dqs[0][:HD], dqs[1][HD:]], axis=0) * SCALE
        dq_ref[rows, :] = dq.T.astype(BF16)
    own_ref[0] = dk[0] * SCALE
    own_ref[1] = dv[0]
    far_ref[0] = (dk[1] * SCALE).astype(BF16)
    far_ref[1] = dv[1].astype(BF16)


def attend_back(perm, lens, p, kv, do, logs, flat):
    rows = p.shape[0]
    block = lambda first: pl.BlockSpec((rows, PAIR), lambda h, m, n: (0, first + h))
    both = pl.BlockSpec((2, rows, PAIR), lambda h, m, n: (0, 0, h))
    return pl.pallas_call(
        attend_back_kernel,
        grid_spec=pltpu.PrefetchScalarGridSpec(
            num_scalar_prefetch=2,
            grid=(PAIRS,),
            in_specs=[
                block(0),
                block(PAIRS),
                block(0),
                block(2 * PAIRS),
                block(PAIRS),
                pl.BlockSpec((rows, PAIR), lambda h, m, n: (0, m[8 + h])),
                block(0),
                block(0),
            ],
            out_specs=[block(0), both, both],
        ),
        out_shape=[
            jax.ShapeDtypeStruct((rows, D), BF16),
            jax.ShapeDtypeStruct((2, rows, D), F32),
            jax.ShapeDtypeStruct((2, rows, D), BF16),
        ],
        compiler_params=params(VMEM),
        cost_estimate=pl.CostEstimate(
            flops=20 * rows * rows * D,
            bytes_accessed=28 * rows * D,
            transcendentals=2 * rows * rows * HEADS,
        ),
        name="attend_back",
    )(perm, lens, p, p, kv, p, kv, do, logs, flat)


def iota(shape, dim):
    return lax.broadcasted_iota(jnp.int32, shape, dim)


def render_kernel(
    views_ref, inv_ref, z_ref, zx_ref, rd_ref, mc_ref, dz_ref, dzx_ref, loss_ref,
    tf_ref, both_ref, o_ref, wm_ref, a_ref, dt_ref, tok_ref, edge_ref, zs_ref,
):
    width = 256
    pixels = rd_ref.shape[-1]
    kg = 8

    lanes = 128
    parts = z_ref.shape[1] // lanes
    for i in range(parts):
        zs_ref[i] = z_ref[:, i * lanes : (i + 1) * lanes]
    zs_ref[parts] = zx_ref[...]

    def values(i):
        return [zs_ref[i, pl.ds(v, NG, stride=GV), :] for v in range(GV)]

    def shade(z):
        colour = [jax.nn.sigmoid(z[i]) for i in range(3)]
        gate = jax.nn.sigmoid(z[3])
        square = z[4] * z[4]
        for i in range(5, GV):
            square = square + z[i] * z[i]
        opacity = gate * jnp.exp(-0.5 * (square / (GV - 4)))
        return colour, gate, opacity

    own_group = iota((NG, width), 0) % 16 == iota((NG, width), 1) // 16

    def spread(base):
        return (iota((128, width), 0) == base + iota((128, width), 1) % 16).astype(F32)

    def rim_rows(table, base):
        wide = lax.dot_general(
            table, spread(base), (((1,), (0,)), ((), ())), precision=HIGHEST,
            preferred_element_type=F32,
        )
        return jnp.sum(jnp.where(own_group, wide, 0.0).reshape(4, 16, width), axis=1)

    def rim_back(rows, base):
        wide = jnp.concatenate(
            [jnp.broadcast_to(rows[j : j + 1, :], (16, width)) for j in range(4)], axis=0
        )
        return lax.dot_general(
            jnp.where(own_group, wide, 0.0), spread(base), (((1,), (1,)), ((), ())),
            precision=HIGHEST, preferred_element_type=F32,
        )

    def place(i):
        if i == parts:
            return edge_ref, slice(0, lanes)
        return tok_ref, slice(i * lanes, (i + 1) * lanes)

    for i in range(parts + 1):
        out_ref, cols = place(i)
        colour, gate, opacity = shade(values(i))
        for ch in range(3):
            out_ref[ch * NG : (ch + 1) * NG, cols] = colour[ch] * opacity
        out_ref[3 * NG : 4 * NG, cols] = opacity

    for ch in range(4):
        rows = slice(ch * NG, (ch + 1) * NG)
        at = ch * TABLE
        tf_ref[0, at : at + NG, :] = tok_ref[rows, 0:width]
        tf_ref[1, at : at + NG, :] = tok_ref[rows, width : 2 * width]
        tf_ref[0, at + NG : at + NG + 4, :] = rim_rows(edge_ref[rows, :], 0)
        tf_ref[0, at + NG + 4 : at + NG + 8, :] = rim_rows(tok_ref[rows, width : width + 128], 0)
        tf_ref[1, at + NG : at + NG + 4, :] = rim_rows(tok_ref[rows, width - 128 : width], 112)
        tf_ref[1, at + NG + 4 : at + NG + 8, :] = rim_rows(edge_ref[rows, :], 16)
    for block in range(2):
        table = tf_ref[block]
        high = table.astype(BF16)
        both_ref[block, : 4 * TABLE] = high
        both_ref[block, 4 * TABLE :] = (table - high.astype(F32)).astype(BF16)
    dt_ref[...] = jnp.zeros_like(dt_ref)
    inverse = inv_ref[0]
    row_hi = iota((width, pixels), 0).astype(F32).astype(BF16)
    row_lo = iota((TABLE, pixels), 0)
    one_low, zero_low = jnp.ones((), BF16), jnp.zeros((), BF16)

    def features(c):
        return jnp.tanh(mc_ref[0] * c[0] + mc_ref[1] * c[1] + mc_ref[2] * c[2])

    def view(t, loss):
        for block in range(2):
            r = rd_ref[block, t, 0:kg, :].astype(jnp.int32)
            weight = rd_ref[block, t, kg : 2 * kg, :]
            token = lax.shift_right_logical(r, 6)
            g = jnp.bitwise_and(r, NG - 1)
            after = token >= HT + width
            inside = jnp.logical_and(token >= HT, jnp.logical_not(after))
            rim = jnp.where(after, token - (HT + width), token)
            high = jnp.where(inside, token - HT, jnp.bitwise_and(g, 15) * 16 + rim)
            low = jnp.where(
                inside, g, NG + lax.shift_right_logical(g, 4) + jnp.where(after, 4, 0)
            )
            sums = [jnp.zeros((8, pixels), F32) for _ in range(4)]
            high = high.astype(F32).astype(BF16)
            table = both_ref[block]
            for k in range(kg):
                cols = slice(k * pixels, (k + 1) * pixels)
                one = jnp.where(row_hi == high[k : k + 1, :], one_low, zero_low)
                o_ref[block, :, cols] = one
                wm = jnp.where(row_lo == low[k : k + 1, :], weight[k : k + 1, :], 0.0)
                wm_ref[block, :, cols] = wm
                picked = nn(table, one)
                picked = picked[: 4 * TABLE] + picked[4 * TABLE :]
                for ch in range(4):
                    part = picked[ch * TABLE : (ch + 1) * TABLE, :] * wm
                    sums[ch] = sums[ch] + jnp.sum(part.reshape(TABLE // 8, 8, pixels), axis=0)
            sums = [jnp.sum(s, axis=0, keepdims=True) for s in sums]
            scale = 1.0 / (1.0 + sums[3])
            seen = [sums[i] * scale for i in range(3)]
            goal = [rd_ref[block, t, 2 * kg + i : 2 * kg + i + 1, :] for i in range(3)]
            f_seen = features(seen)
            gap = f_seen - features(goal)
            diff = [seen[i] - goal[i] for i in range(3)]
            loss = loss + diff[0] * diff[0] + diff[1] * diff[1] + diff[2] * diff[2]
            loss = loss + 0.5 * jnp.sum(gap * gap, axis=0, keepdims=True)
            pull = gap * (1.0 - f_seen * f_seen)
            d_seen = [
                inverse * (2.0 * diff[i] + jnp.sum(pull * mc_ref[i], axis=0, keepdims=True))
                for i in range(3)
            ]
            d_sum = [d * scale for d in d_seen]
            d_sum.append(
                -(d_seen[0] * seen[0] + d_seen[1] * seen[1] + d_seen[2] * seen[2]) * scale
            )
            for k in range(kg):
                cols = slice(k * pixels, (k + 1) * pixels)
                wm = wm_ref[block, :, cols]
                full = jnp.concatenate([wm * d_sum[ch] for ch in range(4)], axis=0)
                a_ref[block, :, cols] = full.astype(BF16)
            dt_ref[block] += nt(a_ref[block], o_ref[block])
        return loss

    loss = lax.fori_loop(0, views_ref[0], view, jnp.zeros((1, pixels), F32))
    loss_ref[...] = jnp.broadcast_to(jnp.sum(loss, axis=1, keepdims=True), loss_ref.shape)

    for ch in range(4):
        rows = slice(ch * NG, (ch + 1) * NG)
        at = ch * TABLE + NG
        tok_ref[rows, 0:width] = dt_ref[0, at - NG : at, :]
        tok_ref[rows, width : 2 * width] = dt_ref[1, at - NG : at, :]
        tok_ref[rows, width : width + 128] += rim_back(dt_ref[0, at + 4 : at + 8, :], 0)
        tok_ref[rows, width - 128 : width] += rim_back(dt_ref[1, at : at + 4, :], 112)
        edge_ref[rows, :] = rim_back(dt_ref[0, at : at + 4, :], 0) + rim_back(
            dt_ref[1, at + 4 : at + 8, :], 16
        )

    for part in range(parts + 1):
        grad_ref, cols = place(part)
        z = values(part)
        colour, gate, opacity = shade(z)
        d = [grad_ref[i * NG : (i + 1) * NG, cols] for i in range(4)]
        d_opacity = d[3]
        for i in range(3):
            d_opacity = d_opacity + d[i] * colour[i]
            zs_ref[part, pl.ds(i, NG, stride=GV), :] = d[i] * opacity * colour[i] * (1.0 - colour[i])
        both = d_opacity * opacity
        zs_ref[part, pl.ds(3, NG, stride=GV), :] = both * (1.0 - gate)
        for i in range(4, GV):
            zs_ref[part, pl.ds(i, NG, stride=GV), :] = both * z[i] * (-1.0 / (GV - 4))
    for i in range(parts):
        dz_ref[:, i * lanes : (i + 1) * lanes] = zs_ref[i]
    dzx_ref[...] = zs_ref[parts]


def render(views, inverse, zt, zx, rd):
    tokens = zt.shape[1]
    pixels = rd.shape[-1]
    slots = 8 * pixels
    counter = np.arange(48, dtype=np.float32).reshape(16, 3)
    mix = (np.float32(0.8) * np.cos(np.float32(1.7) * counter + np.float32(0.3))).astype(np.float32)
    mix = jnp.broadcast_to(jnp.asarray(mix.T)[:, :, None], (3, 16, pixels))
    whole = lambda x: pl.BlockSpec(x.shape, lambda: (0,) * x.ndim)
    smem = pl.BlockSpec(memory_space=pltpu.SMEM)
    shape = jax.ShapeDtypeStruct
    return pl.pallas_call(
        render_kernel,
        in_specs=[smem, smem, whole(zt), whole(zx), whole(rd), whole(mix)],
        out_specs=[whole(zt), whole(zx), pl.BlockSpec((8, 128), lambda: (0, 0))],
        out_shape=[shape(zt.shape, F32), shape(zx.shape, F32), shape((8, 128), F32)],
        scratch_shapes=[
            pltpu.VMEM((2, 4 * TABLE, 256), F32),
            pltpu.VMEM((2, 8 * TABLE, 256), BF16),
            pltpu.VMEM((2, 256, slots), BF16),
            pltpu.VMEM((2, TABLE, slots), F32),
            pltpu.VMEM((2, 4 * TABLE, slots), BF16),
            pltpu.VMEM((2, 4 * TABLE, 256), F32),
            pltpu.VMEM((4 * NG, tokens), F32),
            pltpu.VMEM((4 * NG, 128), F32),
            pltpu.VMEM((tokens // 128 + 1, POUT, 128), F32),
        ],
        compiler_params=pltpu.CompilerParams(vmem_limit_bytes=VMEM * VMEM_MB),
        cost_estimate=pl.CostEstimate(
            flops=24 * slots * 4 * TABLE * 256 * 6, bytes_accessed=4 * 1024 * 1024, transcendentals=0
        ),
        name="render",
    )(views, inverse, zt, zx, rd, mix)


def flip_pairs(n, bit):
    return [(i, i ^ bit) for i in range(n)]


def swap(x, axis, bit):
    return lax.ppermute(x, axis, flip_pairs(lax.axis_size(axis), bit))


CORE, XBIT, YBIT = 1, 2, 4
PLACES = np.array([0, 2, 4, 6, 1, 3, 5, 7], np.int32)


def total_sum(x):
    if lax.axis_size("scene") == BLOCKS and lax.axis_size("rows") == 4:
        x = x + swap(x, "scene", CORE)
        near, far, both = (swap(x, "scene", bit) for bit in (XBIT, YBIT, XBIT | YBIT))
        x = (x + near) + (far + both)
        near, far, both = (swap(x, "rows", bit) for bit in (1, 2, 3))
        return (x + near) + (far + both)
    for axis in ("scene", "rows"):
        bit = 1
        while bit < lax.axis_size(axis):
            x = x + swap(x, axis, bit)
            bit = 2 * bit
    return x


def gather_whole(shard):
    whole = lax.all_gather(shard, ("scene", "rows"), axis=0)
    return (whole.reshape((BLOCKS, 4) + shard.shape),) * 2


def gather_plain(shards, turned):
    parts = []
    for shard in shards:
        if turned:
            wide = lax.all_gather(shard, "rows", axis=0, tiled=True)
            full = lax.all_gather(wide, "scene", axis=1, tiled=True)
            parts.append(jnp.transpose(full.reshape(4, -1, BLOCKS, WIDE), (2, 0, 1, 3)))
        else:
            wide = lax.all_gather(shard, "rows", axis=1, tiled=True)
            full = lax.all_gather(wide, "scene", axis=0, tiled=True)
            blocks = full.reshape(BLOCKS, full.shape[0] // BLOCKS, 4, -1)
            parts.append(jnp.transpose(blocks, (0, 2, 1, 3)))
    chunk = jnp.concatenate(parts, axis=2 if turned else 3)
    return chunk[:4], chunk[4:]


def scatter_plain(grad, turned):
    both = jnp.concatenate(grad, axis=0)
    if turned:
        full = jnp.transpose(both, (1, 2, 0, 3)).reshape(-1, D)
    else:
        full = jnp.transpose(both, (0, 2, 1, 3)).reshape(both.shape[0] * both.shape[2], -1)
    part = lax.psum_scatter(full, "scene", scatter_dimension=int(turned), tiled=True)
    return lax.psum_scatter(part, "rows", scatter_dimension=1 - turned, tiled=True).astype(F32)


def stack_kernel(*refs):
    own, x, y, *both, out_ref = refs
    for i, ref in enumerate((own, x, y)):
        out_ref[i] = ref[...]
    if len(both) == 1:
        out_ref[3] = both[0][...]
    else:
        early = pl.program_id(0) < 2
        for ref, now in zip(both, (early, jnp.logical_not(early))):

            @pl.when(now)
            def _(ref=ref):
                out_ref[3] = ref[...]


def stack(parts, both):
    both = both if isinstance(both, list) else [both]
    shape = parts[0].shape
    block = (1,) + shape[1:]
    places = [lambda i: (i, 0, 0)] * 4
    if len(both) == 2:
        places[3:] = [lambda i: (jnp.minimum(i, 1), 0, 0), lambda i: (jnp.maximum(i - 2, 0), 0, 0)]
    return pl.pallas_call(
        stack_kernel,
        grid=(4,),
        in_specs=[pl.BlockSpec(block, place) for place in places],
        out_specs=pl.BlockSpec((4,) + block, lambda i: (0, i, 0, 0)),
        out_shape=jax.ShapeDtypeStruct((4,) + shape, parts[0].dtype),
        compiler_params=params(VMEM),
        cost_estimate=pl.CostEstimate(
            flops=0, bytes_accessed=16 * parts[0].size, transcendentals=0
        ),
        name="stack",
    )(*parts, *both)


def together(*arrays):
    return lax.optimization_barrier(arrays)


def share_rows(x):
    return lax.all_to_all(x, "rows", 0, 0)


class Gather:
    def __init__(self, shard, order):
        self.shard = shard
        self.first, self.second = (XBIT, YBIT) if order == "xy" else (YBIT, XBIT)

    def rows(self):
        self.own = share_rows(jnp.broadcast_to(self.shard[None], (4,) + self.shard.shape))

    def near(self):
        self.one = swap(self.own, "scene", self.first)
        self.two = swap(self.own, "scene", self.second)

    def cross(self):
        self.both = swap(self.one, "scene", self.second)

    def cross_halves(self):
        self.both = [
            swap(self.one[:2], "scene", self.second),
            swap(self.two[2:], "scene", self.first),
        ]

    def get(self):
        x, y = (self.one, self.two) if self.first == XBIT else (self.two, self.one)
        half = stack([self.own, x, y], self.both)
        return half, swap(half, "scene", CORE)


class Scatter:
    def __init__(self, grad, streams):
        self.keep, send = grad
        self.streams = streams
        self.got = swap(send, "scene", CORE)

    def near(self):
        shape = (2, 2) + self.keep.shape[1:]
        keep, got = self.keep.reshape(shape), self.got.reshape(shape)
        count = 4 // len(self.streams)
        self.sums, self.away = [], []
        for i, order in enumerate(self.streams):
            zs = slice(i * count, (i + 1) * count)

            def part(place):
                pick = (slice(None), place, zs) if order == "xy" else (place, slice(None), zs)
                return keep[pick].astype(F32) + got[pick].astype(F32)

            self.sums.append(part(0))
            self.away.append(part(1).astype(BF16))

    def send(self, step):
        bits = {"xy": (XBIT, YBIT), "yx": (YBIT, XBIT)}
        self.moved = [
            swap(away, "scene", bits[order][step])
            for away, order in zip(self.away, self.streams)
        ]

    def cross(self):
        whole = [near + moved.astype(F32) for near, moved in zip(self.sums, self.moved)]
        self.sums = [part[0] for part in whole]
        self.away = [part[1].astype(BF16) for part in whole]

    def last(self):
        mine = [
            (near + moved.astype(F32)).astype(BF16) for near, moved in zip(self.sums, self.moved)
        ]
        self.away = [mine[0] if len(mine) == 1 else jnp.concatenate(mine, axis=0)]

    def rows(self):
        self.total = share_rows(self.away[0])

    def rows_apart(self):
        z = lax.axis_index("rows")
        block = lambda k: lax.dynamic_index_in_dim(self.away[0], z ^ k, 0, keepdims=False)
        self.total = jnp.stack([block(0)] + [swap(block(k), "rows", k) for k in (1, 2, 3)])

    def get(self):
        return jnp.sum(self.total.astype(F32), axis=0)


def settle(scatters, *arrays):
    flat = [a for t in scatters for a in t.away]
    out = list(together(*flat, *arrays))
    for t in scatters:
        t.away = [out.pop(0) for _ in t.away]
    return out[0] if len(out) == 1 else out


def weight_step(grad, factor, moment, master, average):
    clipped = grad * factor
    moment_new = MOMENTUM * moment + clipped
    weight_new = master - STEP_RATE * (clipped + MOMENTUM * moment_new)
    return moment_new, weight_new, AVERAGE_DECAY * average + (1.0 - AVERAGE_DECAY) * weight_new


def items_sent(x):
    scenes, rows = lax.axis_size("scene"), lax.axis_size("rows")
    z = lax.axis_index("rows")
    pairs = [[], []]
    for s in range(scenes):
        for b in range(rows):
            for turn in range(2):
                m = (b % 2) ^ turn
                to = ((s // 2) * 2 + b // 2) * rows + 2 * m + s % 2
                pairs[turn].append((s * rows + b, to))
    even = z % 2 == 0
    first = lax.ppermute(jnp.where(even, x[0], x[1]), ("scene", "rows"), pairs[0])
    second = lax.ppermute(jnp.where(even, x[1], x[0]), ("scene", "rows"), pairs[1])
    return first, second


def items_placed(parts):
    first, second = parts
    early = lax.axis_index("rows") // 2 == 0
    return jnp.stack([jnp.where(early, first, second), jnp.where(early, second, first)])


def body(patches, scene_length, target_views, gauss_index, raster_weight, target_color, *state):
    masters, moments, averages = state[:7], state[7:14], state[14:]
    vectors = masters[6]
    scene, row = lax.axis_index("scene"), lax.axis_index("rows")
    side = scene % 2
    item_m, item_s = row // 2, (scene // 2) * 2 + row % 2
    block_rows = patches.shape[2]
    tokens = 2 * block_rows
    length = scene_length[item_m, item_s]
    views = target_views[item_m, item_s].reshape(1)
    lens = jnp.stack([length - side * tokens, length - (1 - side) * tokens])
    pixel_count = jnp.sum(target_views).astype(F32) * (
        raster_weight.shape[-1] * lax.axis_size("rows")
    )
    natural = jnp.arange(BLOCKS, dtype=jnp.int32)
    plain = jnp.concatenate([natural, natural, natural[:4]])
    placed = lax.axis_size("scene") == BLOCKS and lax.axis_size("rows") == 4
    if placed:
        apart = jnp.bitwise_xor(natural, scene.astype(jnp.int32))
        at = jnp.bitwise_xor(jnp.asarray(PLACES), scene.astype(jnp.int32))
        spots = jnp.bitwise_and(apart, 1) * 4 + lax.shift_right_logical(apart, 1)
        perm = jnp.concatenate([at, spots, natural[:4]])
    else:
        perm = plain

    gains = [vectors[None, i * D : (i + 1) * D] for i in range(9)]
    bias_up = vectors[None, 9 * D : 9 * D + FF]
    bias_gauss = vectors[9 * D + FF :]

    low = [w.astype(BF16) for w in masters[:6]]
    low[5] = low[5].T
    x_in = patches[:, 0]
    drawn = jnp.concatenate(
        [gauss_index[:, 0].astype(F32), raster_weight[:, 0], target_color[:, 0]], axis=1
    )
    drawn = jnp.transpose(drawn, (0, 2, 1, 3))
    if placed:
        side_w = Gather(jnp.concatenate([low[0], low[5]], axis=0), "yx")
        first_w = Gather(low[1], "xy")
        second_w = Gather(jnp.concatenate([low[3], low[2]], axis=1), "yx")
        side_w.rows()
        side_w.own, first_w.shard = together(side_w.own, first_w.shard)
        first_w.rows()
        side_w.near()
        first_w.own, side_w.one, side_w.two, x_in = together(
            first_w.own, side_w.one, side_w.two, x_in
        )
        first_w.near()
        side_w.cross()
        x = items_sent(x_in)
        second_w.shard, *x = together(second_w.shard, *x)
        second_w.rows()
        first_w.one, first_w.two, side_w.both = together(
            first_w.one, first_w.two, side_w.both
        )
        first_w.cross()
        w_side = side_w.get()
        x = items_placed(x)
    else:
        w_side = gather_plain([low[0], low[5]], True)
        w_first = gather_plain([low[1]], False)
        w_second = gather_plain([low[3], low[2]], False)
        w_third = gather_plain([low[4]], False)
    if not placed:
        x = items_placed(items_sent(x_in))
    x = x.reshape(tokens, -1)
    h0, a1 = embed(perm, x, w_side, gains[6], gains[0], gains[3])
    if placed:
        second_w.own, a1, first_w.both, shard = together(second_w.own, a1, first_w.both, low[4])
        second_w.near()
        w_third = gather_whole(shard)
        w_first = first_w.get()
    p = joint(perm, a1, w_first)
    kv = swap(p[:, D:], "scene", 1)
    mixed, logs, flat = attend(perm, lens, p, kv)
    if placed:
        mixed, logs, second_w.one, second_w.two = together(
            mixed, logs, second_w.one, second_w.two
        )
        second_w.cross_halves()
        w_second = second_w.get()
    rd = items_sent(drawn)
    h1, a2 = project(perm, mixed, w_second, 4, h0, gains[7], gains[1], gains[4])
    u, act = up_project(plain, a2, w_second, bias_up)
    h2, a3 = project(perm, act, w_third, 0, h1, gains[8], gains[2], gains[5], WIDE_VMEM)
    zt = gauss(perm, a3, w_side, bias_gauss)
    zt, *rd = together(zt, *rd)
    rd = items_placed(rd)

    edge = swap(jnp.where(side == 0, zt[:, tokens - HT :], zt[:, :HT]), "scene", 1)
    before = jnp.where(side == 0, 0.0, edge)
    after = jnp.where(side == 0, edge, 0.0)
    zx = jnp.concatenate([before, after, jnp.zeros((POUT, 128 - 2 * HT), F32)], axis=1)
    dzt, dzx, loss = render(views, (1.0 / pixel_count).reshape(1), zt, zx, rd)
    back = swap(jnp.where(side == 0, dzx[:, HT : 2 * HT], dzx[:, :HT]), "scene", 1)
    dzt = jnp.concatenate(
        [
            dzt[:, :HT] + jnp.where(side == 0, 0.0, back),
            dzt[:, HT : tokens - HT],
            dzt[:, tokens - HT :] + jnp.where(side == 0, back, 0.0),
        ],
        axis=1,
    )
    d_bias_gauss = jnp.sum(dzt, axis=1)
    dz = dzt.astype(BF16)

    streams = ("xy", "yx")
    dw_gauss = side_grad(perm, dz, a3)
    if placed:
        sg = Scatter(dw_gauss, ("yx",))
        sg.keep, dz = together(sg.keep, dz)
    dh2, dh2_low, sums3 = norm_back(perm, dz, w_side, True, h2, gains[2], None, False)
    dw_down = weight_grad(plain, act, dh2_low, placed)
    d_low = dh2_low
    if placed:
        whole_down, d_low = together(dw_down[0], d_low)
        part_down = lax.psum_scatter(whole_down, "scene", scatter_dimension=0)
        sg.near()
        d_low = settle([sg], d_low)
        sg.send(0)
    du, d_bias_up = down_back(plain, d_low, w_third, u)
    if placed:
        du, *sg.moved = together(du, *sg.moved)
        sg.cross()
        du = settle([sg], du)
        sg.send(1)
    dw_up = weight_grad(perm, a2, du)
    if placed:
        su = Scatter(dw_up, streams)
        su.keep, du = together(su.keep, du)
    dh1, dh1_low, sums2 = norm_back(perm, du, w_second, False, h1, gains[1], dh2, False)
    if placed:
        dh1_low, su.got, *sg.moved = together(dh1_low, su.got, *sg.moved)
        su.near()
        sg.last()
        dh1_low = settle([su, sg], dh1_low)
        su.send(0)
        sg.rows()
    dw_out = weight_grad(perm, mixed, dh1_low)
    if placed:
        so = Scatter(dw_out, ("xy",))
        so.keep, dh1_low = together(so.keep, dh1_low)
    do = out_back(perm, dh1_low, w_second)
    dq, own, far = attend_back(perm, lens, p, kv, do, logs, flat)
    if placed:
        dq, own, far, so.got, sg.total, part_down, *su.moved = together(
            dq, own, far, so.got, sg.total, part_down, *su.moved
        )
        r_down = lax.psum_scatter(part_down, "rows", scatter_dimension=0)
    got = swap(far, "scene", 1)
    if placed:
        su.cross()
        so.near()
        got = settle([su, so], got)
        su.send(1)
        so.send(0)
    dkv = (own + got.astype(F32)).astype(BF16)
    dp = jnp.concatenate([dq, dkv[0], dkv[1]], axis=1)
    dw_joint = weight_grad(perm, a1, dp)
    if placed:
        sj = Scatter(dw_joint, streams)
        sj.keep, dp = together(sj.keep, dp)
    dh0_low, sums1 = norm_back(perm, dp, w_first, False, h0, gains[0], dh1, True)
    if placed:
        dh0_low, sj.got, *su.moved = together(dh0_low, sj.got, *su.moved)
        sj.near()
        first, *su.moved = settle([sj], su.moved[0], su.moved[1], dh0_low)
        dh0_low = su.moved.pop()
        su.moved.insert(0, first)
        sj.send(0)
        su.last()
        su.rows()
    dw_patch = side_grad(perm, x.T, dh0_low)
    if placed:
        sp = Scatter(dw_patch, ("yx",))
        sp.keep, *so.moved = together(sp.keep, *so.moved)
        so.cross()
        sp.keep = settle([so], sp.keep)
        so.send(1)
        sp.keep, r_down, *sj.moved = together(sp.keep, r_down, *sj.moved)
        r_down = r_down.astype(F32)
        sj.cross()
        settle([sj])
        sj.send(1)
        sp.near()
        sp.send(0)
        sj.last()
        so.last()
        wide = sj.away[0].shape[-1]
        sj.away = [jnp.concatenate([sj.away[0], so.away[0]], axis=-1)]
        sj.rows()
        sj.total, so.total = sj.total[..., :wide], sj.total[..., wide:]
        sp.cross()
        sp.send(1)
        sp.last()
        sp.rows_apart()
        reduced = [t.get() for t in (sp, sj, so, su)] + [r_down, sg.get()]
    else:
        grads = [dw_patch, dw_joint, dw_out, dw_up, dw_down, dw_gauss]
        reduced = [scatter_plain(g, i in (0, 5)) for i, g in enumerate(grads)]
    reduced[5] = reduced[5].T
    vector_part = jnp.concatenate(
        [sums1[0], sums2[0], sums3[0], sums1[1], sums2[1], sums3[1], sums1[2], sums2[2], sums3[2]]
        + [d_bias_up[0], d_bias_gauss, loss[0]]
    )
    squares = sum(jnp.sum(item * item) for item in reduced)
    totals = total_sum(jnp.concatenate([vector_part, jnp.broadcast_to(squares, (128,))]).reshape(-1, 128))
    totals = totals.reshape(-1)
    vec = vectors.shape[0]
    vector_grad, loss_sum, square_sum = totals[:vec], totals[vec], totals[vec + 128]
    grad_norm = jnp.sqrt(square_sum + jnp.sum(vector_grad * vector_grad))
    factor = jnp.minimum(1.0, CLIP_NORM / (grad_norm + 1e-06))
    next_moments, next_weights, next_averages = ([], [], [])
    for grad, moment, master, average in zip(reduced + [vector_grad], moments, masters, averages):
        moment, weight, mean = weight_step(grad, factor, moment, master, average)
        next_moments.append(moment)
        next_weights.append(weight)
        next_averages.append(mean)
    return (loss_sum, pixel_count, grad_norm, *next_moments, *next_weights, *next_averages)


def solution(mesh):
    item = P(None, "scene", None, None, "rows")
    weight_specs = (P("rows", "scene"),) + (P("scene", "rows"),) * 5 + (P(),)
    in_specs = (P(None, "scene", "rows", None), P(), P(), item, item, item) + 3 * weight_specs
    out_specs = (P(), P(), P()) + 3 * weight_specs
    return jax.shard_map(body, mesh=mesh, in_specs=in_specs, out_specs=out_specs, check_vma=False)
```
